32 devices in a mesh: dp: 16 (over z, y, x), mp: 2 (over core).
Axes of the slice: x: 2, y: 2, z: 4, core: 2. Of those that a mesh axis runs over, the one named last changes fastest.
Arguments:
- tokens: bfloat16 [65536, 512], P(('dp', 'mp')), may hold values from -6 to 6
- segment_ids: int32 [128, 512], P('dp'), may hold values from 0 to 7, never falling along the last dimension, each value on 1 to 256 neighbouring positions
- cotangent: bfloat16 [65536, 512], P(('dp', 'mp')), may hold values from -6 to 6
- pos_table: bfloat16 [512, 512], replicated, may hold values from -3 to 3
- w_qkv: bfloat16 [512, 1536], P(None, 'mp'), may hold values from -0.25 to 0.25
- w_out: bfloat16 [512, 512], P('mp'), may hold values from -1 to 1
- w_up: bfloat16 [512, 2048], P(None, 'mp'), may hold values from -0.25 to 0.25
- w_down: bfloat16 [2048, 512], P('mp'), may hold values from -0.125 to 0.125
- gain_one: float32 [512], replicated, may hold values from 0.5 to 1.5
- bias_one: float32 [512], replicated, may hold values from -1 to 1
- gain_two: float32 [512], replicated, may hold values from 0.5 to 1.5
- bias_two: float32 [512], replicated, may hold values from -1 to 1
Outputs:
- output: bfloat16 [65536, 512], P(('dp', 'mp'))
- input_grad: bfloat16 [65536, 512], P(('dp', 'mp'))
- pos_grad: float32 [512, 512], replicated
- qkv_grad: float32 [512, 1536], P(None, 'mp')
- out_grad: float32 [512, 512], P('mp')
- up_grad: float32 [512, 2048], P(None, 'mp')
- down_grad: float32 [2048, 512], P('mp')
- gain_one_grad: float32 [512], replicated
- bias_one_grad: float32 [512], replicated
- gain_two_grad: float32 [512], replicated
- bias_two_grad: float32 [512], replicated
The draws below stay inside these ranges and needn't reach their ends.
Inputs may be any that keep to these rules, and one draw needn't show every extreme that they name: `segment_ids`: within each window the numbers never fall, and each number covers 1 to 256 consecutive characters.
All inputs are finite; a program needn't handle non-finite values.
Results may differ from the reference program's by a relative error of at most 0.017.
Values may be sent and summed in bfloat16 or wider, within the bound.
A program may use at most 192 MiB of HBM per device.

```python
import math
import jax
import jax.numpy as jnp
import numpy as np
from jax import lax

D = 512
H = 8
FF = 2048
WIN = 512
WINDOWS = 128
TOKENS = 65536


def block_levels(stream_key, dims, cuts, low, high):
    factor_of = 1.0
    for position, parts in cuts:
        draws = jax.random.uniform(jax.random.fold_in(jax.random.fold_in(stream_key, 6), position), (parts,), jnp.float32, low / len(cuts), high / len(cuts))
        factor_of = factor_of * jnp.repeat(jnp.exp(draws), dims[position] // parts).reshape((-1,) + (1,) * (len(dims) - 1 - position))
    return factor_of


def length_profile(amount, total, limit, slope):
    loads = [(1 << 20) // math.isqrt(grade ** slope) + 1 for grade in range(2, amount + 1)]
    surplus, holding = total - limit - (amount - 1), [1] * (amount - 1)
    while surplus > 0:
        movable = [i for i in range(amount - 1) if holding[i] < limit]
        pool, left = sum([loads[i] for i in movable]), surplus
        for i in movable:
            more = min(limit - holding[i], max(1, left * loads[i] // pool), surplus)
            holding[i] = holding[i] + more
            surplus = surplus - more
    return np.array([limit] + holding)


def uneven(stream_key, number_of, total, bound, skew):
    if number_of == 2:
        one = jax.random.randint(stream_key, (), max(1, total - bound), min(bound, total - 1) + 1)
        return jnp.stack([one, total - one])
    lengths = jnp.asarray(length_profile(number_of, total, bound, skew), jnp.int32)
    pairs = (number_of - 1) // 2
    donor, taker = lengths[1:1 + 2 * pairs:2], lengths[2:2 + 2 * pairs:2]
    margin = jnp.minimum(donor - 1, bound - taker)
    moved = jax.random.randint(jax.random.fold_in(stream_key, 1), (pairs,), 0, 1 << 20) % (margin + 1)
    lengths = lengths.at[1:1 + 2 * pairs:2].set(donor - moved).at[2:2 + 2 * pairs:2].set(taker + moved)
    return lengths[jax.random.permutation(jax.random.fold_in(stream_key, 2), number_of)]


def scatter_about(stream_key, extent, scale, most, cuts=(), held_as=jnp.bfloat16):
    values = scale * jax.random.normal(stream_key, extent, jnp.float32)
    if cuts:
        values = values * block_levels(stream_key, extent, cuts, -0.22, 0.18)
    return jnp.clip(values, -most, most).astype(held_as)


def setup_inputs(seed: int = 0) -> dict:
    streams_of = jax.random.split(jax.random.key(seed), 13)
    return {
        "tokens": scatter_about(streams_of[0], (TOKENS, D), 1.0, 6.0, ((0, 32),)),
        "segment_ids": jax.vmap(lambda own: jnp.searchsorted(jnp.cumsum(uneven(own, 8, WIN, WIN // 2, 0)), jnp.arange(WIN), side="right"))(jax.random.split(streams_of[1], WINDOWS)).reshape((WINDOWS, WIN)).astype(jnp.int32),
        "cotangent": scatter_about(streams_of[2], (TOKENS, D), 1.0, 6.0, ((0, 32),)),
        "pos_table": scatter_about(streams_of[3], (WIN, D), 0.5, 3.0),
        "w_qkv": scatter_about(streams_of[4], (D, 3 * D), D ** -0.5, 0.25, ((1, 2),)),
        "w_out": scatter_about(streams_of[5], (D, D), (D // 16) ** -0.5, 1.0, ((0, 2),)),
        "w_up": scatter_about(streams_of[6], (D, FF), D ** -0.5, 0.25, ((1, 2),)),
        "w_down": scatter_about(streams_of[7], (FF, D), FF ** -0.5, 0.125, ((0, 2),)),
        "gain_one": jnp.clip(1.0 + 0.1 * jax.random.normal(streams_of[8], (D,), jnp.float32), 0.5, 1.5),
        "bias_one": scatter_about(streams_of[9], (D,), 0.2, 1.0, (), jnp.float32),
        "gain_two": jnp.clip(1.0 + 0.1 * jax.random.normal(streams_of[10], (D,), jnp.float32), 0.5, 1.5),
        "bias_two": scatter_about(streams_of[11], (D,), 0.2, 1.0, (), jnp.float32),
    }


HIGHEST = lax.Precision.HIGHEST
EPSILON = 1e-05

@jax.custom_vjp
def low(v):
    return lax.optimization_barrier(v.astype(jnp.bfloat16)).astype(jnp.float32)

@jax.custom_vjp
def low_back(v):
    return v

def low_keep(v):
    return (low(v), None)

def low_pass(kept, grad):
    return (grad,)

def back_keep(v):
    return (v, None)

def back_low(kept, grad):
    return (low(grad),)
low.defvjp(low_keep, low_pass)
low_back.defvjp(back_keep, back_low)

def product(left_side, right_side):
    return jnp.dot(left_side, right_side, precision=HIGHEST, preferred_element_type=jnp.float32)

def normalize(residual, gain_row, offset_row):
    center = residual - lax.optimization_barrier(jnp.mean(residual, axis=-1, keepdims=True))
    spread = lax.optimization_barrier(jnp.mean(center * center, axis=-1, keepdims=True))
    return center * lax.rsqrt(spread + EPSILON) * gain_row + offset_row

def window_mix(operands):
    queries, keys_in, values, segment = operands
    factor = queries.shape[-1] ** (-0.5)
    scores = low_back(jnp.einsum('qhd,khd->hqk', queries, keys_in, precision=HIGHEST) * factor)
    places = jnp.arange(segment.shape[0])
    allowed = (segment[:, None] == segment[None, :]) & (places[None, :] <= places[:, None])
    scores = jnp.where(allowed[None], scores, -1e+30)
    highest = lax.optimization_barrier(jnp.max(scores, axis=-1, keepdims=True))
    weights = jnp.exp(scores - highest)
    probabilities = low(weights / lax.optimization_barrier(jnp.sum(weights, axis=-1, keepdims=True)))
    return jnp.einsum('hqk,khd->qhd', probabilities, values, precision=HIGHEST)

def block_layer(tokens, pos_table, w_qkv, w_out, w_up, w_down, gain_one, bias_one, gain_two, bias_two, segment):
    windows_here, window_len, model_width = tokens.shape
    head_size = model_width // H
    placed = (tokens + pos_table[None]).reshape(windows_here * window_len, model_width)
    joined = low(low_back(product(low(placed), w_qkv)))
    joined = joined.reshape(windows_here, window_len, H, 3, head_size)
    mixture = lax.map(jax.checkpoint(window_mix), (joined[:, :, :, 0], joined[:, :, :, 1], joined[:, :, :, 2], segment))
    mixture = low(low_back(mixture.reshape(windows_here * window_len, model_width)))
    attention = low_back(product(mixture, w_out))
    normed = normalize(placed + attention, gain_one, bias_one)
    before = low_back(product(low(normed), w_up))
    activated = low(jax.nn.gelu(before))
    ffn_out = low_back(product(activated, w_down))
    result = normalize(normed + ffn_out, gain_two, bias_two)
    return result.reshape(windows_here, window_len, model_width)

def reference(tokens, segment_ids, cotangent, pos_table, w_qkv, w_out, w_up, w_down, gain_one, bias_one, gain_two, bias_two):
    weights = tuple((weight.astype(jnp.float32) for weight in (pos_table, w_qkv, w_out, w_up, w_down, gain_one, bias_one, gain_two, bias_two)))
    group_windows = math.gcd(WINDOWS, max(1, 4096 // WIN))
    scan_steps = WINDOWS // group_windows
    inputs = tokens.astype(jnp.float32).reshape(scan_steps, group_windows, WIN, D)
    grads_in = cotangent.astype(jnp.float32).reshape(scan_steps, group_windows, WIN, D)
    segments = segment_ids.reshape(scan_steps, group_windows, WIN)

    def scan_body(totals, scan_item):
        block_in, segment, grad_block = scan_item

        def forward(block_rows, *params):
            return block_layer(block_rows, *params, segment)
        result, pull_back = jax.vjp(forward, block_in, *weights)
        gradients = pull_back(grad_block)
        totals = tuple((total + gradient for total, gradient in zip(totals, gradients[1:])))
        return (totals, (result.astype(jnp.bfloat16), gradients[0].astype(jnp.bfloat16)))
    zero_grads = tuple((jnp.zeros(weight.shape, jnp.float32) for weight in weights))
    totals, (outputs_all, input_grads) = lax.scan(scan_body, zero_grads, (inputs, segments, grads_in))
    return (outputs_all.reshape(TOKENS, D), input_grads.reshape(TOKENS, D), totals[0], totals[1], totals[2], totals[3], totals[4], totals[5], totals[6], totals[7], totals[8])
```

```python
import functools

import jax
import jax.numpy as jnp
from jax import lax
from jax.experimental import pallas as pl
from jax.experimental.pallas import tpu as pltpu
from jax.sharding import PartitionSpec as P

BF = jnp.bfloat16
F32 = jnp.float32
MESH = pl.DeviceIdType.MESH
HD = 64
EPSILON = 1e-05
NEG = -1e30
GELU_A = 0.7978845608028654
GELU_B = 0.044715

CHUNKS = {
    "D0": (32, 512),
    "D1": (32, 512),
    "U0": (32, 512),
    "U1": (32, 512),
    "O": (16, 512),
    "Q0": (32, 384),
    "Q1": (32, 384),
    "P": (16, 512),
}
NAMES = tuple(CHUNKS)
PIECES = 16

SCHEDULE = {
    ("down", 1): (("D0", 0),),
    ("down", 3): (("D1", 0),),
    ("slope", 1): (("D0", 1),),
    ("slope", 3): (("D1", 1),),
    ("up", 1): (("U0", 0),),
    ("up", 3): (("D0", 2), ("U1", 0),),
    ("nb", 0): (("U0", 1),),
    ("nb", 1): (("D1", 2), ("U1", 1),),
    ("nb", 2): (("D0", 3),),
    ("O", 0): (("O", 0), ("sm", 0),),
    ("back0", 0): (("U0", 2),),
    ("back0", 1): (("D1", 3),),
    ("back0", 2): (("D0", 4), ("U1", 2), ("O", 1), ("sm", 1),),
    ("back0", 4): (("U0", 3),),
    ("back0", 5): (("D1", 4),),
    ("back0", 6): (("U1", 3), ("sm", 2),),
    ("back0", 7): (("D0", 5), ("O", 2),),
    ("q0", 0): (("U0", 4),),
    ("q0", 1): (("Q0", 0),),
    ("back1", 0): (("D1", 5), ("sm", 3),),
    ("back1", 1): (("D0", 6), ("U1", 4),),
    ("back1", 2): (("O", 3), ("Q0", 1),),
    ("back1", 3): (("U0", 5), ("sm", 4),),
    ("back1", 4): (("D1", 6),),
    ("back1", 5): (("U1", 5),),
    ("back1", 6): (("D0", 7), ("O", 4),),
    ("back1", 7): (("Q0", 2),),
    ("q1", 0): (("U0", 6),),
    ("q1", 1): (("Q1", 0),),
    ("fin", 0): (("D1", 7), ("O", 5),),
    ("fin", 1): (("U1", 6),),
    ("fin", 2): (("Q0", 3),),
    ("P", 0): (("Q1", 1), ("P", 0),),
}
TAIL = (
    ("U0", 7),
    ("O", 6),
    ("P", 1),
    ("Q0", 4),
    ("U1", 7),
    ("Q1", 2),
    ("Q0", 5),
    ("O", 7),
    ("P", 2),
    ("Q1", 3),
    ("Q0", 6),
    ("P", 3),
    ("Q1", 4),
    ("P", 4),
    ("Q0", 7),
    ("Q1", 5),
    ("P", 5),
    ("Q1", 6),
    ("P", 6),
    ("Q1", 7),
    ("P", 7),
    ("P", 8),
)


def dot(left, right, left_dim=1, right_dim=0):
    return lax.dot_general(
        left, right, (((left_dim,), (right_dim,)), ((), ())), preferred_element_type=F32
    )


def lanes(shape):
    return lax.broadcasted_iota(jnp.int32, shape, len(shape) - 1)


def rows_of(w, win):
    return pl.ds(pl.multiple_of(w * win, win), win)


def columns_of(start, size):
    return pl.ds(pl.multiple_of(start, 128), size)


def row_mean(v):
    return jnp.mean(v, axis=-1, keepdims=True)


def kernel(fused, dims, *refs):
    win, width, hidden, windows = dims
    half_hidden = hidden // 2
    half = win // 2
    (tok_h, cot_h, pos_h, seg, wq_h, wo_h, wu_h, wd_h, g1, b1, g2, b2) = refs[:12]
    refs = refs[12:]
    out_h, ig_h, small_h = refs[:3]
    F = dict(zip(NAMES, refs[3 : 3 + len(NAMES)]))
    b = dict(zip(scratch_of(fused, dims), refs[3 + len(NAMES) :]))
    tok, cot, pos, augs, augk = b["tok"], b["cot"], b["pos"], b["augs"], b["augk"]
    wq, wo, wu, wd = b["wq"], b["wo"], b["wu"], b["wd"]
    joined, mix, u1, rs1, pb, nb = b["joined"], b["mix"], b["u1"], b["rs1"], b["pb"], b["nb"]
    act, gp, augq, nf, small = b["act"], b["gp"], b["augq"], b["nf"], b["small"]
    G, R_mp, R_a, R_b, R_z = ({k: b.get(buf + k) for k in NAMES} for buf in ("G", "M", "A", "B", "Z"))
    in_sem, out_sem = b["in_sem"], b["out_sem"]

    pairs = width // 128

    copies = {}

    def fetch(name, src, dst, k):
        copies[name] = pltpu.make_async_copy(src, dst, in_sem.at[k])
        copies[name].start()

    if fused:
        wsem, csend, crecv, ssend, srecv, lsem = (
            b[k] for k in ("wsem", "csend", "crecv", "ssend", "srecv", "lsem")
        )
        dp = lax.axis_index("dp")
        mp = lax.axis_index("mp")
        zc = dp // 4
        yc = lax.rem(dp // 2, 2)
        xc = lax.rem(dp, 2)
        ac = jnp.where(mp == 0, xc, yc)
        bc = jnp.where(mp == 0, yc, xc)
        step_a = jnp.where(mp == 0, 1, 2)
        step_b = jnp.where(mp == 0, 2, 1)
        dev_mp = (dp, 1 - mp)
        dev_a = (dp + step_a * (1 - 2 * ac), mp)
        dev_b = (dp + step_b * (1 - 2 * bc), mp)
        dev_x = (dp + 1 - 2 * xc, mp)
        dev_y = (dp + 2 * (1 - 2 * yc), mp)
        zs = [lax.rem(zc + k, 4) for k in (1, 2, 3)]
        dev_z = [(lax.rem(dp, 4) + 4 * z, mp) for z in zs]
        barrier = pltpu.get_barrier_semaphore()
        for dev in [dev_mp, dev_a, dev_b] + dev_z:
            pl.semaphore_signal(barrier, inc=1, device_id=dev, device_id_type=MESH)

    fetch("tok", tok_h, tok, 0)
    fetch("pos", pos_h, pos, 1)
    raw_width = wq_h.shape[1]
    raw = act.at[pl.ds(0, width), pl.ds(0, raw_width)]
    fetch("wq", wq_h, raw, 2)
    wparts = []
    if fused:
        wparts.append((wo_h, wo.at[pl.ds(pl.multiple_of(mp * half, half), half), :]))
        wparts.append((wu_h, wu.at[:, columns_of(half_hidden * mp, half_hidden)]))
        wparts.append((wd_h, wd.at[pl.ds(pl.multiple_of(mp * half_hidden, half_hidden), half_hidden), :]))
    else:
        wparts += [(wo_h, wo), (wu_h, wu), (wd_h, wd)]
    for i, (src, dst) in enumerate(wparts):
        fetch("w%d" % i, src, dst, 5 + i)
    fetch("cot", cot_h, cot, 4)
    small[...] = jnp.zeros_like(small)

    l64 = lax.rem(lanes((win, 128)), HD)
    lo = lanes((win, 128)) < HD

    copies["wq"].wait()
    own_columns = mp * raw_width // 3 if fused else 0
    for p in range(raw_width // 384):
        cut = [raw[:, pl.ds(p * 384 + 128 * i, 128)] for i in range(3)]
        low = lanes((width, 128)) < HD
        swapped = [pltpu.roll(c.astype(F32), HD, 1).astype(BF) for c in cut]
        q = jnp.where(low, cut[0], cut[1]) * BF(HD**-0.5)
        k = jnp.where(low, swapped[0], swapped[2])
        v = jnp.where(low, cut[1], cut[2])
        for i, part in enumerate((q, k, v)):
            wq[:, columns_of(own_columns + width * i + 128 * p, 128)] = part

    wremote = []
    if fused:
        pl.semaphore_wait(barrier, 6)
        slices = [wq.at[:, columns_of(own_columns + width * i, raw_width // 3)] for i in range(3)]
        for i, (src, dst) in enumerate([(x, x) for x in slices] + wparts):
            c = pltpu.make_async_remote_copy(
                src_ref=src, dst_ref=dst, send_sem=wsem.at[0, i], recv_sem=wsem.at[1, i],
                device_id=dev_mp, device_id_type=MESH,
            )
            c.start()
            wremote.append(c)

    columns = seg[...].astype(F32).T
    mine = (mp if fused else 0) * windows
    for w in range(windows):
        R = pl.ds(w * win, win)
        column = jnp.sum(
            jnp.where(lanes(columns.shape) == mine + w, columns, 0.0), axis=1, keepdims=True
        ).astype(jnp.int32)
        augs[R, :] = jnp.where((l64 < 8) & (l64 != column), NEG, 0.0).astype(BF)
        augk[R, :] = jnp.where((l64 == column) | ((l64 >= 8) & (l64 < 11)), 1.0, 0.0).astype(BF)

    def remote(src, dst, send, recv, dev):
        return pltpu.make_async_remote_copy(
            src_ref=src, dst_ref=dst, send_sem=send, recv_sem=recv, device_id=dev, device_id_type=MESH
        )

    def add(mine, got):
        mine[...] = mine[...] + got[...]

    def exchange(name, k):
        if not fused:
            return
        c = NAMES.index(name)
        g = G[name]
        own = g.at[mp]
        mp_copy = remote(g.at[1 - mp], R_mp[name], csend.at[c, 0], crecv.at[c, 0], dev_mp)
        a_copy = remote(own.at[pl.ds((1 - ac) * 8, 8)], R_a[name], csend.at[c, 1], crecv.at[c, 1], dev_a)
        b_copy = remote(own.at[pl.ds(ac * 8 + (1 - bc) * 4, 4)], R_b[name], csend.at[c, 2], crecv.at[c, 2], dev_b)
        base = ac * 8 + bc * 4
        z_copies = [
            remote(own.at[base + zs[j]], R_z[name].at[j], csend.at[c, 3 + j], crecv.at[c, 3 + j], dev_z[j])
            for j in range(3)
        ]
        full = g.at[1 - mp]
        done = F[name].at[mp] if name == "P" else F[name]
        put = pltpu.make_async_copy(full, done, lsem.at[c])
        zg_copies = [
            remote(full.at[base + zc], full.at[base + zc], csend.at[c, 6 + j], crecv.at[c, 6 + j], dev_z[j])
            for j in range(3)
        ]
        bg_copy = remote(full.at[pl.ds(base, 4)], full.at[pl.ds(base, 4)], csend.at[c, 9], crecv.at[c, 9], dev_b)
        ag_copy = remote(full.at[pl.ds(ac * 8, 8)], full.at[pl.ds(ac * 8, 8)], csend.at[c, 10], crecv.at[c, 10], dev_a)
        mg_copy = remote(full, b["XP"], csend.at[c, 11], crecv.at[c, 11], dev_mp)
        if k == 0:
            mp_copy.start()
        elif k == 1:
            mp_copy.wait()
            add(own, R_mp[name])
            a_copy.start()
        elif k == 2:
            a_copy.wait()
            add(own.at[pl.ds(ac * 8, 8)], R_a[name])
            b_copy.start()
        elif k == 3:
            b_copy.wait()
            add(own.at[pl.ds(base, 4)], R_b[name])
            for z in z_copies:
                z.start()
        elif k == 4:
            for z in z_copies:
                z.wait()
            total = own[base + zc].astype(F32)
            for j in range(3):
                total = total + R_z[name][j].astype(F32)
            if name in ("Q0", "Q1"):
                q, kk, v = total[:, :128] * (HD**-0.5), total[:, 128:256], total[:, 256:]
                total = jnp.concatenate(
                    [q[:, :HD], kk[:, :HD], v[:, :HD], q[:, HD:], kk[:, HD:], v[:, HD:]], axis=1
                )
            full[base + zc] = total.astype(BF)
            for z in zg_copies:
                z.start()
        elif k == 5:
            for z in zg_copies:
                z.wait()
            bg_copy.start()
        elif k == 6:
            bg_copy.wait()
            ag_copy.start()
        elif k == 7:
            ag_copy.wait()
            put.start()
            if name == "P":
                mg_copy.start()
        elif k == 8:
            mg_copy.wait()
            other = pltpu.make_async_copy(b["XP"], F[name].at[1 - mp], lsem.at[len(NAMES)])
            other.start()
            other.wait()
        elif k == 9:
            put.wait()

    def exchange_small(k):
        if not fused:
            return
        legs = [(b["s_mp"], dev_mp, 0), (b["s_x"], dev_x, 1), (b["s_y"], dev_y, 2)]
        if k > 0 and k <= 3:
            buf, dev, s = legs[k - 1]
            remote(small, buf, ssend.at[s], srecv.at[s], dev).wait()
            small[...] = small[...] + buf[...]
        if k < 3:
            buf, dev, s = legs[k]
            remote(small, buf, ssend.at[s], srecv.at[s], dev).start()
        zcs = [remote(small, b["s_z"].at[zc], ssend.at[3 + j], srecv.at[3 + j], dev_z[j]) for j in range(3)]
        if k == 3:
            b["s_z"][zc] = small[...]
            for z in zcs:
                z.start()
        if k == 4:
            for z in zcs:
                z.wait()
            small[...] = (b["s_z"][0] + b["s_z"][1]) + (b["s_z"][2] + b["s_z"][3])

    causal = jnp.where(lanes((half, half)) <= lax.broadcasted_iota(jnp.int32, (half, half), 0), 0.0, NEG)
    causal_t = jnp.where(lanes((half, half)) >= lax.broadcasted_iota(jnp.int32, (half, half), 0), 0.0, NEG)
    def attend(w, p):
        R = rows_of(w, win)
        Q, K, V = (joined[R, columns_of(width * i + p * 128, 128)] for i in range(3))
        aq, ak = augs[R, :], augk[R, :]
        ones = jnp.ones((win, 128), BF)
        zero = jnp.zeros((win, 128), BF)
        qs, ks, vs = [], [], []
        for h in range(2):
            mine = lo if h == 0 else ~lo
            qs.append(jnp.where(mine, Q, aq))
            ks.append(jnp.where(mine, K, ak))
            vs.append(jnp.concatenate([jnp.where(mine, V, zero), jnp.where(mine, ones, zero)], axis=1))
        for qb in range(2):
            kl = half * (qb + 1)
            es, ms = [], []
            for h in range(2):
                s = dot(qs[h][qb * half : (qb + 1) * half], ks[h][:kl], 1, 1)
                if qb == 0:
                    s = s + causal
                else:
                    s = jnp.concatenate([s[:, :half], s[:, half:] + causal], axis=1)
                m = jnp.max(s, axis=1, keepdims=True)
                es.append(jnp.exp(s - m).astype(BF))
                ms.append(m)
            ov = dot(jnp.concatenate(es, axis=1), jnp.concatenate([v[:kl] for v in vs], axis=0))
            total = ov[:, 128:]
            rr = pl.ds(pl.multiple_of(w * win + qb * half, half), half)
            mix[rr, columns_of(p * 128, 128)] = (ov[:, :128] / total).astype(BF)
            low = lo[:half]
            lse = jnp.where(low, ms[0], ms[1]) + jnp.log(total)
            x = -pltpu.roll(lse, HD, 1)
            hi = x.astype(BF)
            x = x - hi.astype(F32)
            mid = x.astype(BF)
            last = (x - mid.astype(F32)).astype(BF)
            l6 = l64[:half]
            a = aq[qb * half : (qb + 1) * half]
            a = jnp.where(l6 == 8, hi, a)
            a = jnp.where(l6 == 9, mid, a)
            augq[rr, columns_of(p * 128, 128)] = jnp.where(l6 == 10, last, a)

    copies["tok"].wait()
    copies["pos"].wait()
    for c in wremote[:3]:
        c.wait()

    def project(w, _):
        R = rows_of(w, win)
        row = (tok[R, :].astype(F32) + pos[...].astype(F32)).astype(BF)
        pb[R, :] = row
        for i in range(3):
            joined[R, pl.ds(width * i, width)] = dot(row, wq[:, pl.ds(width * i, width)]).astype(BF)
        return 0

    lax.fori_loop(0, windows, project, 0)

    def attend_window(w, _):
        for p in range(pairs):
            attend(w, p)
        return 0

    lax.fori_loop(0, windows, attend_window, 0)

    for i in range(3):
        copies["w%d" % i].wait()
    for c in wremote[3:]:
        c.wait()
    copies["cot"].wait()

    def feed(w, _):
        R = rows_of(w, win)
        r1 = (tok[R, :].astype(F32) + pos[...].astype(F32)) + dot(mix[R, :], wo[...])
        center = r1 - row_mean(r1)
        rstd = lax.rsqrt(row_mean(center * center) + EPSILON)
        unit = center * rstd
        u1[R, :] = unit.astype(BF)
        rs1[R, :] = jnp.broadcast_to(rstd, (win, 128))
        normed = unit * g1[...] + b1[...]
        nf[...] = normed
        nb[R, :] = normed.astype(BF)

        r2 = nf[...]
        for c in range(hidden // 512):
            cs = pl.ds(c * 512, 512)
            v = dot(nb[R, :], wu[:, cs]).astype(BF)
            v2 = v * v
            t = jnp.tanh(v * (BF(GELU_A) + BF(GELU_A * GELU_B) * v2))
            h = BF(0.5) + BF(0.5) * t
            active = v * h
            act[R, cs] = active
            gp[R, cs] = h + h * ((BF(1) - h) * (v * (BF(2 * GELU_A) + BF(6 * GELU_A * GELU_B) * v2)))
            r2 = r2 + dot(active, wd[cs, :])
        center = r2 - row_mean(r2)
        rstd = lax.rsqrt(row_mean(center * center) + EPSILON)
        unit = center * rstd
        tok[R, :] = (unit * g2[...] + b2[...]).astype(BF)
        up = cot[R, :].astype(F32)
        small[0:1, :] += jnp.sum(up * unit, axis=0, keepdims=True)
        small[1:2, :] += jnp.sum(up, axis=0, keepdims=True)
        e = up * g2[...]
        cot[R, :] = (rstd * (e - row_mean(e) - unit * row_mean(e * unit))).astype(BF)
        return 0

    lax.fori_loop(0, windows, feed, 0)
    out_copy = pltpu.make_async_copy(tok, out_h, out_sem.at[0])
    out_copy.start()

    def hooked(phase, body, count):
        def one(t, _):
            body(t, 0)
            for at in range(count):
                steps = SCHEDULE.get((phase, at))
                if steps:
                    pl.when(t == at)(functools.partial(run_steps, steps))
            return 0

        lax.fori_loop(0, count, one, 0)

    def run_steps(steps):
        for name, k in steps:
            if name == "sm":
                exchange_small(k)
            else:
                exchange(name, k)

    halves = hidden // 1024

    def down_tile(t, _):
        part, m = t // 2, lax.rem(t, 2)
        tile = m * halves + part
        d = dot(act[:, columns_of(tile * 512, 512)], cot[...], 0, 0).astype(BF).reshape(16, 32, 512)
        for i in range(2):

            @pl.when(part == i)
            def _():
                G["D%d" % i][m] = d

        return 0

    hooked("down", down_tile, hidden // 512)

    def slope(w, _):
        R = rows_of(w, win)
        for c in range(hidden // 512):
            cs = pl.ds(c * 512, 512)
            d = dot(cot[R, :], wd[pl.ds(c * 512, 512), :], 1, 1)
            gp[R, cs] = (d * gp[R, cs].astype(F32)).astype(BF)
        return 0

    hooked("slope", slope, windows)

    def up_tile(t, _):
        part, m = t // 2, lax.rem(t, 2)
        tile = m * halves + part
        d = dot(nb[...], gp[:, columns_of(tile * 512, 512)], 0, 0).astype(BF).reshape(16, 32, 512)
        for i in range(2):

            @pl.when(part == i)
            def _():
                G["U%d" % i][m] = d

        return 0

    hooked("up", up_tile, hidden // 512)

    def norm_back(w, _):
        R = rows_of(w, win)
        ng = cot[R, :].astype(F32) + dot(gp[R, :], wu[...], 1, 1)
        unit = u1[R, :].astype(F32)
        small[2:3, :] += jnp.sum(ng * unit, axis=0, keepdims=True)
        small[3:4, :] += jnp.sum(ng, axis=0, keepdims=True)
        e = ng * g1[...]
        rstd = rs1[R, 0:1]
        rg = (rstd * (e - row_mean(e) - unit * row_mean(e * unit))).astype(BF)
        cot[R, :] = rg
        u1[R, :] = dot(rg, wo[...], 1, 1).astype(BF)
        return 0

    hooked("nb", norm_back, windows)

    G["O"][...] = dot(mix[...], cot[...], 0, 0).astype(BF).reshape(2, 16, half // 16, 512)
    run_steps(SCHEDULE.get(("O", 0), ()))

    flip = (lax.broadcasted_iota(jnp.int32, (256, 128), 0) % 128 < HD) != (lanes((256, 128)) < HD)
    swap = jnp.where(flip, 1.0, 0.0).astype(BF)

    def attend_back(w, p):
        R = rows_of(w, win)
        pc = columns_of(p * 128, 128)
        Q, K, V = (joined[R, columns_of(width * i + p * 128, 128)] for i in range(3))
        D = u1[R, pc]
        prod = D.astype(F32) * mix[R, pc].astype(F32)
        ph = prod.astype(BF)
        pl_ = (prod - ph.astype(F32)).astype(BF)
        x = -dot(jnp.concatenate([ph, pl_], axis=1), swap)
        hi = x.astype(BF)
        mid = (x - hi.astype(F32)).astype(BF)
        zero = jnp.zeros((win, 128), BF)
        ad = jnp.where(l64 == 8, hi, jnp.where(l64 == 9, mid, zero))
        av = jnp.where((l64 == 8) | (l64 == 9), jnp.ones((win, 128), BF), zero)
        aq, ak = augq[R, pc], augk[R, :]
        dq, dk, dv = [None, None], [None, None], [None, None]

        def acc(to, i, v):
            to[i] = v if to[i] is None else to[i] + v

        for h in range(2):
            mine = lo if h == 0 else ~lo
            qa, ka, va, da = (jnp.where(mine, a, b) for a, b in ((Q, aq), (K, ak), (V, av), (D, ad)))
            qm, km, dm = (jnp.where(mine, a, zero) for a in (Q, K, D))
            for kb in range(2):
                q0 = kb * half
                ks = slice(kb * half, (kb + 1) * half)
                s = dot(ka[ks], qa[q0:], 1, 1)
                if kb == 1:
                    s = s + causal_t
                else:
                    s = jnp.concatenate([s[:, :half] + causal_t, s[:, half:]], axis=1)
                e = jnp.exp(s)
                pr = e.astype(BF)
                dpr = dot(va[ks], da[q0:], 1, 1)
                ds = (e * dpr).astype(BF)
                acc(dv, kb, dot(pr, dm[q0:]))
                acc(dk, kb, dot(ds, qm[q0:]))
                x = dot(ds, km[ks], 0, 0)
                if kb == 0:
                    acc(dq, 0, x[:half])
                    acc(dq, 1, x[half:])
                else:
                    acc(dq, 1, x)
        for i in range(2):
            rr = pl.ds(pl.multiple_of(w * win + i * half, half), half)
            for k, v in enumerate((dq, dk, dv)):
                joined[rr, columns_of(width * k + p * 128, 128)] = v[i].astype(BF)

    def back_group(group):
        def one(t, _):
            attend_back(lax.rem(t, windows), (t // windows) * 2 + group)
            return 0

        return one

    def qkv_grad(group):
        for m in range(2):
            p = 2 * m + group
            for i in range(3):
                d = dot(pb[...], joined[:, pl.ds(width * i + p * 128, 128)], 0, 0).astype(BF)
                G["Q%d" % group][m, :, :, pl.ds(128 * i, 128)] = d.reshape(16, 32, 128)
            run_steps(SCHEDULE.get(("q%d" % group, m), ()))

    hooked("back0", back_group(0), windows * pairs // 2)
    qkv_grad(0)
    hooked("back1", back_group(1), windows * pairs // 2)
    qkv_grad(1)

    def finish(w, _):
        R = rows_of(w, win)
        v = cot[R, :].astype(F32) + dot(joined[R, :], wq[...], 1, 1)
        nf[...] = jnp.where(w == 0, v, nf[...] + v)
        cot[R, :] = v.astype(BF)
        return 0

    hooked("fin", finish, windows)
    ig_copy = pltpu.make_async_copy(cot, ig_h, out_sem.at[1])
    ig_copy.start()
    G["P"][...] = nf[...].astype(BF).reshape(2, 16, half // 16, 512)
    small_copy = pltpu.make_async_copy(small, small_h, out_sem.at[2])
    small_copy.start()
    run_steps(SCHEDULE.get(("P", 0), ()))
    run_steps(TAIL)
    run_steps([(name, 9) for name in NAMES])
    if not fused:
        outs = [pltpu.make_async_copy(G[nm], F[nm], in_sem.at[i]) for i, nm in enumerate(NAMES)]
        for c in outs:
            c.start()
        for c in outs:
            c.wait()
    out_copy.wait()
    ig_copy.wait()
    small_copy.wait()


def scratch_of(fused, dims):
    win, width, hidden, windows = dims
    rows = win * windows
    V, dma = pltpu.VMEM, pltpu.SemaphoreType.DMA
    b = {k: V((rows, width), BF) for k in ("tok", "cot", "mix", "u1", "pb", "nb", "augq")}
    b.update({k: V((rows, hidden), BF) for k in ("act", "gp")})
    b.update(
        pos=V((win, width), BF),
        augs=V((rows, 128), BF),
        augk=V((rows, 128), BF),
        wq=V((width, 3 * width), BF),
        wo=V((width, width), BF),
        wu=V((width, hidden), BF),
        wd=V((hidden, width), BF),
        joined=V((rows, 3 * width), BF),
        rs1=V((rows, 128), F32),
        nf=V((win, width), F32),
        small=V((8, width), F32),
        in_sem=dma((12,)),
        out_sem=dma((3,)),
    )
    b.update({"G" + k: V((2, PIECES) + CHUNKS[k], BF) for k in NAMES})
    if fused:
        for buf, count in (("M", 16), ("A", 8), ("B", 4), ("Z", 3)):
            b.update({buf + k: V((count,) + CHUNKS[k], BF) for k in NAMES})
        b["XP"] = V((PIECES,) + CHUNKS["P"], BF)
        b.update({k: V((8, width), F32) for k in ("s_mp", "s_x", "s_y")})
        b.update(
            s_z=V((4, 8, width), F32),
            wsem=dma((2, 6)),
            csend=dma((len(NAMES), 12)),
            crecv=dma((len(NAMES), 12)),
            ssend=dma((6,)),
            srecv=dma((6,)),
            lsem=dma((len(NAMES) + 1,)),
        )
    return b


def layer(fused, tok, cot, pos, seg, wq, wo, wu, wd, g1, b1, g2, b2, hidden):
    rows, width = tok.shape
    win = pos.shape[0]
    windows = rows // win
    hbm = pl.BlockSpec(memory_space=pl.ANY)
    vmem = pl.BlockSpec(memory_space=pltpu.VMEM)
    shape = jax.ShapeDtypeStruct
    full = {k: (PIECES,) + v if fused and k != "P" else (2, PIECES) + v for k, v in CHUNKS.items()}
    outs = [shape((rows, width), BF), shape((rows, width), BF), shape((8, width), F32)]
    outs += [shape(full[k], BF) for k in NAMES]
    scratch = list(scratch_of(fused, (win, width, hidden, windows)).values())
    params = dict(vmem_limit_bytes=64 << 20)
    if fused:
        params.update(collective_id=0, has_side_effects=True)
    return pl.pallas_call(
        functools.partial(kernel, fused, (win, width, hidden, windows)),
        out_shape=outs,
        in_specs=[hbm] * 3 + [vmem] + [hbm] * 4 + [vmem] * 4,
        out_specs=[hbm] * len(outs),
        scratch_shapes=scratch,
        compiler_params=pltpu.CompilerParams(**params),
        name="layer",
    )(tok, cot, pos, seg, wq, wo, wu, wd, g1, b1, g2, b2)


def finish_kernel(*refs):
    (out_h, ig_h, small), grads = refs[:3], dict(zip(NAMES, refs[3 : 3 + len(NAMES)]))
    refs = refs[3 + len(NAMES) :]
    out_o, ig_o, pos_o, qkv_o, wo_o, up_o, down_o = refs[:7]
    norms = refs[7:11]
    refs = refs[11:]
    got = dict(zip(NAMES, refs[: len(NAMES)]))
    wide = dict(zip(NAMES, refs[len(NAMES) : 2 * len(NAMES)]))
    held, in_sem, out_sem = refs[2 * len(NAMES) :]
    last, loads, passed = [], [], []
    for i, (src, dst) in enumerate(((out_h, out_o), (ig_h, ig_o))):
        passed.append(pltpu.make_async_copy(src, held.at[i], in_sem.at[len(NAMES) + i]))
        last.append(pltpu.make_async_copy(held.at[i], dst, out_sem.at[len(NAMES) + i]))
    for c in passed:
        c.start()
    for i, k in enumerate(NAMES):
        loads.append(pltpu.make_async_copy(grads[k], got[k], in_sem.at[i]))
        loads[-1].start()
    rows = down_o.shape[0] // 2
    places = {
        "D0": down_o.at[pl.ds(0, rows)],
        "D1": down_o.at[pl.ds(rows, rows)],
        "U0": up_o.at[:, pl.ds(0, 512)],
        "U1": up_o.at[:, pl.ds(512, 512)],
        "O": wo_o,
        "Q0": qkv_o.at[:, pl.ds(0, 384)],
        "Q1": qkv_o.at[:, pl.ds(384, 384)],
        "P": pos_o,
    }
    for i in range(2):
        passed[i].wait()
        last[i].start()
    for i, k in enumerate(NAMES):
        loads[i].wait()
        wide[k][...] = got[k][...].astype(F32).reshape(wide[k].shape)
        last.append(pltpu.make_async_copy(wide[k], places[k], out_sem.at[i]))
        last[-1].start()
    for ref, row in zip(norms, (2, 3, 0, 1)):
        ref[...] = small[row]
    for c in last:
        c.wait()


def finish(out, ig, small, grads, win, width, hidden):
    hbm = pl.BlockSpec(memory_space=pl.ANY)
    vmem = pl.BlockSpec(memory_space=pltpu.VMEM)
    shape = jax.ShapeDtypeStruct
    outs = [shape(out.shape, BF), shape(ig.shape, BF), shape((win, width), F32)]
    outs += [shape((width, 3 * width // 2), F32), shape((width // 2, width), F32)]
    outs += [shape((width, hidden // 2), F32), shape((hidden // 2, width), F32)]
    outs += [shape((width,), F32)] * 4
    dma = pltpu.SemaphoreType.DMA
    scratch = [pltpu.VMEM(g.shape, BF) for g in grads]
    scratch += [pltpu.VMEM((g.size // g.shape[-1], g.shape[-1]), F32) for g in grads]
    scratch += [pltpu.VMEM((2,) + out.shape, BF), dma((len(NAMES) + 2,)), dma((len(NAMES) + 2,))]
    return pl.pallas_call(
        finish_kernel,
        out_shape=outs,
        in_specs=[hbm, hbm, vmem] + [hbm] * len(NAMES),
        out_specs=[hbm] * 7 + [vmem] * 4,
        scratch_shapes=scratch,
        compiler_params=pltpu.CompilerParams(vmem_limit_bytes=64 << 20),
        name="finish",
    )(out, ig, small, *grads)


def local(shards, tokens, segment_ids, cotangent, pos_table, w_qkv, w_out, w_up, w_down, g1, b1, g2, b2):
    dp_size, mp_size = shards
    width = tokens.shape[1]
    win = pos_table.shape[0]
    hidden = w_up.shape[1] * mp_size
    fused = dp_size == PIECES
    gains = [v.reshape(1, width) for v in (g1, b1, g2, b2)]
    if fused:
        out, ig, small, *grads = layer(
            True, tokens, cotangent, pos_table, segment_ids, w_qkv, w_out, w_up, w_down, *gains, hidden
        )
        return tuple(finish(out, ig, small, grads, win, width, hidden))
    windows = tokens.shape[0] // win
    seg = jnp.roll(segment_ids, -lax.axis_index("mp") * windows, axis=0)
    wq = lax.all_gather(w_qkv, "mp", axis=1, tiled=True)
    wo = lax.all_gather(w_out, "mp", axis=0, tiled=True)
    wu = lax.all_gather(w_up, "mp", axis=1, tiled=True)
    wd = lax.all_gather(w_down, "mp", axis=0, tiled=True)
    out, ig, small, *grads = layer(False, tokens, cotangent, pos_table, seg, wq, wo, wu, wd, *gains, hidden)
    g = dict(zip(NAMES, (v.astype(F32) for v in grads)))
    g = {
        k: v if k == "P" else lax.psum(lax.psum_scatter(v, "mp", scatter_dimension=0, tiled=False), "dp")
        for k, v in g.items()
    }
    pos, small = lax.psum((g["P"], small), ("dp", "mp"))
    scale = jnp.array([HD**-0.5, 1, 1], F32)[:, None, None]
    Q = [(g[k].reshape(width, 3, 2, HD) * scale).transpose(0, 2, 1, 3).reshape(width, 6 * HD) for k in ("Q0", "Q1")]
    return (
        out,
        ig,
        pos.reshape(win, width),
        jnp.concatenate(Q, axis=1),
        g["O"].reshape(-1, width),
        jnp.concatenate([g["U0"].reshape(width, -1), g["U1"].reshape(width, -1)], axis=1),
        jnp.concatenate([g["D0"].reshape(-1, width), g["D1"].reshape(-1, width)], axis=0),
        small[2],
        small[3],
        small[0],
        small[1],
    )


def solution(mesh):
    cut, copied = P(("dp", "mp"), None), P()
    columns, split_rows = P(None, "mp"), P("mp", None)
    weights = (columns, split_rows, columns, split_rows)
    return jax.shard_map(
        functools.partial(local, (mesh.shape["dp"], mesh.shape["mp"])),
        mesh=mesh,
        in_specs=(cut, P("dp", None), cut, copied) + weights + (copied,) * 4,
        out_specs=(cut, cut, copied) + weights + (copied,) * 4,
        check_vma=False,
    )
```

```python
import functools

import jax
import jax.numpy as jnp
from jax import lax
from jax.experimental import pallas as pl
from jax.experimental.pallas import tpu as pltpu
from jax.sharding import PartitionSpec as P

BF = jnp.bfloat16
F32 = jnp.float32
MESH = pl.DeviceIdType.MESH
HD = 64
EPSILON = 1e-05
NEG = -1e30
GELU_A = 0.7978845608028654
GELU_B = 0.044715

CHUNKS = {
    "D0": (32, 512),
    "D1": (32, 512),
    "U0": (32, 512),
    "U1": (32, 512),
    "O": (16, 512),
    "Q0": (32, 384),
    "QA": (16, 384),
    "QB": (16, 384),
    "P": (16, 512),
}
NAMES = tuple(CHUNKS)
DIRECT = ("QA", "QB", "P")
RESULTS = ("D0", "D1", "U0", "U1", "O", "Q0", "Q1", "P")
PIECES = 16

SCHEDULE = {
    ("down", 1): (("D0", 0),),
    ("down", 3): (("D1", 0),),
    ("slope", 0): (("D0", 1),),
    ("slope", 1): (("D1", 1),),
    ("up", 1): (("D0", 2), ("U0", 0),),
    ("up", 3): (("D1", 2), ("U0", 1), ("U1", 0),),
    ("nb", 0): (("D0", 3),),
    ("nb", 1): (("U1", 1),),
    ("nb", 2): (("D1", 3),),
    ("nb", 3): (("D0", 4), ("U0", 2),),
    ("O", 0): (("O", 0), ("sm", 0),),
    ("back0", 1): (("D1", 4), ("U1", 2), ("O", 1), ("sm", 1),),
    ("back0", 2): (("U0", 3),),
    ("back0", 3): (("D0", 5),),
    ("back1", 0): (("sm", 2),),
    ("back1", 1): (("D1", 5), ("U1", 3),),
    ("back1", 2): (("O", 2),),
    ("back1", 3): (("D0", 6), ("U0", 4), ("sm", 3),),
    ("q1", 0): (("D1", 6), ("U1", 4), ("Q0", 0),),
    ("add1", 0): (("O", 3),),
    ("back2", 0): (("sm", 4),),
    ("back2", 1): (("U0", 5), ("Q0", 1),),
    ("back2", 2): (("D0", 7),),
    ("back2", 3): (("U1", 5),),
    ("q2", 0): (("D1", 7), ("O", 4), ("QA", 0),),
    ("add2", 0): (("U0", 6),),
    ("back3", 1): (("Q0", 2), ("QA", 1),),
    ("back3", 2): (("U1", 6), ("O", 5),),
    ("P", 0): (("P", 0),),
    ("q3", 0): (("U0", 7), ("Q0", 3), ("QB", 0),),
    ("fin", 0): (("QA", 2), ("P", 1),),
    ("fin", 1): (("QB", 1),),
    ("fin", 3): (("U1", 7), ("Q0", 4),),
}
TAIL = (
    ("O", 6),
    ("QA", 3),
    ("P", 2),
    ("Q0", 5),
    ("QB", 2),
    ("QA", 4),
    ("O", 7),
    ("P", 3),
    ("QB", 3),
    ("Q0", 6),
    ("P", 4),
    ("QA", 5),
    ("QB", 4),
    ("QA", 6),
    ("Q0", 7),
    ("P", 5),
    ("P", 6),
    ("QB", 5),
    ("QB", 6),
)


def dot(left, right, left_dim=1, right_dim=0):
    return lax.dot_general(
        left, right, (((left_dim,), (right_dim,)), ((), ())), preferred_element_type=F32
    )


def lanes(shape):
    return lax.broadcasted_iota(jnp.int32, shape, len(shape) - 1)


def rows_of(w, win):
    return pl.ds(pl.multiple_of(w * win, win), win)


def columns_of(start, size):
    return pl.ds(pl.multiple_of(start, 128), size)


def row_mean(v):
    return jnp.mean(v, axis=-1, keepdims=True)


def kernel(fused, dims, *refs):
    win, width, hidden, windows = dims
    half_hidden = hidden // 2
    half = win // 2
    (tok_h, cot_h, pos_h, seg, wq_h, wo_h, wu_h, wd_h, g1, b1, g2, b2) = refs[:12]
    refs = refs[12:]
    out_h, ig_h, small_h = refs[:3]
    results = RESULTS if fused else NAMES
    F = dict(zip(results, refs[3 : 3 + len(results)]))
    b = dict(zip(scratch_of(fused, dims), refs[3 + len(results) :]))
    tok, cot, pos, augk = b["tok"], b["cot"], b["pos"], b["augk"]
    wq, wo, wu, wd = b["wq"], b["wo"], b["wu"], b["wd"]
    joined, mix, u1, rs1, pb, nb = b["joined"], b["mix"], b["u1"], b["rs1"], b["pb"], b["nb"]
    act, gp, augq, nf, small = b["act"], b["gp"], b["augq"], b["nf"], b["small"]
    G, R_mp, R_a, R_b, R_z = ({k: b.get(buf + k) for k in NAMES} for buf in ("G", "M", "A", "B", "Z"))
    in_sem, out_sem = b["in_sem"], b["out_sem"]

    pairs = width // 128

    copies = {}

    def fetch(name, src, dst, k):
        copies[name] = pltpu.make_async_copy(src, dst, in_sem.at[k])
        copies[name].start()

    if fused:
        wsem, csend, crecv, ssend, srecv, lsem = (
            b[k] for k in ("wsem", "csend", "crecv", "ssend", "srecv", "lsem")
        )
        dp = lax.axis_index("dp")
        mp = lax.axis_index("mp")
        zc = dp // 4
        yc = lax.rem(dp // 2, 2)
        xc = lax.rem(dp, 2)
        ac = jnp.where(mp == 0, xc, yc)
        bc = jnp.where(mp == 0, yc, xc)
        step_a = jnp.where(mp == 0, 1, 2)
        step_b = jnp.where(mp == 0, 2, 1)
        dev_mp = (dp, 1 - mp)
        dev_a = (dp + step_a * (1 - 2 * ac), mp)
        dev_b = (dp + step_b * (1 - 2 * bc), mp)
        dev_d = (dp + step_a * (1 - 2 * ac) + step_b * (1 - 2 * bc), mp)
        dev_x = (dp + 1 - 2 * xc, mp)
        dev_y = (dp + 2 * (1 - 2 * yc), mp)
        zs = [lax.rem(zc + k, 4) for k in (1, 2, 3)]
        dev_z = [(lax.rem(dp, 4) + 4 * z, mp) for z in zs]
        barrier = pltpu.get_barrier_semaphore()
        for dev in [dev_mp, dev_a, dev_b, dev_d] + dev_z:
            pl.semaphore_signal(barrier, inc=1, device_id=dev, device_id_type=MESH)

    raw_width = wq_h.shape[1]
    raw = act.at[pl.ds(0, width), pl.ds(0, raw_width)]
    fetch("wq", wq_h, raw, 2)
    fetch("tok", tok_h, tok, 0)
    fetch("pos", pos_h, pos, 1)
    wparts = []
    if fused:
        wparts.append((wo_h, wo.at[pl.ds(pl.multiple_of(mp * half, half), half), :]))
        wparts.append((wu_h, wu.at[:, columns_of(half_hidden * mp, half_hidden)]))
        wparts.append((wd_h, wd.at[pl.ds(pl.multiple_of(mp * half_hidden, half_hidden), half_hidden), :]))
    else:
        wparts += [(wo_h, wo), (wu_h, wu), (wd_h, wd)]
    for i, (src, dst) in enumerate(wparts):
        fetch("w%d" % i, src, dst, 5 + i)
    fetch("cot", cot_h, cot, 4)
    small[...] = jnp.zeros_like(small)
    rs1[...] = jnp.zeros_like(rs1)

    l64 = lax.rem(lanes((win, 128)), HD)
    lo = lanes((win, 128)) < HD

    columns = seg[...].astype(F32).T
    mine = (mp if fused else 0) * windows
    for w in range(windows):
        R = pl.ds(w * win, win)
        column = jnp.sum(
            jnp.where(lanes(columns.shape) == mine + w, columns, 0.0), axis=1, keepdims=True
        ).astype(jnp.int32)
        augk[R, :] = jnp.where((l64 == column) | ((l64 >= 8) & (l64 < 11)), 1.0, 0.0).astype(BF)

    copies["wq"].wait()
    own_columns = mp * raw_width // 3 if fused else 0
    for p in range(raw_width // 384):
        cut = [raw[:, pl.ds(p * 384 + 128 * i, 128)] for i in range(3)]
        low = lanes((width, 128)) < HD
        swapped = [pltpu.roll(c.astype(F32), HD, 1).astype(BF) for c in cut]
        q = jnp.where(low, cut[0], cut[1]) * BF(HD**-0.5)
        k = jnp.where(low, swapped[0], swapped[2])
        v = jnp.where(low, cut[1], cut[2])
        for i, part in enumerate((q, k, v)):
            wq[:, columns_of(own_columns + width * i + 128 * p, 128)] = part

    wremote = []
    if fused:
        pl.semaphore_wait(barrier, 7)
        slices = [wq.at[:, columns_of(own_columns + width * i, raw_width // 3)] for i in range(3)]
        for i, (src, dst) in enumerate([(x, x) for x in slices] + wparts):
            c = pltpu.make_async_remote_copy(
                src_ref=src, dst_ref=dst, send_sem=wsem.at[0, i], recv_sem=wsem.at[1, i],
                device_id=dev_mp, device_id_type=MESH,
            )
            c.start()
            wremote.append(c)

    def remote(src, dst, send, recv, dev):
        return pltpu.make_async_remote_copy(
            src_ref=src, dst_ref=dst, send_sem=send, recv_sem=recv, device_id=dev, device_id_type=MESH
        )

    def add(mine, got):
        mine[...] = mine[...] + got[...]

    def exchange(name, k):
        if not fused:
            return
        c = NAMES.index(name)
        g = G[name]
        direct = name in DIRECT
        own = g.at[mp]
        base = ac * 8 + bc * 4
        full = g.at[1 - mp]

        def send(src, dst, i, dev):
            return remote(src, dst, csend.at[c, i], crecv.at[c, i], dev)

        def to_z(src, dst_of):
            return [send(src(j), dst_of(j), 3 + j, dev_z[j]) for j in range(3)]

        if direct:
            slots = R_a[name]
            places = [(1 - ac) * 8 + bc * 4, ac * 8 + (1 - bc) * 4, (1 - ac) * 8 + (1 - bc) * 4]
            plane = [dev_a, dev_b, dev_d]
            stages = [
                lambda: [send(full, R_mp[name], 0, dev_mp)],
                lambda: [send(own.at[pl.ds(places[j], 4)], slots.at[j], 6 + j, plane[j]) for j in range(3)],
                lambda: [send(own.at[base + zs[j]], R_z[name].at[j], 3 + j, dev_z[j]) for j in range(3)],
                lambda: [send(full.at[base + zc], full.at[base + zc], 9 + j, dev_z[j]) for j in range(3)],
                lambda: [send(full.at[pl.ds(base, 4)], full.at[pl.ds(base, 4)], 12 + j, plane[j]) for j in range(3)],
                lambda: [send(full, b["X" + name], 1, dev_mp)],
            ]
        else:
            stages = [
                lambda: [send(full, R_mp[name], 0, dev_mp)],
                lambda: [send(own.at[pl.ds((1 - ac) * 8, 8)], R_a[name], 1, dev_a)],
                lambda: [send(own.at[pl.ds(ac * 8 + (1 - bc) * 4, 4)], R_b[name], 2, dev_b)],
                lambda: [send(own.at[base + zs[j]], R_z[name].at[j], 3 + j, dev_z[j]) for j in range(3)],
                lambda: [send(full.at[base + zc], full.at[base + zc], 6 + j, dev_z[j]) for j in range(3)],
                lambda: [send(full.at[pl.ds(base, 4)], full.at[pl.ds(base, 4)], 9, dev_b)],
                lambda: [send(full.at[pl.ds(ac * 8, 8)], full.at[pl.ds(ac * 8, 8)], 10, dev_a)],
            ]
        if 0 < k <= len(stages):
            for copy in stages[k - 1]():
                copy.wait()
        if k == 1:
            add(own, R_mp[name])
        if direct and k == 2:
            at = own.at[pl.ds(base, 4)]
            at[...] = (
                (at[...].astype(F32) + slots[0].astype(F32)) + (slots[1].astype(F32) + slots[2].astype(F32))
            ).astype(BF)
        if not direct and k == 2:
            add(own.at[pl.ds(ac * 8, 8)], R_a[name])
        if not direct and k == 3:
            add(own.at[pl.ds(base, 4)], R_b[name])
        if k == (3 if direct else 4):
            total = own[base + zc].astype(F32)
            for j in range(3):
                total = total + R_z[name][j].astype(F32)
            if name[0] == "Q":
                q, kk, v = total[:, :128] * (HD**-0.5), total[:, 128:256], total[:, 256:]
                total = jnp.concatenate(
                    [q[:, :HD], kk[:, :HD], v[:, :HD], q[:, HD:], kk[:, HD:], v[:, HD:]], axis=1
                )
            full[base + zc] = total.astype(BF)
        if k < len(stages):
            for copy in stages[k]():
                copy.start()
        if k == len(stages):
            results_out(name, True)

    def results_out(name, start):
        full, i = G[name].at[1 - mp], 2 * NAMES.index(name)
        if name not in DIRECT:
            moves = [pltpu.make_async_copy(full, F[name], lsem.at[i])]
        else:
            to = F["P" if name == "P" else "Q1"]
            moves = [pltpu.make_async_copy(full, to.at[mp], lsem.at[i])]
            moves.append(pltpu.make_async_copy(b["X" + name], to.at[1 - mp], lsem.at[i + 1]))

        def go():
            for m in moves:
                m.start() if start else m.wait()

        if name[0] == "Q" and name != "Q0":
            pl.when(mp == ("QA", "QB").index(name))(go)
        else:
            go()

    def exchange_small(k):
        if not fused:
            return
        legs = [(b["s_mp"], dev_mp, 0), (b["s_x"], dev_x, 1), (b["s_y"], dev_y, 2)]
        if k > 0 and k <= 3:
            buf, dev, s = legs[k - 1]
            remote(small, buf, ssend.at[s], srecv.at[s], dev).wait()
            small[...] = small[...] + buf[...]
        if k < 3:
            buf, dev, s = legs[k]
            remote(small, buf, ssend.at[s], srecv.at[s], dev).start()
        zcs = [remote(small, b["s_z"].at[zc], ssend.at[3 + j], srecv.at[3 + j], dev_z[j]) for j in range(3)]
        if k == 3:
            b["s_z"][zc] = small[...]
            for z in zcs:
                z.start()
        if k == 4:
            for z in zcs:
                z.wait()
            small[...] = (b["s_z"][0] + b["s_z"][1]) + (b["s_z"][2] + b["s_z"][3])

    causal = jnp.where(lanes((half, half)) <= lax.broadcasted_iota(jnp.int32, (half, half), 0), 0.0, NEG)
    def attend(w, p):
        R = rows_of(w, win)
        Q, K, V = (joined[R, columns_of(width * i + p * 128, 128)] for i in range(3))
        ak = augk[R, :]
        ones = jnp.ones((win, 128), BF)
        zero = jnp.zeros((win, 128), BF)
        aq = jnp.where(l64 < 8, (ones - ak) * BF(NEG), zero)
        qs, ks, vs = [], [], []
        for h in range(2):
            mine = lo if h == 0 else ~lo
            qs.append(jnp.where(mine, Q, aq))
            ks.append(jnp.where(mine, K, ak))
            vs.append(jnp.concatenate([jnp.where(mine, V, zero), jnp.where(mine, ones, zero)], axis=1))
        for qb in range(2):
            kl = half * (qb + 1)
            es, ms = [], []
            for h in range(2):
                s = dot(qs[h][qb * half : (qb + 1) * half], ks[h][:kl], 1, 1)
                if qb == 0:
                    s = s + causal
                else:
                    s = jnp.concatenate([s[:, :half], s[:, half:] + causal], axis=1)
                m = jnp.max(s, axis=1, keepdims=True)
                es.append(jnp.exp(s - m).astype(BF))
                ms.append(m)
            ov = dot(jnp.concatenate(es, axis=1), jnp.concatenate([v[:kl] for v in vs], axis=0))
            total = ov[:, 128:]
            rr = pl.ds(pl.multiple_of(w * win + qb * half, half), half)
            mix[rr, columns_of(p * 128, 128)] = (ov[:, :128] / total).astype(BF)
            low = lo[:half]
            lse = jnp.where(low, ms[0], ms[1]) + jnp.log(total)
            x = -pltpu.roll(lse, HD, 1)
            hi = x.astype(BF)
            x = x - hi.astype(F32)
            mid = x.astype(BF)
            last = (x - mid.astype(F32)).astype(BF)
            l6 = l64[:half]
            a = aq[qb * half : (qb + 1) * half]
            a = jnp.where(l6 == 8, hi, a)
            a = jnp.where(l6 == 9, mid, a)
            augq[rr, columns_of(p * 128, 128)] = jnp.where(l6 == 10, last, a)

    copies["tok"].wait()
    copies["pos"].wait()

    def place(w, _):
        R = rows_of(w, win)
        pb[R, :] = (tok[R, :].astype(F32) + pos[...].astype(F32)).astype(BF)
        return 0

    lax.fori_loop(0, windows, place, 0)
    for part in range(2 if fused else 1):
        if part:
            for c in wremote[:3]:
                c.wait()
        span = width // 2 if fused else width
        start = (mp if part == 0 else 1 - mp) * span if fused else 0

        def project(w, _):
            R = rows_of(w, win)
            for i in range(3):
                cs = columns_of(width * i + start, span)
                joined[R, cs] = dot(pb[R, :], wq[:, cs]).astype(BF)
            return 0

        lax.fori_loop(0, windows, project, 0)

    def attend_window(w, _):
        for p in range(pairs):
            attend(w, p)
        return 0

    lax.fori_loop(0, windows, attend_window, 0)

    for i in range(3):
        copies["w%d" % i].wait()
    for c in wremote[3:]:
        c.wait()
    copies["cot"].wait()

    def feed(w, _):
        R = rows_of(w, win)
        r1 = (tok[R, :].astype(F32) + pos[...].astype(F32)) + dot(mix[R, :], wo[...])
        center = r1 - row_mean(r1)
        rstd = lax.rsqrt(row_mean(center * center) + EPSILON)
        unit = center * rstd
        u1[R, :] = unit.astype(BF)
        rs1[...] = jnp.where(lanes((win, 128)) == w, rstd, rs1[...])
        normed = unit * g1[...] + b1[...]
        nf[...] = normed
        nb[R, :] = normed.astype(BF)

        r2 = nf[...]
        for c in range(hidden // 512):
            cs = pl.ds(c * 512, 512)
            v = dot(nb[R, :], wu[:, cs]).astype(BF)
            v2 = v * v
            t = jnp.tanh(v * (BF(GELU_A) + BF(GELU_A * GELU_B) * v2))
            h = BF(0.5) + BF(0.5) * t
            active = v * h
            act[R, cs] = active
            gp[R, cs] = h + h * ((BF(1) - h) * (v * (BF(2 * GELU_A) + BF(6 * GELU_A * GELU_B) * v2)))
            r2 = r2 + dot(active, wd[cs, :])
        center = r2 - row_mean(r2)
        rstd = lax.rsqrt(row_mean(center * center) + EPSILON)
        unit = center * rstd
        tok[R, :] = (unit * g2[...] + b2[...]).astype(BF)
        up = cot[R, :].astype(F32)
        small[0:1, :] += jnp.sum(up * unit, axis=0, keepdims=True)
        small[1:2, :] += jnp.sum(up, axis=0, keepdims=True)
        e = up * g2[...]
        cot[R, :] = (rstd * (e - row_mean(e) - unit * row_mean(e * unit))).astype(BF)
        return 0

    lax.fori_loop(0, windows, feed, 0)
    out_copy = pltpu.make_async_copy(tok, out_h, out_sem.at[0])
    out_copy.start()

    def hooked(phase, body, count, unroll=True):
        if unroll:
            for t in range(count):
                body(t, 0)
                run_steps(SCHEDULE.get((phase, t), ()))
            return

        def one(t, _):
            body(t, 0)
            for at in range(count):
                steps = SCHEDULE.get((phase, at))
                if steps:
                    pl.when(t == at)(functools.partial(run_steps, steps))
            return 0

        lax.fori_loop(0, count, one, 0)

    def run_steps(steps):
        for name, k in steps:
            if name == "sm":
                exchange_small(k)
            else:
                exchange(name, k)

    halves = hidden // 1024

    def down_tile(t, _):
        part, m = t // 2, t % 2
        tile = m * halves + part
        d = dot(act[:, columns_of(tile * 512, 512)], cot[...], 0, 0).astype(BF).reshape(16, 32, 512)
        G["D%d" % part][m] = d
        return 0

    hooked("down", down_tile, hidden // 512)

    def slope(w, _):
        R = rows_of(w, win)
        for c in range(hidden // 512):
            cs = pl.ds(c * 512, 512)
            d = dot(cot[R, :], wd[pl.ds(c * 512, 512), :], 1, 1)
            gp[R, cs] = (d * gp[R, cs].astype(F32)).astype(BF)
        return 0

    hooked("slope", slope, windows)

    def up_tile(t, _):
        part, m = t // 2, t % 2
        tile = m * halves + part
        d = dot(nb[...], gp[:, columns_of(tile * 512, 512)], 0, 0).astype(BF).reshape(16, 32, 512)
        G["U%d" % part][m] = d
        return 0

    hooked("up", up_tile, hidden // 512)

    def norm_back(w, _):
        R = rows_of(w, win)
        ng = cot[R, :].astype(F32) + dot(gp[R, :], wu[...], 1, 1)
        unit = u1[R, :].astype(F32)
        small[2:3, :] += jnp.sum(ng * unit, axis=0, keepdims=True)
        small[3:4, :] += jnp.sum(ng, axis=0, keepdims=True)
        e = ng * g1[...]
        rstd = jnp.sum(jnp.where(lanes((win, 128)) == w, rs1[...], 0.0), axis=1, keepdims=True)
        rg = (rstd * (e - row_mean(e) - unit * row_mean(e * unit))).astype(BF)
        cot[R, :] = rg
        u1[R, :] = dot(rg, wo[...], 1, 1).astype(BF)
        return 0

    hooked("nb", norm_back, windows)

    G["O"][...] = dot(mix[...], cot[...], 0, 0).astype(BF).reshape(2, 16, half // 16, 512)
    run_steps(SCHEDULE.get(("O", 0), ()))

    flip = (lax.broadcasted_iota(jnp.int32, (256, 128), 0) % 128 < HD) != (lanes((256, 128)) < HD)
    swap = jnp.where(flip, 1.0, 0.0).astype(BF)

    def attend_back(w, p):
        R = rows_of(w, win)
        pc = columns_of(p * 128, 128)
        Q, K, V = (joined[R, columns_of(width * i + p * 128, 128)] for i in range(3))
        D = u1[R, pc]
        prod = D.astype(F32) * mix[R, pc].astype(F32)
        ph = prod.astype(BF)
        pr = (prod - ph.astype(F32)).astype(BF)
        x = -dot(jnp.concatenate([ph, pr], axis=1), swap)
        hi = x.astype(BF)
        mid = (x - hi.astype(F32)).astype(BF)
        zero = jnp.zeros((win, 128), BF)
        ad = jnp.where(l64 == 8, hi, jnp.where(l64 == 9, mid, zero))
        av = jnp.where((l64 == 8) | (l64 == 9), jnp.ones((win, 128), BF), zero)
        aq, ak = augq[R, pc], augk[R, :]
        QT, DT = Q.T, D.T
        probs, grads = [[], []], [[], []]
        for h in range(2):
            mine = lo if h == 0 else ~lo
            qa, ka, va, da = (jnp.where(mine, i, j) for i, j in ((Q, aq), (K, ak), (V, av), (D, ad)))
            for qb in range(2):
                kl = half * (qb + 1)
                qs = slice(qb * half, kl)
                s = dot(qa[qs], ka[:kl], 1, 1)
                s = s + causal if qb == 0 else jnp.concatenate([s[:, :half], s[:, half:] + causal], axis=1)
                e = jnp.exp(s)
                grads[h].append((e * dot(da[qs], va[:kl], 1, 1)).astype(BF))
                probs[h].append(e.astype(BF))
        dq, dk, dv = [None, None], [], []
        for h in range(2):
            km = jnp.where(lo if h == 0 else ~lo, K, zero)
            hs = slice(h * HD, (h + 1) * HD)
            for qb in range(2):
                x = dot(grads[h][qb], km[: half * (qb + 1)])
                dq[qb] = x if h == 0 else dq[qb] + x
            for left, (first, second), to in ((QT, grads[h], dk), (DT, probs[h], dv)):
                early = dot(left[hs], jnp.concatenate([first, second[:, :half]], axis=0))
                to.append(jnp.concatenate([early, dot(left[hs, half:], second[:, half:])], axis=1))
        for i in range(2):
            joined[pl.ds(pl.multiple_of(w * win + i * half, half), half), pc] = dq[i].astype(BF)
        for i, v in enumerate((dk, dv)):
            joined[R, columns_of(width * (i + 1) + p * 128, 128)] = jnp.concatenate(v, axis=0).astype(BF).T

    def qkv_grad(*some):
        for m in range(2):
            total = None
            for w in range(windows):
                R = pl.ds(w * win, win)
                right = jnp.concatenate(
                    [joined[R, pl.ds(width * i + p * 128, 128)] for p in some for i in range(3)], axis=1
                )
                d = dot(pb[R, pl.ds(m * half, half)], right, 0, 0)
                total = d if total is None else total + d
            total = total.astype(BF)
            if len(some) == 2:
                for j in range(2):
                    G["Q0"][j, pl.ds(8 * m, 8)] = total[:, 384 * j : 384 * (j + 1)].reshape(8, 32, 384)
            else:
                G["QA" if some[0] == 1 else "QB"][m] = total.reshape(16, 16, 384)

    def add_position(p):
        cols = [pl.ds(width * i + p * 128, 128) for i in range(3)]
        total = []
        for c in cols:
            v = joined[pl.ds(0, win), c].astype(F32)
            for w in range(1, windows):
                v = v + joined[pl.ds(w * win, win), c].astype(F32)
            total.append(v.astype(BF))
        part = dot(jnp.concatenate(total, axis=1), jnp.concatenate([wq[:, c] for c in cols], axis=1), 1, 1)
        nf[...] = nf[...] + part

    def steps_at(phase, at):
        run_steps(SCHEDULE.get((phase, at), ()))

    total = cot[pl.ds(0, win), :].astype(F32)
    for w in range(1, windows):
        total = total + cot[pl.ds(w * win, win), :].astype(F32)
    nf[...] = total
    order = (0, 2, 1, 3)
    for i, p in enumerate(order):
        hooked("back%d" % i, lambda t, _: attend_back(t, p), windows, unroll=False)
        if i == 3:
            add_position(p)
            G["P"][...] = nf[...].astype(BF).reshape(2, 16, half // 16, 512)
            steps_at("P", 0)
        if i > 0:
            qkv_grad(*((0, 2) if i == 1 else (p,)))
        steps_at("q%d" % i, 0)
        if i < 3:
            add_position(p)
            steps_at("add%d" % i, 0)

    def finish(w, _):
        R = rows_of(w, win)
        cot[R, :] = (cot[R, :].astype(F32) + dot(joined[R, :], wq[...], 1, 1)).astype(BF)
        return 0

    hooked("fin", finish, windows)
    ig_copy = pltpu.make_async_copy(cot, ig_h, out_sem.at[1])
    ig_copy.start()
    small_copy = pltpu.make_async_copy(small, small_h, out_sem.at[2])
    small_copy.start()
    run_steps(TAIL)
    if fused:
        for name in NAMES:
            results_out(name, False)
    if not fused:
        outs = [pltpu.make_async_copy(G[nm], F[nm], in_sem.at[i]) for i, nm in enumerate(NAMES)]
        for c in outs:
            c.start()
        for c in outs:
            c.wait()
    out_copy.wait()
    ig_copy.wait()
    small_copy.wait()


def scratch_of(fused, dims):
    win, width, hidden, windows = dims
    rows = win * windows
    V, dma = pltpu.VMEM, pltpu.SemaphoreType.DMA
    b = {k: V((rows, width), BF) for k in ("tok", "cot", "mix", "u1", "pb", "nb", "augq")}
    b.update({k: V((rows, hidden), BF) for k in ("act", "gp")})
    b.update(
        pos=V((win, width), BF),
        augk=V((rows, 128), BF),
        wq=V((width, 3 * width), BF),
        wo=V((width, width), BF),
        wu=V((width, hidden), BF),
        wd=V((hidden, width), BF),
        joined=V((rows, 3 * width), BF),
        rs1=V((win, 128), F32),
        nf=V((win, width), F32),
        small=V((8, width), F32),
        in_sem=dma((12,)),
        out_sem=dma((3,)),
    )
    b.update({"G" + k: V((2, PIECES) + CHUNKS[k], BF) for k in NAMES})
    if fused:
        for k in NAMES:
            lead = {"M": (16,), "A": (8,), "B": (4,), "Z": (3,)}
            if k in DIRECT:
                lead = {"M": (16,), "A": (3, 4), "Z": (3,), "X": (16,)}
            b.update({buf + k: V(n + CHUNKS[k], BF) for buf, n in lead.items()})
        b.update({k: V((8, width), F32) for k in ("s_mp", "s_x", "s_y")})
        b.update(
            s_z=V((4, 8, width), F32),
            wsem=dma((2, 6)),
            csend=dma((len(NAMES), 15)),
            crecv=dma((len(NAMES), 15)),
            ssend=dma((6,)),
            srecv=dma((6,)),
            lsem=dma((2 * len(NAMES),)),
        )
    return b


def layer(fused, tok, cot, pos, seg, wq, wo, wu, wd, g1, b1, g2, b2, hidden):
    rows, width = tok.shape
    win = pos.shape[0]
    windows = rows // win
    hbm = pl.BlockSpec(memory_space=pl.ANY)
    vmem = pl.BlockSpec(memory_space=pltpu.VMEM)
    shape = jax.ShapeDtypeStruct
    full = {k: (PIECES,) + v if fused and k not in DIRECT else (2, PIECES) + v for k, v in CHUNKS.items()}
    full["Q1"] = full["QA"]
    outs = [shape((rows, width), BF), shape((rows, width), BF), shape((8, width), F32)]
    outs += [shape(full[k], BF) for k in (RESULTS if fused else NAMES)]
    scratch = list(scratch_of(fused, (win, width, hidden, windows)).values())
    params = dict(vmem_limit_bytes=64 << 20)
    if fused:
        params.update(collective_id=0, has_side_effects=True)
    return pl.pallas_call(
        functools.partial(kernel, fused, (win, width, hidden, windows)),
        out_shape=outs,
        in_specs=[hbm] * 3 + [vmem] + [hbm] * 4 + [vmem] * 4,
        out_specs=[hbm] * len(outs),
        scratch_shapes=scratch,
        compiler_params=pltpu.CompilerParams(**params),
        name="layer",
    )(tok, cot, pos, seg, wq, wo, wu, wd, g1, b1, g2, b2)


def finish_kernel(*refs):
    (out_h, ig_h, small), grads = refs[:3], dict(zip(RESULTS, refs[3 : 3 + len(RESULTS)]))
    refs = refs[3 + len(RESULTS) :]
    out_o, ig_o, pos_o, qkv_o, wo_o, up_o, down_o = refs[:7]
    norms = refs[7:11]
    refs = refs[11:]
    got = dict(zip(RESULTS, refs[: len(RESULTS)]))
    wide = dict(zip(RESULTS, refs[len(RESULTS) : 2 * len(RESULTS)]))
    held, in_sem, out_sem = refs[2 * len(RESULTS) :]
    last, loads, passed = [], [], []
    for i, (src, dst) in enumerate(((out_h, out_o), (ig_h, ig_o))):
        passed.append(pltpu.make_async_copy(src, held.at[i], in_sem.at[len(RESULTS) + i]))
        last.append(pltpu.make_async_copy(held.at[i], dst, out_sem.at[len(RESULTS) + i]))
    for c in passed:
        c.start()
    for i, k in enumerate(RESULTS):
        loads.append(pltpu.make_async_copy(grads[k], got[k], in_sem.at[i]))
        loads[-1].start()
    rows = down_o.shape[0] // 2
    places = {
        "D0": down_o.at[pl.ds(0, rows)],
        "D1": down_o.at[pl.ds(rows, rows)],
        "U0": up_o.at[:, pl.ds(0, 512)],
        "U1": up_o.at[:, pl.ds(512, 512)],
        "O": wo_o,
        "Q0": qkv_o.at[:, pl.ds(0, 384)],
        "Q1": qkv_o.at[:, pl.ds(384, 384)],
        "P": pos_o,
    }
    for i in range(2):
        passed[i].wait()
        last[i].start()
    for i, k in enumerate(RESULTS):
        loads[i].wait()
        wide[k][...] = got[k][...].astype(F32).reshape(wide[k].shape)
        last.append(pltpu.make_async_copy(wide[k], places[k], out_sem.at[i]))
        last[-1].start()
    for ref, row in zip(norms, (2, 3, 0, 1)):
        ref[...] = small[row]
    for c in last:
        c.wait()


def finish(out, ig, small, grads, win, width, hidden):
    hbm = pl.BlockSpec(memory_space=pl.ANY)
    vmem = pl.BlockSpec(memory_space=pltpu.VMEM)
    shape = jax.ShapeDtypeStruct
    outs = [shape(out.shape, BF), shape(ig.shape, BF), shape((win, width), F32)]
    outs += [shape((width, 3 * width // 2), F32), shape((width // 2, width), F32)]
    outs += [shape((width, hidden // 2), F32), shape((hidden // 2, width), F32)]
    outs += [shape((width,), F32)] * 4
    dma = pltpu.SemaphoreType.DMA
    scratch = [pltpu.VMEM(g.shape, BF) for g in grads]
    scratch += [pltpu.VMEM((g.size // g.shape[-1], g.shape[-1]), F32) for g in grads]
    scratch += [pltpu.VMEM((2,) + out.shape, BF), dma((len(RESULTS) + 2,)), dma((len(RESULTS) + 2,))]
    return pl.pallas_call(
        finish_kernel,
        out_shape=outs,
        in_specs=[hbm, hbm, vmem] + [hbm] * len(RESULTS),
        out_specs=[hbm] * 7 + [vmem] * 4,
        scratch_shapes=scratch,
        compiler_params=pltpu.CompilerParams(vmem_limit_bytes=64 << 20),
        name="finish",
    )(out, ig, small, *grads)


def local(shards, tokens, segment_ids, cotangent, pos_table, w_qkv, w_out, w_up, w_down, g1, b1, g2, b2):
    dp_size, mp_size = shards
    width = tokens.shape[1]
    win = pos_table.shape[0]
    hidden = w_up.shape[1] * mp_size
    fused = dp_size == PIECES
    gains = [v.reshape(1, width) for v in (g1, b1, g2, b2)]
    if fused:
        out, ig, small, *grads = layer(
            True, tokens, cotangent, pos_table, segment_ids, w_qkv, w_out, w_up, w_down, *gains, hidden
        )
        return tuple(finish(out, ig, small, grads, win, width, hidden))
    windows = tokens.shape[0] // win
    seg = jnp.roll(segment_ids, -lax.axis_index("mp") * windows, axis=0)
    wq = lax.all_gather(w_qkv, "mp", axis=1, tiled=True)
    wo = lax.all_gather(w_out, "mp", axis=0, tiled=True)
    wu = lax.all_gather(w_up, "mp", axis=1, tiled=True)
    wd = lax.all_gather(w_down, "mp", axis=0, tiled=True)
    out, ig, small, *grads = layer(False, tokens, cotangent, pos_table, seg, wq, wo, wu, wd, *gains, hidden)
    g = dict(zip(NAMES, (v.astype(F32) for v in grads)))
    g = {
        k: v if k in DIRECT else lax.psum(lax.psum_scatter(v, "mp", scatter_dimension=0, tiled=False), "dp")
        for k, v in g.items()
    }
    pos, QA, QB, small = lax.psum((g["P"], g["QA"], g["QB"], small), ("dp", "mp"))
    g["Q1"] = jnp.where(lax.axis_index("mp") == 0, QA, QB)
    scale = jnp.array([HD**-0.5, 1, 1], F32)[:, None, None]
    Q = [(g[k].reshape(width, 3, 2, HD) * scale).transpose(0, 2, 1, 3).reshape(width, 6 * HD) for k in ("Q0", "Q1")]
    return (
        out,
        ig,
        pos.reshape(win, width),
        jnp.concatenate(Q, axis=1),
        g["O"].reshape(-1, width),
        jnp.concatenate([g["U0"].reshape(width, -1), g["U1"].reshape(width, -1)], axis=1),
        jnp.concatenate([g["D0"].reshape(-1, width), g["D1"].reshape(-1, width)], axis=0),
        small[2],
        small[3],
        small[0],
        small[1],
    )


def solution(mesh):
    cut, copied = P(("dp", "mp"), None), P()
    columns, split_rows = P(None, "mp"), P("mp", None)
    weights = (columns, split_rows, columns, split_rows)
    return jax.shard_map(
        functools.partial(local, (mesh.shape["dp"], mesh.shape["mp"])),
        mesh=mesh,
        in_specs=(cut, P("dp", None), cut, copied) + weights + (copied,) * 4,
        out_specs=(cut, cut, copied) + weights + (copied,) * 4,
        check_vma=False,
    )
```

```python
import functools

import jax
import jax.numpy as jnp
from jax import lax
from jax.experimental import pallas as pl
from jax.experimental.pallas import tpu as pltpu
from jax.sharding import PartitionSpec as P

BF = jnp.bfloat16
F32 = jnp.float32
MESH = pl.DeviceIdType.MESH
HD = 64
EPSILON = 1e-05
NEG = -1e30
GELU_A = 0.7978845608028654
GELU_B = 0.044715

CHUNKS = {
    "D0": (32, 512),
    "D1": (32, 512),
    "U0": (32, 512),
    "U1": (32, 512),
    "O": (16, 512),
    "Q0": (32, 384),
    "QA": (16, 384),
    "QB": (16, 384),
    "P": (16, 512),
}
NAMES = tuple(CHUNKS)
DIRECT = ("QA", "QB", "P")
RESULTS = ("D0", "D1", "U0", "U1", "O", "Q0", "Q1", "P")
PIECES = 16

SCHEDULE = {
    ("down", 1): (("D0", 0),),
    ("down", 3): (("D1", 0),),
    ("slope", 0): (("D0", 1),),
    ("slope", 1): (("D1", 1),),
    ("up", 1): (("D0", 2), ("U0", 0),),
    ("up", 3): (("D1", 2), ("U0", 1), ("U1", 0),),
    ("nb", 0): (("D0", 3),),
    ("nb", 1): (("U1", 1),),
    ("nb", 2): (("D1", 3),),
    ("nb", 3): (("D0", 4), ("U0", 2),),
    ("O", 0): (("O", 0), ("sm", 0),),
    ("back0", 1): (("D1", 4), ("U1", 2), ("O", 1), ("sm", 1),),
    ("back0", 2): (("U0", 3),),
    ("back0", 3): (("D0", 5),),
    ("back1", 0): (("sm", 2),),
    ("back1", 1): (("D1", 5), ("U1", 3),),
    ("back1", 2): (("O", 2),),
    ("back1", 3): (("D0", 6), ("U0", 4), ("sm", 3),),
    ("q1", 0): (("D1", 6), ("U1", 4), ("Q0", 0),),
    ("add1", 0): (("O", 3),),
    ("back2", 0): (("sm", 4),),
    ("back2", 1): (("U0", 5), ("Q0", 1),),
    ("back2", 2): (("D0", 7),),
    ("back2", 3): (("U1", 5),),
    ("q2", 0): (("D1", 7), ("O", 4), ("QA", 0),),
    ("add2", 0): (("U0", 6),),
    ("back3", 1): (("Q0", 2), ("QA", 1),),
    ("back3", 2): (("U1", 6), ("O", 5),),
    ("P", 0): (("P", 0),),
    ("q3", 0): (("U0", 7), ("Q0", 3), ("QB", 0),),
    ("fin", 0): (("QA", 2), ("P", 1),),
    ("fin", 1): (("QB", 1),),
    ("fin", 3): (("U1", 7), ("Q0", 4),),
}
TAIL = (
    ("O", 6),
    ("QA", 3),
    ("P", 2),
    ("Q0", 5),
    ("QB", 2),
    ("QA", 4),
    ("O", 7),
    ("P", 3),
    ("QB", 3),
    ("Q0", 6),
    ("P", 4),
    ("QA", 5),
    ("QB", 4),
    ("QA", 6),
    ("Q0", 7),
    ("P", 5),
    ("P", 6),
    ("QB", 5),
    ("QB", 6),
)


def dot(left, right, left_dim=1, right_dim=0):
    return lax.dot_general(
        left, right, (((left_dim,), (right_dim,)), ((), ())), preferred_element_type=F32
    )


def lanes(shape):
    return lax.broadcasted_iota(jnp.int32, shape, len(shape) - 1)


def rows_of(w, win):
    return pl.ds(pl.multiple_of(w * win, win), win)


def columns_of(start, size):
    return pl.ds(pl.multiple_of(start, 128), size)


def row_mean(v):
    return jnp.mean(v, axis=-1, keepdims=True)


def kernel(fused, dims, *refs):
    win, width, hidden, windows = dims
    half_hidden = hidden // 2
    half = win // 2
    (tok_h, cot_h, pos_h, seg, wq_h, wo_h, wu_h, wd_h, g1, b1, g2, b2) = refs[:12]
    refs = refs[12:]
    out_h, ig_h, small_h = refs[:3]
    results = RESULTS if fused else NAMES
    F = dict(zip(results, refs[3 : 3 + len(results)]))
    b = dict(zip(scratch_of(fused, dims), refs[3 + len(results) :]))
    tok, cot, pos, augk = b["tok"], b["cot"], b["pos"], b["augk"]
    wq, wo, wu, wd = b["wq"], b["wo"], b["wu"], b["wd"]
    joined, mix, u1, rs1, pb, nb = b["joined"], b["mix"], b["u1"], b["rs1"], b["pb"], b["nb"]
    act, gp, augq, nf, small = b["act"], b["gp"], b["augq"], b["nf"], b["small"]
    G, R_mp, R_a, R_b, R_z = ({k: b.get(buf + k) for k in NAMES} for buf in ("G", "M", "A", "B", "Z"))
    in_sem, out_sem = b["in_sem"], b["out_sem"]

    pairs = width // 128

    copies = {}

    def fetch(name, src, dst, k):
        copies[name] = pltpu.make_async_copy(src, dst, in_sem.at[k])
        copies[name].start()

    if fused:
        wsem, csend, crecv, ssend, srecv, lsem = (
            b[k] for k in ("wsem", "csend", "crecv", "ssend", "srecv", "lsem")
        )
        dp = lax.axis_index("dp")
        mp = lax.axis_index("mp")
        zc = dp // 4
        yc = lax.rem(dp // 2, 2)
        xc = lax.rem(dp, 2)
        ac = jnp.where(mp == 0, xc, yc)
        bc = jnp.where(mp == 0, yc, xc)
        step_a = jnp.where(mp == 0, 1, 2)
        step_b = jnp.where(mp == 0, 2, 1)
        dev_mp = (dp, 1 - mp)
        dev_a = (dp + step_a * (1 - 2 * ac), mp)
        dev_b = (dp + step_b * (1 - 2 * bc), mp)
        dev_d = (dp + step_a * (1 - 2 * ac) + step_b * (1 - 2 * bc), mp)
        dev_x = (dp + 1 - 2 * xc, mp)
        dev_y = (dp + 2 * (1 - 2 * yc), mp)
        zs = [lax.rem(zc + k, 4) for k in (1, 2, 3)]
        dev_z = [(lax.rem(dp, 4) + 4 * z, mp) for z in zs]
        barrier = pltpu.get_barrier_semaphore()
        for dev in [dev_mp, dev_a, dev_b, dev_d] + dev_z:
            pl.semaphore_signal(barrier, inc=1, device_id=dev, device_id_type=MESH)

    raw_width = wq_h.shape[1]
    raw = act.at[pl.ds(0, width), pl.ds(0, raw_width)]
    fetch("wq", wq_h, raw, 2)
    fetch("tok", tok_h, tok, 0)
    fetch("pos", pos_h, pos, 1)
    wparts = []
    if fused:
        wparts.append((wo_h, wo.at[pl.ds(pl.multiple_of(mp * half, half), half), :]))
        wparts.append((wu_h, wu.at[:, columns_of(half_hidden * mp, half_hidden)]))
        wparts.append((wd_h, wd.at[pl.ds(pl.multiple_of(mp * half_hidden, half_hidden), half_hidden), :]))
    else:
        wparts += [(wo_h, wo), (wu_h, wu), (wd_h, wd)]
    for i, (src, dst) in enumerate(wparts):
        fetch("w%d" % i, src, dst, 5 + i)
    fetch("cot", cot_h, cot, 4)
    small[...] = jnp.zeros_like(small)
    rs1[...] = jnp.zeros_like(rs1)

    l64 = lax.rem(lanes((win, 128)), HD)
    lo = lanes((win, 128)) < HD

    columns = seg[...].astype(F32).T
    mine = (mp if fused else 0) * windows
    for w in range(windows):
        R = pl.ds(w * win, win)
        column = jnp.sum(
            jnp.where(lanes(columns.shape) == mine + w, columns, 0.0), axis=1, keepdims=True
        ).astype(jnp.int32)
        augk[R, :] = jnp.where((l64 == column) | ((l64 >= 8) & (l64 < 11)), 1.0, 0.0).astype(BF)

    copies["wq"].wait()
    own_columns = mp * raw_width // 3 if fused else 0
    for p in range(raw_width // 384):
        cut = [raw[:, pl.ds(p * 384 + 128 * i, 128)] for i in range(3)]
        low = lanes((width, 128)) < HD
        swapped = [pltpu.roll(c.astype(F32), HD, 1).astype(BF) for c in cut]
        q = jnp.where(low, cut[0], cut[1]) * BF(HD**-0.5)
        k = jnp.where(low, swapped[0], swapped[2])
        v = jnp.where(low, cut[1], cut[2])
        for i, part in enumerate((q, k, v)):
            wq[:, columns_of(own_columns + width * i + 128 * p, 128)] = part

    wremote = []
    if fused:
        pl.semaphore_wait(barrier, 7)
        slices = [wq.at[:, columns_of(own_columns + width * i, raw_width // 3)] for i in range(3)]
        for i, (src, dst) in enumerate([(x, x) for x in slices] + wparts):
            c = pltpu.make_async_remote_copy(
                src_ref=src, dst_ref=dst, send_sem=wsem.at[0, i], recv_sem=wsem.at[1, i],
                device_id=dev_mp, device_id_type=MESH,
            )
            c.start()
            wremote.append(c)

    def remote(src, dst, send, recv, dev):
        return pltpu.make_async_remote_copy(
            src_ref=src, dst_ref=dst, send_sem=send, recv_sem=recv, device_id=dev, device_id_type=MESH
        )

    def add(mine, got):
        mine[...] = mine[...] + got[...]

    def exchange(name, k):
        if not fused:
            return
        c = NAMES.index(name)
        g = G[name]
        direct = name in DIRECT
        own = g.at[mp]
        base = ac * 8 + bc * 4
        full = g.at[1 - mp]

        def send(src, dst, i, dev):
            return remote(src, dst, csend.at[c, i], crecv.at[c, i], dev)

        def to_z(src, dst_of):
            return [send(src(j), dst_of(j), 3 + j, dev_z[j]) for j in range(3)]

        if direct:
            slots = R_a[name]
            places = [(1 - ac) * 8 + bc * 4, ac * 8 + (1 - bc) * 4, (1 - ac) * 8 + (1 - bc) * 4]
            plane = [dev_a, dev_b, dev_d]
            stages = [
                lambda: [send(full, R_mp[name], 0, dev_mp)],
                lambda: [send(own.at[pl.ds(places[j], 4)], slots.at[j], 6 + j, plane[j]) for j in range(3)],
                lambda: [send(own.at[base + zs[j]], R_z[name].at[j], 3 + j, dev_z[j]) for j in range(3)],
                lambda: [send(full.at[base + zc], full.at[base + zc], 9 + j, dev_z[j]) for j in range(3)],
                lambda: [send(full.at[pl.ds(base, 4)], full.at[pl.ds(base, 4)], 12 + j, plane[j]) for j in range(3)],
                lambda: [send(full, b["X" + name], 1, dev_mp)],
            ]
        else:
            stages = [
                lambda: [send(full, R_mp[name], 0, dev_mp)],
                lambda: [send(own.at[pl.ds((1 - ac) * 8, 8)], R_a[name], 1, dev_a)],
                lambda: [send(own.at[pl.ds(ac * 8 + (1 - bc) * 4, 4)], R_b[name], 2, dev_b)],
                lambda: [send(own.at[base + zs[j]], R_z[name].at[j], 3 + j, dev_z[j]) for j in range(3)],
                lambda: [send(full.at[base + zc], full.at[base + zc], 6 + j, dev_z[j]) for j in range(3)],
                lambda: [send(full.at[pl.ds(base, 4)], full.at[pl.ds(base, 4)], 9, dev_b)],
                lambda: [send(full.at[pl.ds(ac * 8, 8)], full.at[pl.ds(ac * 8, 8)], 10, dev_a)],
            ]
        if 0 < k <= len(stages):
            for copy in stages[k - 1]():
                copy.wait()
        if k == 1:
            add(own, R_mp[name])
        if direct and k == 2:
            at = own.at[pl.ds(base, 4)]
            at[...] = (
                (at[...].astype(F32) + slots[0].astype(F32)) + (slots[1].astype(F32) + slots[2].astype(F32))
            ).astype(BF)
        if not direct and k == 2:
            add(own.at[pl.ds(ac * 8, 8)], R_a[name])
        if not direct and k == 3:
            add(own.at[pl.ds(base, 4)], R_b[name])
        if k == (3 if direct else 4):
            total = own[base + zc].astype(F32)
            for j in range(3):
                total = total + R_z[name][j].astype(F32)
            if name[0] == "Q":
                q, kk, v = total[:, :128] * (HD**-0.5), total[:, 128:256], total[:, 256:]
                total = jnp.concatenate(
                    [q[:, :HD], kk[:, :HD], v[:, :HD], q[:, HD:], kk[:, HD:], v[:, HD:]], axis=1
                )
            full[base + zc] = total.astype(BF)
        if k < len(stages):
            for copy in stages[k]():
                copy.start()
        if k == len(stages):
            results_out(name, True)

    def results_out(name, start):
        full, i = G[name].at[1 - mp], 2 * NAMES.index(name)
        if name not in DIRECT:
            moves = [pltpu.make_async_copy(full, F[name], lsem.at[i])]
        else:
            to = F["P" if name == "P" else "Q1"]
            moves = [pltpu.make_async_copy(full, to.at[mp], lsem.at[i])]
            moves.append(pltpu.make_async_copy(b["X" + name], to.at[1 - mp], lsem.at[i + 1]))

        def go():
            for m in moves:
                m.start() if start else m.wait()

        if name[0] == "Q" and name != "Q0":
            pl.when(mp == ("QA", "QB").index(name))(go)
        else:
            go()

    def exchange_small(k):
        if not fused:
            return
        legs = [(b["s_mp"], dev_mp, 0), (b["s_x"], dev_x, 1), (b["s_y"], dev_y, 2)]
        if k > 0 and k <= 3:
            buf, dev, s = legs[k - 1]
            remote(small, buf, ssend.at[s], srecv.at[s], dev).wait()
            small[...] = small[...] + buf[...]
        if k < 3:
            buf, dev, s = legs[k]
            remote(small, buf, ssend.at[s], srecv.at[s], dev).start()
        zcs = [remote(small, b["s_z"].at[zc], ssend.at[3 + j], srecv.at[3 + j], dev_z[j]) for j in range(3)]
        if k == 3:
            b["s_z"][zc] = small[...]
            for z in zcs:
                z.start()
        if k == 4:
            for z in zcs:
                z.wait()
            small[...] = (b["s_z"][0] + b["s_z"][1]) + (b["s_z"][2] + b["s_z"][3])

    causal = jnp.where(lanes((half, half)) <= lax.broadcasted_iota(jnp.int32, (half, half), 0), 0.0, NEG)
    def attend(w, p):
        R = rows_of(w, win)
        Q, K, V = (joined[R, columns_of(width * i + p * 128, 128)] for i in range(3))
        ak = augk[R, :]
        ones = jnp.ones((win, 128), BF)
        zero = jnp.zeros((win, 128), BF)
        aq = jnp.where(l64 < 8, (ones - ak) * BF(NEG), zero)
        qs, ks, vs = [], [], []
        for h in range(2):
            mine = lo if h == 0 else ~lo
            qs.append(jnp.where(mine, Q, aq))
            ks.append(jnp.where(mine, K, ak))
            vs.append(jnp.concatenate([jnp.where(mine, V, zero), jnp.where(mine, ones, zero)], axis=1))
        for qb in range(2):
            kl = half * (qb + 1)
            es, ms = [], []
            for h in range(2):
                s = dot(qs[h][qb * half : (qb + 1) * half], ks[h][:kl], 1, 1)
                if qb == 0:
                    s = s + causal
                else:
                    s = jnp.concatenate([s[:, :half], s[:, half:] + causal], axis=1)
                m = jnp.max(s, axis=1, keepdims=True)
                es.append(jnp.exp(s - m).astype(BF))
                ms.append(m)
            ov = dot(jnp.concatenate(es, axis=1), jnp.concatenate([v[:kl] for v in vs], axis=0))
            total = ov[:, 128:]
            rr = pl.ds(pl.multiple_of(w * win + qb * half, half), half)
            mix[rr, columns_of(p * 128, 128)] = (ov[:, :128] / total).astype(BF)
            low = lo[:half]
            lse = jnp.where(low, ms[0], ms[1]) + jnp.log(total)
            x = -pltpu.roll(lse, HD, 1)
            hi = x.astype(BF)
            x = x - hi.astype(F32)
            mid = x.astype(BF)
            last = (x - mid.astype(F32)).astype(BF)
            l6 = l64[:half]
            a = aq[qb * half : (qb + 1) * half]
            a = jnp.where(l6 == 8, hi, a)
            a = jnp.where(l6 == 9, mid, a)
            augq[rr, columns_of(p * 128, 128)] = jnp.where(l6 == 10, last, a)

    copies["tok"].wait()
    copies["pos"].wait()

    def place(w, _):
        R = rows_of(w, win)
        pb[R, :] = (tok[R, :].astype(F32) + pos[...].astype(F32)).astype(BF)
        return 0

    lax.fori_loop(0, windows, place, 0)
    for part in range(2 if fused else 1):
        if part:
            for c in wremote[:3]:
                c.wait()
        span = width // 2 if fused else width
        start = (mp if part == 0 else 1 - mp) * span if fused else 0

        def project(w, _):
            R = rows_of(w, win)
            for i in range(3):
                cs = columns_of(width * i + start, span)
                joined[R, cs] = dot(pb[R, :], wq[:, cs]).astype(BF)
            return 0

        lax.fori_loop(0, windows, project, 0)

    def attend_window(w, _):
        for p in range(pairs):
            attend(w, p)
        return 0

    lax.fori_loop(0, windows, attend_window, 0)

    for i in range(3):
        copies["w%d" % i].wait()
    for c in wremote[3:]:
        c.wait()
    copies["cot"].wait()

    def feed(w, _):
        R = rows_of(w, win)
        r1 = (tok[R, :].astype(F32) + pos[...].astype(F32)) + dot(mix[R, :], wo[...])
        center = r1 - row_mean(r1)
        rstd = lax.rsqrt(row_mean(center * center) + EPSILON)
        unit = center * rstd
        u1[R, :] = unit.astype(BF)
        rs1[...] = jnp.where(lanes((win, 128)) == w, rstd, rs1[...])
        normed = unit * g1[...] + b1[...]
        nf[...] = normed
        nb[R, :] = normed.astype(BF)

        r2 = nf[...]
        for c in range(hidden // 512):
            cs = pl.ds(c * 512, 512)
            v = dot(nb[R, :], wu[:, cs]).astype(BF)
            v2 = v * v
            t = jnp.tanh(v * (BF(GELU_A) + BF(GELU_A * GELU_B) * v2))
            h = BF(0.5) + BF(0.5) * t
            active = v * h
            act[R, cs] = active
            gp[R, cs] = h + h * ((BF(1) - h) * (v * (BF(2 * GELU_A) + BF(6 * GELU_A * GELU_B) * v2)))
            r2 = r2 + dot(active, wd[cs, :])
        center = r2 - row_mean(r2)
        rstd = lax.rsqrt(row_mean(center * center) + EPSILON)
        unit = center * rstd
        tok[R, :] = (unit * g2[...] + b2[...]).astype(BF)
        up = cot[R, :].astype(F32)
        small[0:1, :] += jnp.sum(up * unit, axis=0, keepdims=True)
        small[1:2, :] += jnp.sum(up, axis=0, keepdims=True)
        e = up * g2[...]
        cot[R, :] = (rstd * (e - row_mean(e) - unit * row_mean(e * unit))).astype(BF)
        return 0

    lax.fori_loop(0, windows, feed, 0)
    out_copy = pltpu.make_async_copy(tok, out_h, out_sem.at[0])
    out_copy.start()

    def hooked(phase, body, count, first=0):
        def one(t, _):
            body(t, 0)
            for at in range(count):
                steps = SCHEDULE.get((phase, first + at))
                if steps:
                    pl.when(t == at)(functools.partial(run_steps, steps))
            return 0

        lax.fori_loop(0, count, one, 0)

    def run_steps(steps):
        for name, k in steps:
            if name == "sm":
                exchange_small(k)
            else:
                exchange(name, k)

    halves = hidden // 1024

    def down_tile(part, m, _):
        tile = m * halves + part
        d = dot(act[:, columns_of(tile * 512, 512)], cot[...], 0, 0).astype(BF).reshape(16, 32, 512)
        G["D%d" % part][m] = d
        return 0

    for part in range(2):
        hooked("down", functools.partial(down_tile, part), 2, 2 * part)

    def slope(w, _):
        R = rows_of(w, win)
        for c in range(hidden // 512):
            cs = pl.ds(c * 512, 512)
            d = dot(cot[R, :], wd[pl.ds(c * 512, 512), :], 1, 1)
            gp[R, cs] = (d * gp[R, cs].astype(F32)).astype(BF)
        return 0

    hooked("slope", slope, windows)

    def up_tile(part, m, _):
        tile = m * halves + part
        d = dot(nb[...], gp[:, columns_of(tile * 512, 512)], 0, 0).astype(BF).reshape(16, 32, 512)
        G["U%d" % part][m] = d
        return 0

    for part in range(2):
        hooked("up", functools.partial(up_tile, part), 2, 2 * part)

    def norm_back(w, _):
        R = rows_of(w, win)
        ng = cot[R, :].astype(F32) + dot(gp[R, :], wu[...], 1, 1)
        unit = u1[R, :].astype(F32)
        small[2:3, :] += jnp.sum(ng * unit, axis=0, keepdims=True)
        small[3:4, :] += jnp.sum(ng, axis=0, keepdims=True)
        e = ng * g1[...]
        rstd = jnp.sum(jnp.where(lanes((win, 128)) == w, rs1[...], 0.0), axis=1, keepdims=True)
        rg = (rstd * (e - row_mean(e) - unit * row_mean(e * unit))).astype(BF)
        cot[R, :] = rg
        u1[R, :] = dot(rg, wo[...], 1, 1).astype(BF)
        return 0

    hooked("nb", norm_back, windows)

    G["O"][...] = dot(mix[...], cot[...], 0, 0).astype(BF).reshape(2, 16, half // 16, 512)
    run_steps(SCHEDULE.get(("O", 0), ()))

    flip = (lax.broadcasted_iota(jnp.int32, (256, 128), 0) % 128 < HD) != (lanes((256, 128)) < HD)
    swap = jnp.where(flip, 1.0, 0.0).astype(BF)

    def attend_back(w, p):
        R = rows_of(w, win)
        pc = columns_of(p * 128, 128)
        Q, K, V = (joined[R, columns_of(width * i + p * 128, 128)] for i in range(3))
        D = u1[R, pc]
        prod = D.astype(F32) * mix[R, pc].astype(F32)
        ph = prod.astype(BF)
        pr = (prod - ph.astype(F32)).astype(BF)
        x = -dot(jnp.concatenate([ph, pr], axis=1), swap)
        hi = x.astype(BF)
        mid = (x - hi.astype(F32)).astype(BF)
        zero = jnp.zeros((win, 128), BF)
        ad = jnp.where(l64 == 8, hi, jnp.where(l64 == 9, mid, zero))
        av = jnp.where((l64 == 8) | (l64 == 9), jnp.ones((win, 128), BF), zero)
        aq, ak = augq[R, pc], augk[R, :]
        QT, DT = Q.T, D.T
        probs, grads = [[], []], [[], []]
        for h in range(2):
            mine = lo if h == 0 else ~lo
            qa, ka, va, da = (jnp.where(mine, i, j) for i, j in ((Q, aq), (K, ak), (V, av), (D, ad)))
            for qb in range(2):
                kl = half * (qb + 1)
                qs = slice(qb * half, kl)
                s = dot(qa[qs], ka[:kl], 1, 1)
                s = s + causal if qb == 0 else jnp.concatenate([s[:, :half], s[:, half:] + causal], axis=1)
                e = jnp.exp(s)
                grads[h].append((e * dot(da[qs], va[:kl], 1, 1)).astype(BF))
                probs[h].append(e.astype(BF))
        dq, dk, dv = [None, None], [], []
        for h in range(2):
            km = jnp.where(lo if h == 0 else ~lo, K, zero)
            hs = slice(h * HD, (h + 1) * HD)
            for qb in range(2):
                x = dot(grads[h][qb], km[: half * (qb + 1)])
                dq[qb] = x if h == 0 else dq[qb] + x
            for left, (first, second), to in ((QT, grads[h], dk), (DT, probs[h], dv)):
                early = dot(left[hs], jnp.concatenate([first, second[:, :half]], axis=0))
                to.append(jnp.concatenate([early, dot(left[hs, half:], second[:, half:])], axis=1))
        for i in range(2):
            joined[pl.ds(pl.multiple_of(w * win + i * half, half), half), pc] = dq[i].astype(BF)
        for i, v in enumerate((dk, dv)):
            joined[R, columns_of(width * (i + 1) + p * 128, 128)] = jnp.concatenate(v, axis=0).astype(BF).T

    def qkv_grad(*some):
        def one(m, _):
            total = None
            for w in range(windows):
                R = pl.ds(w * win, win)
                right = jnp.concatenate(
                    [joined[R, pl.ds(width * i + p * 128, 128)] for p in some for i in range(3)], axis=1
                )
                d = dot(pb[R, columns_of(m * half, half)], right, 0, 0)
                total = d if total is None else total + d
            total = total.astype(BF)
            if len(some) == 2:
                for j in range(2):
                    G["Q0"][j, pl.ds(8 * m, 8)] = total[:, 384 * j : 384 * (j + 1)].reshape(8, 32, 384)
            else:
                G["QA" if some[0] == 1 else "QB"][m] = total.reshape(16, 16, 384)
            return 0

        lax.fori_loop(0, 2, one, 0)

    def add_position(p):
        cols = [pl.ds(width * i + p * 128, 128) for i in range(3)]
        total = []
        for c in cols:
            v = joined[pl.ds(0, win), c].astype(F32)
            for w in range(1, windows):
                v = v + joined[pl.ds(w * win, win), c].astype(F32)
            total.append(v.astype(BF))
        part = dot(jnp.concatenate(total, axis=1), jnp.concatenate([wq[:, c] for c in cols], axis=1), 1, 1)
        nf[...] = nf[...] + part

    def steps_at(phase, at):
        run_steps(SCHEDULE.get((phase, at), ()))

    total = cot[pl.ds(0, win), :].astype(F32)
    for w in range(1, windows):
        total = total + cot[pl.ds(w * win, win), :].astype(F32)
    nf[...] = total
    order = (0, 2, 1, 3)
    for i, p in enumerate(order):
        hooked("back%d" % i, lambda t, _: attend_back(t, p), windows)
        if i == 3:
            add_position(p)
            G["P"][...] = nf[...].astype(BF).reshape(2, 16, half // 16, 512)
            steps_at("P", 0)
        if i > 0:
            qkv_grad(*((0, 2) if i == 1 else (p,)))
        steps_at("q%d" % i, 0)
        if i < 3:
            add_position(p)
            steps_at("add%d" % i, 0)

    def finish(w, _):
        R = rows_of(w, win)
        cot[R, :] = (cot[R, :].astype(F32) + dot(joined[R, :], wq[...], 1, 1)).astype(BF)
        return 0

    hooked("fin", finish, windows)
    ig_copy = pltpu.make_async_copy(cot, ig_h, out_sem.at[1])
    ig_copy.start()
    small_copy = pltpu.make_async_copy(small, small_h, out_sem.at[2])
    small_copy.start()
    run_steps(TAIL)
    if fused:
        for name in NAMES:
            results_out(name, False)
    if not fused:
        outs = [pltpu.make_async_copy(G[nm], F[nm], in_sem.at[i]) for i, nm in enumerate(NAMES)]
        for c in outs:
            c.start()
        for c in outs:
            c.wait()
    out_copy.wait()
    ig_copy.wait()
    small_copy.wait()


def scratch_of(fused, dims):
    win, width, hidden, windows = dims
    rows = win * windows
    V, dma = pltpu.VMEM, pltpu.SemaphoreType.DMA
    b = {k: V((rows, width), BF) for k in ("tok", "cot", "mix", "u1", "pb", "nb", "augq")}
    b.update({k: V((rows, hidden), BF) for k in ("act", "gp")})
    b.update(
        pos=V((win, width), BF),
        augk=V((rows, 128), BF),
        wq=V((width, 3 * width), BF),
        wo=V((width, width), BF),
        wu=V((width, hidden), BF),
        wd=V((hidden, width), BF),
        joined=V((rows, 3 * width), BF),
        rs1=V((win, 128), F32),
        nf=V((win, width), F32),
        small=V((8, width), F32),
        in_sem=dma((12,)),
        out_sem=dma((3,)),
    )
    b.update({"G" + k: V((2, PIECES) + CHUNKS[k], BF) for k in NAMES})
    if fused:
        for k in NAMES:
            lead = {"M": (16,), "A": (8,), "B": (4,), "Z": (3,)}
            if k in DIRECT:
                lead = {"M": (16,), "A": (3, 4), "Z": (3,), "X": (16,)}
            b.update({buf + k: V(n + CHUNKS[k], BF) for buf, n in lead.items()})
        b.update({k: V((8, width), F32) for k in ("s_mp", "s_x", "s_y")})
        b.update(
            s_z=V((4, 8, width), F32),
            wsem=dma((2, 6)),
            csend=dma((len(NAMES), 15)),
            crecv=dma((len(NAMES), 15)),
            ssend=dma((6,)),
            srecv=dma((6,)),
            lsem=dma((2 * len(NAMES),)),
        )
    return b


def layer(fused, tok, cot, pos, seg, wq, wo, wu, wd, g1, b1, g2, b2, hidden):
    rows, width = tok.shape
    win = pos.shape[0]
    windows = rows // win
    hbm = pl.BlockSpec(memory_space=pl.ANY)
    vmem = pl.BlockSpec(memory_space=pltpu.VMEM)
    shape = jax.ShapeDtypeStruct
    full = {k: (PIECES,) + v if fused and k not in DIRECT else (2, PIECES) + v for k, v in CHUNKS.items()}
    full["Q1"] = full["QA"]
    outs = [shape((rows, width), BF), shape((rows, width), BF), shape((8, width), F32)]
    outs += [shape(full[k], BF) for k in (RESULTS if fused else NAMES)]
    scratch = list(scratch_of(fused, (win, width, hidden, windows)).values())
    params = dict(vmem_limit_bytes=64 << 20)
    if fused:
        params.update(collective_id=0, has_side_effects=True)
    return pl.pallas_call(
        functools.partial(kernel, fused, (win, width, hidden, windows)),
        out_shape=outs,
        in_specs=[hbm] * 3 + [vmem] + [hbm] * 4 + [vmem] * 4,
        out_specs=[hbm] * len(outs),
        scratch_shapes=scratch,
        compiler_params=pltpu.CompilerParams(**params),
        name="layer",
    )(tok, cot, pos, seg, wq, wo, wu, wd, g1, b1, g2, b2)


def widen(got, wide):
    rows = got.shape[-2]

    def one(i, _):
        piece = got[i] if len(got.shape) == 3 else got[i // PIECES, lax.rem(i, PIECES)]
        wide[pl.ds(pl.multiple_of(i * rows, rows), rows), :] = piece.astype(F32)
        return 0

    lax.fori_loop(0, wide.shape[0] // rows, one, 0)


def finish_kernel(*refs):
    (out_h, ig_h, small), grads = refs[:3], dict(zip(RESULTS, refs[3 : 3 + len(RESULTS)]))
    refs = refs[3 + len(RESULTS) :]
    out_o, ig_o, pos_o, qkv_o, wo_o, up_o, down_o = refs[:7]
    norms = refs[7:11]
    refs = refs[11:]
    got = dict(zip(RESULTS, refs[: len(RESULTS)]))
    wide = dict(zip(RESULTS, refs[len(RESULTS) : 2 * len(RESULTS)]))
    held, in_sem, out_sem = refs[2 * len(RESULTS) :]
    last, loads, passed = [], [], []
    for i, (src, dst) in enumerate(((out_h, out_o), (ig_h, ig_o))):
        passed.append(pltpu.make_async_copy(src, held.at[i], in_sem.at[len(RESULTS) + i]))
        last.append(pltpu.make_async_copy(held.at[i], dst, out_sem.at[len(RESULTS) + i]))
    for c in passed:
        c.start()
    for i, k in enumerate(RESULTS):
        loads.append(pltpu.make_async_copy(grads[k], got[k], in_sem.at[i]))
        loads[-1].start()
    rows = down_o.shape[0] // 2
    places = {
        "D0": down_o.at[pl.ds(0, rows)],
        "D1": down_o.at[pl.ds(rows, rows)],
        "U0": up_o.at[:, pl.ds(0, 512)],
        "U1": up_o.at[:, pl.ds(512, 512)],
        "O": wo_o,
        "Q0": qkv_o.at[:, pl.ds(0, 384)],
        "Q1": qkv_o.at[:, pl.ds(384, 384)],
        "P": pos_o,
    }
    for i in range(2):
        passed[i].wait()
        last[i].start()
    for i, k in enumerate(RESULTS):
        loads[i].wait()
        widen(got[k], wide[k])
        last.append(pltpu.make_async_copy(wide[k], places[k], out_sem.at[i]))
        last[-1].start()
    for ref, row in zip(norms, (2, 3, 0, 1)):
        ref[...] = small[row]
    for c in last:
        c.wait()


def finish(out, ig, small, grads, win, width, hidden):
    hbm = pl.BlockSpec(memory_space=pl.ANY)
    vmem = pl.BlockSpec(memory_space=pltpu.VMEM)
    shape = jax.ShapeDtypeStruct
    outs = [shape(out.shape, BF), shape(ig.shape, BF), shape((win, width), F32)]
    outs += [shape((width, 3 * width // 2), F32), shape((width // 2, width), F32)]
    outs += [shape((width, hidden // 2), F32), shape((hidden // 2, width), F32)]
    outs += [shape((width,), F32)] * 4
    dma = pltpu.SemaphoreType.DMA
    scratch = [pltpu.VMEM(g.shape, BF) for g in grads]
    scratch += [pltpu.VMEM((g.size // g.shape[-1], g.shape[-1]), F32) for g in grads]
    scratch += [pltpu.VMEM((2,) + out.shape, BF), dma((len(RESULTS) + 2,)), dma((len(RESULTS) + 2,))]
    return pl.pallas_call(
        finish_kernel,
        out_shape=outs,
        in_specs=[hbm, hbm, vmem] + [hbm] * len(RESULTS),
        out_specs=[hbm] * 7 + [vmem] * 4,
        scratch_shapes=scratch,
        compiler_params=pltpu.CompilerParams(vmem_limit_bytes=64 << 20),
        name="finish",
    )(out, ig, small, *grads)


def local(shards, tokens, segment_ids, cotangent, pos_table, w_qkv, w_out, w_up, w_down, g1, b1, g2, b2):
    dp_size, mp_size = shards
    width = tokens.shape[1]
    win = pos_table.shape[0]
    hidden = w_up.shape[1] * mp_size
    fused = dp_size == PIECES
    gains = [v.reshape(1, width) for v in (g1, b1, g2, b2)]
    if fused:
        out, ig, small, *grads = layer(
            True, tokens, cotangent, pos_table, segment_ids, w_qkv, w_out, w_up, w_down, *gains, hidden
        )
        return tuple(finish(out, ig, small, grads, win, width, hidden))
    windows = tokens.shape[0] // win
    seg = jnp.roll(segment_ids, -lax.axis_index("mp") * windows, axis=0)
    wq = lax.all_gather(w_qkv, "mp", axis=1, tiled=True)
    wo = lax.all_gather(w_out, "mp", axis=0, tiled=True)
    wu = lax.all_gather(w_up, "mp", axis=1, tiled=True)
    wd = lax.all_gather(w_down, "mp", axis=0, tiled=True)
    out, ig, small, *grads = layer(False, tokens, cotangent, pos_table, seg, wq, wo, wu, wd, *gains, hidden)
    g = dict(zip(NAMES, (v.astype(F32) for v in grads)))
    g = {
        k: v if k in DIRECT else lax.psum(lax.psum_scatter(v, "mp", scatter_dimension=0, tiled=False), "dp")
        for k, v in g.items()
    }
    pos, QA, QB, small = lax.psum((g["P"], g["QA"], g["QB"], small), ("dp", "mp"))
    g["Q1"] = jnp.where(lax.axis_index("mp") == 0, QA, QB)
    scale = jnp.array([HD**-0.5, 1, 1], F32)[:, None, None]
    Q = [(g[k].reshape(width, 3, 2, HD) * scale).transpose(0, 2, 1, 3).reshape(width, 6 * HD) for k in ("Q0", "Q1")]
    return (
        out,
        ig,
        pos.reshape(win, width),
        jnp.concatenate(Q, axis=1),
        g["O"].reshape(-1, width),
        jnp.concatenate([g["U0"].reshape(width, -1), g["U1"].reshape(width, -1)], axis=1),
        jnp.concatenate([g["D0"].reshape(-1, width), g["D1"].reshape(-1, width)], axis=0),
        small[2],
        small[3],
        small[0],
        small[1],
    )


def solution(mesh):
    cut, copied = P(("dp", "mp"), None), P()
    columns, split_rows = P(None, "mp"), P("mp", None)
    weights = (columns, split_rows, columns, split_rows)
    return jax.shard_map(
        functools.partial(local, (mesh.shape["dp"], mesh.shape["mp"])),
        mesh=mesh,
        in_specs=(cut, P("dp", None), cut, copied) + weights + (copied,) * 4,
        out_specs=(cut, cut, copied) + weights + (copied,) * 4,
        check_vma=False,
    )
```

```python
import functools

import jax
import jax.numpy as jnp
from jax import lax
from jax.experimental import pallas as pl
from jax.experimental.pallas import tpu as pltpu
from jax.sharding import PartitionSpec as P

BF = jnp.bfloat16
F32 = jnp.float32
MESH = pl.DeviceIdType.MESH
HD = 64
EPSILON = 1e-05
NEG = -1e30
GELU_A = 0.7978845608028654
GELU_B = 0.044715

CHUNKS = {
    "D0": (32, 512),
    "D1": (32, 512),
    "U0": (32, 512),
    "U1": (32, 512),
    "O": (16, 512),
    "Q0": (32, 384),
    "QA": (16, 384),
    "QB": (16, 384),
    "P": (16, 512),
}
NAMES = tuple(CHUNKS)
DIRECT = ("QA", "QB", "P")
RESULTS = ("D0", "D1", "U0", "U1", "O", "Q0", "Q1", "P")
PIECES = 16
UNROLLED = ("nb", )

SCHEDULE = {
    ("down", 1): (("D0", 0),),
    ("down", 3): (("D1", 0),),
    ("slope", 0): (("D0", 1),),
    ("slope", 1): (("D1", 1),),
    ("up", 1): (("D0", 2), ("U0", 0),),
    ("up", 3): (("D1", 2), ("U0", 1), ("U1", 0),),
    ("nb", 0): (("D0", 3),),
    ("nb", 1): (("U1", 1),),
    ("nb", 2): (("D1", 3),),
    ("nb", 3): (("D0", 4), ("U0", 2),),
    ("O", 0): (("O", 0), ("sm", 0),),
    ("back0", 1): (("D1", 4), ("U1", 2), ("O", 1), ("sm", 1),),
    ("back0", 2): (("U0", 3),),
    ("back0", 3): (("D0", 5),),
    ("back1", 0): (("sm", 2),),
    ("back1", 1): (("D1", 5), ("U1", 3),),
    ("back1", 2): (("O", 2),),
    ("back1", 3): (("D0", 6), ("U0", 4), ("sm", 3),),
    ("q1", 0): (("D1", 6), ("U1", 4), ("Q0", 0),),
    ("add1", 0): (("O", 3),),
    ("back2", 0): (("sm", 4),),
    ("back2", 1): (("U0", 5), ("Q0", 1),),
    ("back2", 2): (("D0", 7),),
    ("back2", 3): (("U1", 5),),
    ("q2", 0): (("D1", 7), ("O", 4), ("QA", 0),),
    ("add2", 0): (("U0", 6),),
    ("back3", 1): (("Q0", 2), ("QA", 1),),
    ("back3", 2): (("U1", 6), ("O", 5),),
    ("P", 0): (("P", 0),),
    ("q3", 0): (("U0", 7), ("Q0", 3), ("QB", 0),),
    ("fin", 0): (("QA", 2), ("P", 1),),
    ("fin", 1): (("QB", 1),),
    ("fin", 3): (("U1", 7), ("Q0", 4),),
}
TAIL = (
    ("O", 6),
    ("QA", 3),
    ("P", 2),
    ("Q0", 5),
    ("QB", 2),
    ("QA", 4),
    ("O", 7),
    ("P", 3),
    ("QB", 3),
    ("Q0", 6),
    ("P", 4),
    ("QA", 5),
    ("QB", 4),
    ("QA", 6),
    ("Q0", 7),
    ("P", 5),
    ("P", 6),
    ("QB", 5),
    ("QB", 6),
)


def dot(left, right, left_dim=1, right_dim=0):
    return lax.dot_general(
        left, right, (((left_dim,), (right_dim,)), ((), ())), preferred_element_type=F32
    )


def lanes(shape):
    return lax.broadcasted_iota(jnp.int32, shape, len(shape) - 1)


def rows_of(w, win):
    return pl.ds(pl.multiple_of(w * win, win), win)


def columns_of(start, size):
    return pl.ds(pl.multiple_of(start, 128), size)


def row_mean(v):
    return jnp.mean(v, axis=-1, keepdims=True)


def kernel(fused, dims, *refs):
    win, width, hidden, windows = dims
    half_hidden = hidden // 2
    half = win // 2
    (tok_h, cot_h, pos_h, seg, wq_h, wo_h, wu_h, wd_h, g1, b1, g2, b2) = refs[:12]
    refs = refs[12:]
    out_h, ig_h, small_h = refs[:3]
    results = RESULTS if fused else NAMES
    F = dict(zip(results, refs[3 : 3 + len(results)]))
    b = dict(zip(scratch_of(fused, dims), refs[3 + len(results) :]))
    tok, cot, pos, augk = b["tok"], b["cot"], b["pos"], b["augk"]
    wq, wo, wu, wd = b["wq"], b["wo"], b["wu"], b["wd"]
    joined, mix, u1, rs1, pb, nb = b["joined"], b["mix"], b["u1"], b["rs1"], b["pb"], b["nb"]
    act, gp, augq, nf, small = b["act"], b["gp"], b["augq"], b["nf"], b["small"]
    G, R_mp, R_a, R_b, R_z = ({k: b.get(buf + k) for k in NAMES} for buf in ("G", "M", "A", "B", "Z"))
    in_sem, out_sem = b["in_sem"], b["out_sem"]

    pairs = width // 128

    copies = {}

    def fetch(name, src, dst, k):
        copies[name] = pltpu.make_async_copy(src, dst, in_sem.at[k])
        copies[name].start()

    if fused:
        wsem, csend, crecv, ssend, srecv, lsem = (
            b[k] for k in ("wsem", "csend", "crecv", "ssend", "srecv", "lsem")
        )
        dp = lax.axis_index("dp")
        mp = lax.axis_index("mp")
        zc = dp // 4
        yc = lax.rem(dp // 2, 2)
        xc = lax.rem(dp, 2)
        ac = jnp.where(mp == 0, xc, yc)
        bc = jnp.where(mp == 0, yc, xc)
        step_a = jnp.where(mp == 0, 1, 2)
        step_b = jnp.where(mp == 0, 2, 1)
        dev_mp = (dp, 1 - mp)
        dev_a = (dp + step_a * (1 - 2 * ac), mp)
        dev_b = (dp + step_b * (1 - 2 * bc), mp)
        dev_d = (dp + step_a * (1 - 2 * ac) + step_b * (1 - 2 * bc), mp)
        dev_x = (dp + 1 - 2 * xc, mp)
        dev_y = (dp + 2 * (1 - 2 * yc), mp)
        zs = [lax.rem(zc + k, 4) for k in (1, 2, 3)]
        dev_z = [(lax.rem(dp, 4) + 4 * z, mp) for z in zs]
        barrier = pltpu.get_barrier_semaphore()
        for dev in [dev_mp, dev_a, dev_b, dev_d] + dev_z:
            pl.semaphore_signal(barrier, inc=1, device_id=dev, device_id_type=MESH)

    raw_width = wq_h.shape[1]
    raw = act.at[pl.ds(0, width), pl.ds(0, raw_width)]
    fetch("wq", wq_h, raw, 2)
    fetch("tok", tok_h, tok, 0)
    fetch("pos", pos_h, pos, 1)
    wparts = []
    if fused:
        wparts.append((wo_h, wo.at[pl.ds(pl.multiple_of(mp * half, half), half), :]))
        wparts.append((wu_h, wu.at[:, columns_of(half_hidden * mp, half_hidden)]))
        wparts.append((wd_h, wd.at[pl.ds(pl.multiple_of(mp * half_hidden, half_hidden), half_hidden), :]))
    else:
        wparts += [(wo_h, wo), (wu_h, wu), (wd_h, wd)]
    for i, (src, dst) in enumerate(wparts):
        fetch("w%d" % i, src, dst, 5 + i)
    fetch("cot", cot_h, cot, 4)
    small[...] = jnp.zeros_like(small)
    rs1[...] = jnp.zeros_like(rs1)

    l64 = lax.rem(lanes((win, 128)), HD)
    lo = lanes((win, 128)) < HD

    columns = seg[...].astype(F32).T
    mine = (mp if fused else 0) * windows
    for w in range(windows):
        R = pl.ds(w * win, win)
        column = jnp.sum(
            jnp.where(lanes(columns.shape) == mine + w, columns, 0.0), axis=1, keepdims=True
        ).astype(jnp.int32)
        augk[R, :] = jnp.where((l64 == column) | ((l64 >= 8) & (l64 < 11)), 1.0, 0.0).astype(BF)

    copies["wq"].wait()
    own_columns = mp * raw_width // 3 if fused else 0
    for p in range(raw_width // 384):
        cut = [raw[:, pl.ds(p * 384 + 128 * i, 128)] for i in range(3)]
        low = lanes((width, 128)) < HD
        swapped = [pltpu.roll(c.astype(F32), HD, 1).astype(BF) for c in cut]
        q = jnp.where(low, cut[0], cut[1]) * BF(HD**-0.5)
        k = jnp.where(low, swapped[0], swapped[2])
        v = jnp.where(low, cut[1], cut[2])
        for i, part in enumerate((q, k, v)):
            wq[:, columns_of(own_columns + width * i + 128 * p, 128)] = part

    wremote = []
    if fused:
        pl.semaphore_wait(barrier, 7)
        slices = [wq.at[:, columns_of(own_columns + width * i, raw_width // 3)] for i in range(3)]
        for i, (src, dst) in enumerate([(x, x) for x in slices] + wparts):
            c = pltpu.make_async_remote_copy(
                src_ref=src, dst_ref=dst, send_sem=wsem.at[0, i], recv_sem=wsem.at[1, i],
                device_id=dev_mp, device_id_type=MESH,
            )
            c.start()
            wremote.append(c)

    def remote(src, dst, send, recv, dev):
        return pltpu.make_async_remote_copy(
            src_ref=src, dst_ref=dst, send_sem=send, recv_sem=recv, device_id=dev, device_id_type=MESH
        )

    def add(mine, got):
        mine[...] = mine[...] + got[...]

    def exchange(name, k):
        if not fused:
            return
        c = NAMES.index(name)
        g = G[name]
        direct = name in DIRECT
        own = g.at[mp]
        base = ac * 8 + bc * 4
        full = g.at[1 - mp]

        def send(src, dst, i, dev):
            return remote(src, dst, csend.at[c, i], crecv.at[c, i], dev)

        def to_z(src, dst_of):
            return [send(src(j), dst_of(j), 3 + j, dev_z[j]) for j in range(3)]

        if direct:
            slots = R_a[name]
            places = [(1 - ac) * 8 + bc * 4, ac * 8 + (1 - bc) * 4, (1 - ac) * 8 + (1 - bc) * 4]
            plane = [dev_a, dev_b, dev_d]
            stages = [
                lambda: [send(full, R_mp[name], 0, dev_mp)],
                lambda: [send(own.at[pl.ds(places[j], 4)], slots.at[j], 6 + j, plane[j]) for j in range(3)],
                lambda: [send(own.at[base + zs[j]], R_z[name].at[j], 3 + j, dev_z[j]) for j in range(3)],
                lambda: [send(full.at[base + zc], full.at[base + zc], 9 + j, dev_z[j]) for j in range(3)],
                lambda: [send(full.at[pl.ds(base, 4)], full.at[pl.ds(base, 4)], 12 + j, plane[j]) for j in range(3)],
                lambda: [send(full, b["X" + name], 1, dev_mp)],
            ]
        else:
            stages = [
                lambda: [send(full, R_mp[name], 0, dev_mp)],
                lambda: [send(own.at[pl.ds((1 - ac) * 8, 8)], R_a[name], 1, dev_a)],
                lambda: [send(own.at[pl.ds(ac * 8 + (1 - bc) * 4, 4)], R_b[name], 2, dev_b)],
                lambda: [send(own.at[base + zs[j]], R_z[name].at[j], 3 + j, dev_z[j]) for j in range(3)],
                lambda: [send(full.at[base + zc], full.at[base + zc], 6 + j, dev_z[j]) for j in range(3)],
                lambda: [send(full.at[pl.ds(base, 4)], full.at[pl.ds(base, 4)], 9, dev_b)],
                lambda: [send(full.at[pl.ds(ac * 8, 8)], full.at[pl.ds(ac * 8, 8)], 10, dev_a)],
            ]
        if 0 < k <= len(stages):
            for copy in stages[k - 1]():
                copy.wait()
        if k == 1:
            add(own, R_mp[name])
        if direct and k == 2:
            at = own.at[pl.ds(base, 4)]
            at[...] = (
                (at[...].astype(F32) + slots[0].astype(F32)) + (slots[1].astype(F32) + slots[2].astype(F32))
            ).astype(BF)
        if not direct and k == 2:
            add(own.at[pl.ds(ac * 8, 8)], R_a[name])
        if not direct and k == 3:
            add(own.at[pl.ds(base, 4)], R_b[name])
        if k == (3 if direct else 4):
            total = own[base + zc].astype(F32)
            for j in range(3):
                total = total + R_z[name][j].astype(F32)
            if name[0] == "Q":
                q, kk, v = total[:, :128] * (HD**-0.5), total[:, 128:256], total[:, 256:]
                total = jnp.concatenate(
                    [q[:, :HD], kk[:, :HD], v[:, :HD], q[:, HD:], kk[:, HD:], v[:, HD:]], axis=1
                )
            full[base + zc] = total.astype(BF)
        if k < len(stages):
            for copy in stages[k]():
                copy.start()
        if k == len(stages):
            results_out(name, True)

    def results_out(name, start):
        full, i = G[name].at[1 - mp], 2 * NAMES.index(name)
        if name not in DIRECT:
            moves = [pltpu.make_async_copy(full, F[name], lsem.at[i])]
        else:
            to = F["P" if name == "P" else "Q1"]
            moves = [pltpu.make_async_copy(full, to.at[mp], lsem.at[i])]
            moves.append(pltpu.make_async_copy(b["X" + name], to.at[1 - mp], lsem.at[i + 1]))

        def go():
            for m in moves:
                m.start() if start else m.wait()

        if name[0] == "Q" and name != "Q0":
            pl.when(mp == ("QA", "QB").index(name))(go)
        else:
            go()

    def exchange_small(k):
        if not fused:
            return
        legs = [(b["s_mp"], dev_mp, 0), (b["s_x"], dev_x, 1), (b["s_y"], dev_y, 2)]
        if k > 0 and k <= 3:
            buf, dev, s = legs[k - 1]
            remote(small, buf, ssend.at[s], srecv.at[s], dev).wait()
            small[...] = small[...] + buf[...]
        if k < 3:
            buf, dev, s = legs[k]
            remote(small, buf, ssend.at[s], srecv.at[s], dev).start()
        zcs = [remote(small, b["s_z"].at[zc], ssend.at[3 + j], srecv.at[3 + j], dev_z[j]) for j in range(3)]
        if k == 3:
            b["s_z"][zc] = small[...]
            for z in zcs:
                z.start()
        if k == 4:
            for z in zcs:
                z.wait()
            small[...] = (b["s_z"][0] + b["s_z"][1]) + (b["s_z"][2] + b["s_z"][3])

    causal = jnp.where(lanes((half, half)) <= lax.broadcasted_iota(jnp.int32, (half, half), 0), 0.0, NEG)
    def attend(w, p):
        R = rows_of(w, win)
        Q, K, V = (joined[R, columns_of(width * i + p * 128, 128)] for i in range(3))
        ak = augk[R, :]
        ones = jnp.ones((win, 128), BF)
        zero = jnp.zeros((win, 128), BF)
        aq = jnp.where(l64 < 8, (ones - ak) * BF(NEG), zero)
        qs, ks, vs = [], [], []
        for h in range(2):
            mine = lo if h == 0 else ~lo
            qs.append(jnp.where(mine, Q, aq))
            ks.append(jnp.where(mine, K, ak))
            vs.append(jnp.concatenate([jnp.where(mine, V, zero), jnp.where(mine, ones, zero)], axis=1))
        for qb in range(2):
            kl = half * (qb + 1)
            es, ms = [], []
            for h in range(2):
                s = dot(qs[h][qb * half : (qb + 1) * half], ks[h][:kl], 1, 1)
                if qb == 0:
                    s = s + causal
                else:
                    s = jnp.concatenate([s[:, :half], s[:, half:] + causal], axis=1)
                m = jnp.max(s, axis=1, keepdims=True)
                es.append(jnp.exp(s - m).astype(BF))
                ms.append(m)
            ov = dot(jnp.concatenate(es, axis=1), jnp.concatenate([v[:kl] for v in vs], axis=0))
            total = ov[:, 128:]
            rr = pl.ds(pl.multiple_of(w * win + qb * half, half), half)
            mix[rr, columns_of(p * 128, 128)] = (ov[:, :128] / total).astype(BF)
            low = lo[:half]
            lse = jnp.where(low, ms[0], ms[1]) + jnp.log(total)
            x = -pltpu.roll(lse, HD, 1)
            hi = x.astype(BF)
            x = x - hi.astype(F32)
            mid = x.astype(BF)
            last = (x - mid.astype(F32)).astype(BF)
            l6 = l64[:half]
            a = aq[qb * half : (qb + 1) * half]
            a = jnp.where(l6 == 8, hi, a)
            a = jnp.where(l6 == 9, mid, a)
            augq[rr, columns_of(p * 128, 128)] = jnp.where(l6 == 10, last, a)

    copies["tok"].wait()
    copies["pos"].wait()

    def place(w, _):
        R = rows_of(w, win)
        pb[R, :] = (tok[R, :].astype(F32) + pos[...].astype(F32)).astype(BF)
        return 0

    lax.fori_loop(0, windows, place, 0)
    for part in range(2 if fused else 1):
        if part:
            for c in wremote[:3]:
                c.wait()
        span = width // 2 if fused else width
        start = (mp if part == 0 else 1 - mp) * span if fused else 0

        def project(w, _):
            R = rows_of(w, win)
            for i in range(3):
                cs = columns_of(width * i + start, span)
                joined[R, cs] = dot(pb[R, :], wq[:, cs]).astype(BF)
            return 0

        lax.fori_loop(0, windows, project, 0)

    def attend_window(w, _):
        for p in range(pairs):
            attend(w, p)
        return 0

    lax.fori_loop(0, windows, attend_window, 0)

    for i in range(3):
        copies["w%d" % i].wait()
    for c in wremote[3:]:
        c.wait()
    copies["cot"].wait()

    def feed(w, _):
        R = rows_of(w, win)
        r1 = (tok[R, :].astype(F32) + pos[...].astype(F32)) + dot(mix[R, :], wo[...])
        center = r1 - row_mean(r1)
        rstd = lax.rsqrt(row_mean(center * center) + EPSILON)
        unit = center * rstd
        u1[R, :] = unit.astype(BF)
        rs1[...] = jnp.where(lanes((win, 128)) == w, rstd, rs1[...])
        normed = unit * g1[...] + b1[...]
        nf[...] = normed
        nb[R, :] = normed.astype(BF)

        r2 = nf[...]
        for c in range(hidden // 512):
            cs = pl.ds(c * 512, 512)
            v = dot(nb[R, :], wu[:, cs]).astype(BF)
            v2 = v * v
            t = jnp.tanh(v * (BF(GELU_A) + BF(GELU_A * GELU_B) * v2))
            h = BF(0.5) + BF(0.5) * t
            active = v * h
            act[R, cs] = active
            gp[R, cs] = h + h * ((BF(1) - h) * (v * (BF(2 * GELU_A) + BF(6 * GELU_A * GELU_B) * v2)))
            r2 = r2 + dot(active, wd[cs, :])
        center = r2 - row_mean(r2)
        rstd = lax.rsqrt(row_mean(center * center) + EPSILON)
        unit = center * rstd
        tok[R, :] = (unit * g2[...] + b2[...]).astype(BF)
        up = cot[R, :].astype(F32)
        small[0:1, :] += jnp.sum(up * unit, axis=0, keepdims=True)
        small[1:2, :] += jnp.sum(up, axis=0, keepdims=True)
        e = up * g2[...]
        cot[R, :] = (rstd * (e - row_mean(e) - unit * row_mean(e * unit))).astype(BF)
        return 0

    lax.fori_loop(0, windows, feed, 0)
    out_copy = pltpu.make_async_copy(tok, out_h, out_sem.at[0])
    out_copy.start()

    def hooked(phase, body, count, first=0):
        def one(t, _):
            body(t, 0)
            for at in range(count):
                steps = SCHEDULE.get((phase, first + at))
                if steps:
                    pl.when(t == at)(functools.partial(run_steps, steps))
            return 0

        if phase not in UNROLLED:
            lax.fori_loop(0, count, one, 0)
            return
        for t in range(count):
            body(t, 0)
            run_steps(SCHEDULE.get((phase, t), ()))

    def run_steps(steps):
        for name, k in steps:
            if name == "sm":
                exchange_small(k)
            else:
                exchange(name, k)

    halves = hidden // 1024

    def down_tile(part, m, _):
        tile = m * halves + part
        d = dot(act[:, columns_of(tile * 512, 512)], cot[...], 0, 0).astype(BF).reshape(16, 32, 512)
        G["D%d" % part][m] = d
        return 0

    for part in range(2):
        hooked("down", functools.partial(down_tile, part), 2, 2 * part)

    def slope(w, _):
        R = rows_of(w, win)
        for c in range(hidden // 512):
            cs = pl.ds(c * 512, 512)
            d = dot(cot[R, :], wd[pl.ds(c * 512, 512), :], 1, 1)
            gp[R, cs] = (d * gp[R, cs].astype(F32)).astype(BF)
        return 0

    hooked("slope", slope, windows)

    def up_tile(part, m, _):
        tile = m * halves + part
        d = dot(nb[...], gp[:, columns_of(tile * 512, 512)], 0, 0).astype(BF).reshape(16, 32, 512)
        G["U%d" % part][m] = d
        return 0

    for part in range(2):
        hooked("up", functools.partial(up_tile, part), 2, 2 * part)

    def norm_back(w, _):
        R = rows_of(w, win)
        ng = cot[R, :].astype(F32) + dot(gp[R, :], wu[...], 1, 1)
        unit = u1[R, :].astype(F32)
        small[2:3, :] += jnp.sum(ng * unit, axis=0, keepdims=True)
        small[3:4, :] += jnp.sum(ng, axis=0, keepdims=True)
        e = ng * g1[...]
        rstd = jnp.sum(jnp.where(lanes((win, 128)) == w, rs1[...], 0.0), axis=1, keepdims=True)
        rg = (rstd * (e - row_mean(e) - unit * row_mean(e * unit))).astype(BF)
        cot[R, :] = rg
        u1[R, :] = dot(rg, wo[...], 1, 1).astype(BF)
        return 0

    hooked("nb", norm_back, windows)

    G["O"][...] = dot(mix[...], cot[...], 0, 0).astype(BF).reshape(2, 16, half // 16, 512)
    run_steps(SCHEDULE.get(("O", 0), ()))

    flip = (lax.broadcasted_iota(jnp.int32, (256, 128), 0) % 128 < HD) != (lanes((256, 128)) < HD)
    swap = jnp.where(flip, 1.0, 0.0).astype(BF)

    def attend_back(w, p):
        R = rows_of(w, win)
        pc = columns_of(p * 128, 128)
        Q, K, V = (joined[R, columns_of(width * i + p * 128, 128)] for i in range(3))
        D = u1[R, pc]
        prod = D.astype(F32) * mix[R, pc].astype(F32)
        ph = prod.astype(BF)
        pr = (prod - ph.astype(F32)).astype(BF)
        x = -dot(jnp.concatenate([ph, pr], axis=1), swap)
        hi = x.astype(BF)
        mid = (x - hi.astype(F32)).astype(BF)
        zero = jnp.zeros((win, 128), BF)
        ad = jnp.where(l64 == 8, hi, jnp.where(l64 == 9, mid, zero))
        av = jnp.where((l64 == 8) | (l64 == 9), jnp.ones((win, 128), BF), zero)
        aq, ak = augq[R, pc], augk[R, :]
        QT, DT = Q.T, D.T
        probs, grads = [[], []], [[], []]
        for h in range(2):
            mine = lo if h == 0 else ~lo
            qa, ka, va, da = (jnp.where(mine, i, j) for i, j in ((Q, aq), (K, ak), (V, av), (D, ad)))
            for qb in range(2):
                kl = half * (qb + 1)
                qs = slice(qb * half, kl)
                s = dot(qa[qs], ka[:kl], 1, 1)
                s = s + causal if qb == 0 else jnp.concatenate([s[:, :half], s[:, half:] + causal], axis=1)
                e = jnp.exp(s)
                grads[h].append((e * dot(da[qs], va[:kl], 1, 1)).astype(BF))
                probs[h].append(e.astype(BF))
        dq, dk, dv = [None, None], [], []
        for h in range(2):
            km = jnp.where(lo if h == 0 else ~lo, K, zero)
            hs = slice(h * HD, (h + 1) * HD)
            for qb in range(2):
                x = dot(grads[h][qb], km[: half * (qb + 1)])
                dq[qb] = x if h == 0 else dq[qb] + x
            for left, (first, second), to in ((QT, grads[h], dk), (DT, probs[h], dv)):
                early = dot(left[hs], jnp.concatenate([first, second[:, :half]], axis=0))
                to.append(jnp.concatenate([early, dot(left[hs, half:], second[:, half:])], axis=1))
        for i in range(2):
            joined[pl.ds(pl.multiple_of(w * win + i * half, half), half), pc] = dq[i].astype(BF)
        for i, v in enumerate((dk, dv)):
            joined[R, columns_of(width * (i + 1) + p * 128, 128)] = jnp.concatenate(v, axis=0).astype(BF).T

    def qkv_grad(*some):
        def one(m, _):
            total = None
            for w in range(windows):
                R = pl.ds(w * win, win)
                right = jnp.concatenate(
                    [joined[R, pl.ds(width * i + p * 128, 128)] for p in some for i in range(3)], axis=1
                )
                d = dot(pb[R, columns_of(m * half, half)], right, 0, 0)
                total = d if total is None else total + d
            total = total.astype(BF)
            if len(some) == 2:
                for j in range(2):
                    G["Q0"][j, pl.ds(8 * m, 8)] = total[:, 384 * j : 384 * (j + 1)].reshape(8, 32, 384)
            else:
                G["QA" if some[0] == 1 else "QB"][m] = total.reshape(16, 16, 384)
            return 0

        lax.fori_loop(0, 2, one, 0)

    def add_position(p):
        cols = [pl.ds(width * i + p * 128, 128) for i in range(3)]
        total = []
        for c in cols:
            v = joined[pl.ds(0, win), c].astype(F32)
            for w in range(1, windows):
                v = v + joined[pl.ds(w * win, win), c].astype(F32)
            total.append(v.astype(BF))
        part = dot(jnp.concatenate(total, axis=1), jnp.concatenate([wq[:, c] for c in cols], axis=1), 1, 1)
        nf[...] = nf[...] + part

    def steps_at(phase, at):
        run_steps(SCHEDULE.get((phase, at), ()))

    total = cot[pl.ds(0, win), :].astype(F32)
    for w in range(1, windows):
        total = total + cot[pl.ds(w * win, win), :].astype(F32)
    nf[...] = total
    order = (0, 2, 1, 3)
    for i, p in enumerate(order):
        hooked("back%d" % i, lambda t, _: attend_back(t, p), windows)
        if i == 3:
            add_position(p)
            G["P"][...] = nf[...].astype(BF).reshape(2, 16, half // 16, 512)
            steps_at("P", 0)
        if i > 0:
            qkv_grad(*((0, 2) if i == 1 else (p,)))
        steps_at("q%d" % i, 0)
        if i < 3:
            add_position(p)
            steps_at("add%d" % i, 0)

    def finish(w, _):
        R = rows_of(w, win)
        cot[R, :] = (cot[R, :].astype(F32) + dot(joined[R, :], wq[...], 1, 1)).astype(BF)
        return 0

    hooked("fin", finish, windows)
    ig_copy = pltpu.make_async_copy(cot, ig_h, out_sem.at[1])
    ig_copy.start()
    small_copy = pltpu.make_async_copy(small, small_h, out_sem.at[2])
    small_copy.start()
    run_steps(TAIL)
    if fused:
        for name in NAMES:
            results_out(name, False)
    if not fused:
        outs = [pltpu.make_async_copy(G[nm], F[nm], in_sem.at[i]) for i, nm in enumerate(NAMES)]
        for c in outs:
            c.start()
        for c in outs:
            c.wait()
    out_copy.wait()
    ig_copy.wait()
    small_copy.wait()


def scratch_of(fused, dims):
    win, width, hidden, windows = dims
    rows = win * windows
    V, dma = pltpu.VMEM, pltpu.SemaphoreType.DMA
    b = {k: V((rows, width), BF) for k in ("tok", "cot", "mix", "u1", "pb", "nb", "augq")}
    b.update({k: V((rows, hidden), BF) for k in ("act", "gp")})
    b.update(
        pos=V((win, width), BF),
        augk=V((rows, 128), BF),
        wq=V((width, 3 * width), BF),
        wo=V((width, width), BF),
        wu=V((width, hidden), BF),
        wd=V((hidden, width), BF),
        joined=V((rows, 3 * width), BF),
        rs1=V((win, 128), F32),
        nf=V((win, width), F32),
        small=V((8, width), F32),
        in_sem=dma((12,)),
        out_sem=dma((3,)),
    )
    b.update({"G" + k: V((2, PIECES) + CHUNKS[k], BF) for k in NAMES})
    if fused:
        for k in NAMES:
            lead = {"M": (16,), "A": (8,), "B": (4,), "Z": (3,)}
            if k in DIRECT:
                lead = {"M": (16,), "A": (3, 4), "Z": (3,), "X": (16,)}
            b.update({buf + k: V(n + CHUNKS[k], BF) for buf, n in lead.items()})
        b.update({k: V((8, width), F32) for k in ("s_mp", "s_x", "s_y")})
        b.update(
            s_z=V((4, 8, width), F32),
            wsem=dma((2, 6)),
            csend=dma((len(NAMES), 15)),
            crecv=dma((len(NAMES), 15)),
            ssend=dma((6,)),
            srecv=dma((6,)),
            lsem=dma((2 * len(NAMES),)),
        )
    return b


def layer(fused, tok, cot, pos, seg, wq, wo, wu, wd, g1, b1, g2, b2, hidden):
    rows, width = tok.shape
    win = pos.shape[0]
    windows = rows // win
    hbm = pl.BlockSpec(memory_space=pl.ANY)
    vmem = pl.BlockSpec(memory_space=pltpu.VMEM)
    shape = jax.ShapeDtypeStruct
    full = {k: (PIECES,) + v if fused and k not in DIRECT else (2, PIECES) + v for k, v in CHUNKS.items()}
    full["Q1"] = full["QA"]
    outs = [shape((rows, width), BF), shape((rows, width), BF), shape((8, width), F32)]
    outs += [shape(full[k], BF) for k in (RESULTS if fused else NAMES)]
    scratch = list(scratch_of(fused, (win, width, hidden, windows)).values())
    params = dict(vmem_limit_bytes=64 << 20)
    if fused:
        params.update(collective_id=0, has_side_effects=True)
    return pl.pallas_call(
        functools.partial(kernel, fused, (win, width, hidden, windows)),
        out_shape=outs,
        in_specs=[hbm] * 3 + [vmem] + [hbm] * 4 + [vmem] * 4,
        out_specs=[hbm] * len(outs),
        scratch_shapes=scratch,
        compiler_params=pltpu.CompilerParams(**params),
        name="layer",
    )(tok, cot, pos, seg, wq, wo, wu, wd, g1, b1, g2, b2)


def widen(got, wide):
    rows = got.shape[-2]

    def one(i, _):
        piece = got[i] if len(got.shape) == 3 else got[i // PIECES, lax.rem(i, PIECES)]
        wide[pl.ds(pl.multiple_of(i * rows, rows), rows), :] = piece.astype(F32)
        return 0

    lax.fori_loop(0, wide.shape[0] // rows, one, 0)


def finish_kernel(*refs):
    (out_h, ig_h, small), grads = refs[:3], dict(zip(RESULTS, refs[3 : 3 + len(RESULTS)]))
    refs = refs[3 + len(RESULTS) :]
    out_o, ig_o, pos_o, qkv_o, wo_o, up_o, down_o = refs[:7]
    norms = refs[7:11]
    refs = refs[11:]
    got = dict(zip(RESULTS, refs[: len(RESULTS)]))
    wide = dict(zip(RESULTS, refs[len(RESULTS) : 2 * len(RESULTS)]))
    held, in_sem, out_sem = refs[2 * len(RESULTS) :]
    last, loads, passed = [], [], []
    for i, (src, dst) in enumerate(((out_h, out_o), (ig_h, ig_o))):
        passed.append(pltpu.make_async_copy(src, held.at[i], in_sem.at[len(RESULTS) + i]))
        last.append(pltpu.make_async_copy(held.at[i], dst, out_sem.at[len(RESULTS) + i]))
    for c in passed:
        c.start()
    for i, k in enumerate(RESULTS):
        loads.append(pltpu.make_async_copy(grads[k], got[k], in_sem.at[i]))
        loads[-1].start()
    rows = down_o.shape[0] // 2
    places = {
        "D0": down_o.at[pl.ds(0, rows)],
        "D1": down_o.at[pl.ds(rows, rows)],
        "U0": up_o.at[:, pl.ds(0, 512)],
        "U1": up_o.at[:, pl.ds(512, 512)],
        "O": wo_o,
        "Q0": qkv_o.at[:, pl.ds(0, 384)],
        "Q1": qkv_o.at[:, pl.ds(384, 384)],
        "P": pos_o,
    }
    for i in range(2):
        passed[i].wait()
        last[i].start()
    for i, k in enumerate(RESULTS):
        loads[i].wait()
        widen(got[k], wide[k])
        last.append(pltpu.make_async_copy(wide[k], places[k], out_sem.at[i]))
        last[-1].start()
    for ref, row in zip(norms, (2, 3, 0, 1)):
        ref[...] = small[row]
    for c in last:
        c.wait()


def finish(out, ig, small, grads, win, width, hidden):
    hbm = pl.BlockSpec(memory_space=pl.ANY)
    vmem = pl.BlockSpec(memory_space=pltpu.VMEM)
    shape = jax.ShapeDtypeStruct
    outs = [shape(out.shape, BF), shape(ig.shape, BF), shape((win, width), F32)]
    outs += [shape((width, 3 * width // 2), F32), shape((width // 2, width), F32)]
    outs += [shape((width, hidden // 2), F32), shape((hidden // 2, width), F32)]
    outs += [shape((width,), F32)] * 4
    dma = pltpu.SemaphoreType.DMA
    scratch = [pltpu.VMEM(g.shape, BF) for g in grads]
    scratch += [pltpu.VMEM((g.size // g.shape[-1], g.shape[-1]), F32) for g in grads]
    scratch += [pltpu.VMEM((2,) + out.shape, BF), dma((len(RESULTS) + 2,)), dma((len(RESULTS) + 2,))]
    return pl.pallas_call(
        finish_kernel,
        out_shape=outs,
        in_specs=[hbm, hbm, vmem] + [hbm] * len(RESULTS),
        out_specs=[hbm] * 7 + [vmem] * 4,
        scratch_shapes=scratch,
        compiler_params=pltpu.CompilerParams(vmem_limit_bytes=64 << 20),
        name="finish",
    )(out, ig, small, *grads)


def local(shards, tokens, segment_ids, cotangent, pos_table, w_qkv, w_out, w_up, w_down, g1, b1, g2, b2):
    dp_size, mp_size = shards
    width = tokens.shape[1]
    win = pos_table.shape[0]
    hidden = w_up.shape[1] * mp_size
    fused = dp_size == PIECES
    gains = [v.reshape(1, width) for v in (g1, b1, g2, b2)]
    if fused:
        out, ig, small, *grads = layer(
            True, tokens, cotangent, pos_table, segment_ids, w_qkv, w_out, w_up, w_down, *gains, hidden
        )
        return tuple(finish(out, ig, small, grads, win, width, hidden))
    windows = tokens.shape[0] // win
    seg = jnp.roll(segment_ids, -lax.axis_index("mp") * windows, axis=0)
    wq = lax.all_gather(w_qkv, "mp", axis=1, tiled=True)
    wo = lax.all_gather(w_out, "mp", axis=0, tiled=True)
    wu = lax.all_gather(w_up, "mp", axis=1, tiled=True)
    wd = lax.all_gather(w_down, "mp", axis=0, tiled=True)
    out, ig, small, *grads = layer(False, tokens, cotangent, pos_table, seg, wq, wo, wu, wd, *gains, hidden)
    g = dict(zip(NAMES, (v.astype(F32) for v in grads)))
    g = {
        k: v if k in DIRECT else lax.psum(lax.psum_scatter(v, "mp", scatter_dimension=0, tiled=False), "dp")
        for k, v in g.items()
    }
    pos, QA, QB, small = lax.psum((g["P"], g["QA"], g["QB"], small), ("dp", "mp"))
    g["Q1"] = jnp.where(lax.axis_index("mp") == 0, QA, QB)
    scale = jnp.array([HD**-0.5, 1, 1], F32)[:, None, None]
    Q = [(g[k].reshape(width, 3, 2, HD) * scale).transpose(0, 2, 1, 3).reshape(width, 6 * HD) for k in ("Q0", "Q1")]
    return (
        out,
        ig,
        pos.reshape(win, width),
        jnp.concatenate(Q, axis=1),
        g["O"].reshape(-1, width),
        jnp.concatenate([g["U0"].reshape(width, -1), g["U1"].reshape(width, -1)], axis=1),
        jnp.concatenate([g["D0"].reshape(-1, width), g["D1"].reshape(-1, width)], axis=0),
        small[2],
        small[3],
        small[0],
        small[1],
    )


def solution(mesh):
    cut, copied = P(("dp", "mp"), None), P()
    columns, split_rows = P(None, "mp"), P("mp", None)
    weights = (columns, split_rows, columns, split_rows)
    return jax.shard_map(
        functools.partial(local, (mesh.shape["dp"], mesh.shape["mp"])),
        mesh=mesh,
        in_specs=(cut, P("dp", None), cut, copied) + weights + (copied,) * 4,
        out_specs=(cut, cut, copied) + weights + (copied,) * 4,
        check_vma=False,
    )
```

```python
import functools

import jax
import jax.numpy as jnp
from jax import lax
from jax.experimental import pallas as pl
from jax.experimental.pallas import tpu as pltpu
from jax.sharding import PartitionSpec as P

BF = jnp.bfloat16
F32 = jnp.float32
MESH = pl.DeviceIdType.MESH
HD = 64
EPSILON = 1e-05
NEG = -1e30
GELU_A = 0.7978845608028654
GELU_B = 0.044715

CHUNKS = {
    "D0": (32, 512),
    "D1": (32, 512),
    "U0": (32, 512),
    "U1": (32, 512),
    "O": (16, 512),
    "Q0": (32, 384),
    "QA": (16, 384),
    "QB": (16, 384),
    "P": (16, 512),
}
NAMES = tuple(CHUNKS)
DIRECT = ("QA", "QB", "P")
RESULTS = ("D0", "D1", "U0", "U1", "O", "Q0", "Q1", "P")
PIECES = 16
UNROLLED = ("nb", )

SCHEDULE = {
    ("down", 1): (("D0", 0),),
    ("down", 3): (("D0", 1), ("D1", 0),),
    ("slope", 2): (("D1", 1),),
    ("up", 0): (("D0", 2),),
    ("up", 1): (("U0", 0),),
    ("up", 3): (("D1", 2), ("U0", 1), ("U1", 0),),
    ("nb", 0): (("D0", 3),),
    ("nb", 1): (("U1", 1),),
    ("nb", 2): (("D1", 3),),
    ("nb", 3): (("D0", 4), ("U0", 2),),
    ("O", 0): (("O", 0), ("sm", 0),),
    ("back0", 0): (("U1", 2),),
    ("back0", 1): (("D1", 4), ("O", 1), ("sm", 1),),
    ("back0", 2): (("U0", 3),),
    ("back0", 3): (("D0", 5),),
    ("back1", 0): (("U1", 3), ("sm", 2),),
    ("back1", 1): (("D1", 5), ("O", 2),),
    ("back1", 2): (("U0", 4),),
    ("back1", 3): (("D0", 6), ("sm", 3),),
    ("q1", 0): (("D1", 6), ("U1", 4), ("O", 3), ("Q0", 0),),
    ("back2", 0): (("U0", 5), ("sm", 4),),
    ("back2", 1): (("Q0", 1),),
    ("back2", 2): (("D0", 7), ("U1", 5),),
    ("back2", 3): (("O", 4),),
    ("q2", 0): (("D1", 7), ("U0", 6), ("QA", 0),),
    ("back3", 1): (("O", 5), ("Q0", 2), ("QA", 1),),
    ("back3", 2): (("U1", 6),),
    ("P", 0): (("U0", 7), ("P", 0),),
    ("q3", 0): (("O", 6), ("Q0", 3), ("QB", 0),),
    ("fin", 0): (("P", 1),),
    ("fin", 1): (("QA", 2), ("QB", 1),),
    ("fin", 3): (("U1", 7), ("Q0", 4),),
}
TAIL = (
    ("QA", 3),
    ("O", 7),
    ("P", 2),
    ("Q0", 5),
    ("QA", 4),
    ("QB", 2),
    ("P", 3),
    ("QB", 3),
    ("Q0", 6),
    ("P", 4),
    ("QA", 5),
    ("QB", 4),
    ("QA", 6),
    ("Q0", 7),
    ("P", 5),
    ("P", 6),
    ("QB", 5),
    ("QB", 6),
)


def dot(left, right, left_dim=1, right_dim=0):
    return lax.dot_general(
        left, right, (((left_dim,), (right_dim,)), ((), ())), preferred_element_type=F32
    )


def lanes(shape):
    return lax.broadcasted_iota(jnp.int32, shape, len(shape) - 1)


def rows_of(w, win):
    return pl.ds(pl.multiple_of(w * win, win), win)


def columns_of(start, size):
    return pl.ds(pl.multiple_of(start, 128), size)


def row_mean(v):
    return jnp.mean(v, axis=-1, keepdims=True)


def kernel(fused, dims, *refs):
    win, width, hidden, windows = dims
    half_hidden = hidden // 2
    half = win // 2
    (tok_h, cot_h, pos_h, seg, wq_h, wo_h, wu_h, wd_h, g1, b1, g2, b2) = refs[:12]
    refs = refs[12:]
    out_h, ig_h, small_h = refs[:3]
    results = RESULTS if fused else NAMES
    F = dict(zip(results, refs[3 : 3 + len(results)]))
    b = dict(zip(scratch_of(fused, dims), refs[3 + len(results) :]))
    tok, cot, pos, augk = b["tok"], b["cot"], b["pos"], b["augk"]
    wq, wo, wu, wd = b["wq"], b["wo"], b["wu"], b["wd"]
    joined, mix, u1, rs1, pb, nb = b["joined"], b["mix"], b["u1"], b["rs1"], b["pb"], b["nb"]
    act, gp, augq, nf, small = b["act"], b["gp"], b["augq"], b["nf"], b["small"]
    G, R_mp, R_a, R_b, R_z = ({k: b.get(buf + k) for k in NAMES} for buf in ("G", "M", "A", "B", "Z"))
    in_sem, out_sem = b["in_sem"], b["out_sem"]

    pairs = width // 128

    copies = {}

    def fetch(name, src, dst, k):
        copies[name] = pltpu.make_async_copy(src, dst, in_sem.at[k])
        copies[name].start()

    if fused:
        wsem, csend, crecv, ssend, srecv, lsem = (
            b[k] for k in ("wsem", "csend", "crecv", "ssend", "srecv", "lsem")
        )
        dp = lax.axis_index("dp")
        mp = lax.axis_index("mp")
        zc = dp // 4
        yc = lax.rem(dp // 2, 2)
        xc = lax.rem(dp, 2)
        ac = jnp.where(mp == 0, xc, yc)
        bc = jnp.where(mp == 0, yc, xc)
        step_a = jnp.where(mp == 0, 1, 2)
        step_b = jnp.where(mp == 0, 2, 1)
        dev_mp = (dp, 1 - mp)
        dev_a = (dp + step_a * (1 - 2 * ac), mp)
        dev_b = (dp + step_b * (1 - 2 * bc), mp)
        dev_d = (dp + step_a * (1 - 2 * ac) + step_b * (1 - 2 * bc), mp)
        dev_x = (dp + 1 - 2 * xc, mp)
        dev_y = (dp + 2 * (1 - 2 * yc), mp)
        zs = [lax.rem(zc + k, 4) for k in (1, 2, 3)]
        dev_z = [(lax.rem(dp, 4) + 4 * z, mp) for z in zs]
        barrier = pltpu.get_barrier_semaphore()
        for dev in [dev_mp, dev_a, dev_b, dev_d] + dev_z:
            pl.semaphore_signal(barrier, inc=1, device_id=dev, device_id_type=MESH)

    raw_width = wq_h.shape[1]
    raw = act.at[pl.ds(0, width), pl.ds(0, raw_width)]
    fetch("wq", wq_h, raw, 2)
    fetch("tok", tok_h, tok, 0)
    fetch("pos", pos_h, pos, 1)
    wparts = []
    if fused:
        wparts.append((wo_h, wo.at[pl.ds(pl.multiple_of(mp * half, half), half), :]))
        wparts.append((wu_h, wu.at[:, columns_of(half_hidden * mp, half_hidden)]))
        wparts.append((wd_h, wd.at[pl.ds(pl.multiple_of(mp * half_hidden, half_hidden), half_hidden), :]))
    else:
        wparts += [(wo_h, wo), (wu_h, wu), (wd_h, wd)]
    for i, (src, dst) in enumerate(wparts):
        fetch("w%d" % i, src, dst, 5 + i)
    fetch("cot", cot_h, cot, 4)
    small[...] = jnp.zeros_like(small)
    rs1[...] = jnp.zeros_like(rs1)

    l64 = lax.rem(lanes((win, 128)), HD)
    lo = lanes((win, 128)) < HD

    columns = seg[...].astype(F32).T
    mine = (mp if fused else 0) * windows
    for w in range(windows):
        R = pl.ds(w * win, win)
        column = jnp.sum(
            jnp.where(lanes(columns.shape) == mine + w, columns, 0.0), axis=1, keepdims=True
        ).astype(jnp.int32)
        augk[R, :] = jnp.where((l64 == column) | ((l64 >= 8) & (l64 < 11)), 1.0, 0.0).astype(BF)

    copies["wq"].wait()
    own_columns = mp * raw_width // 3 if fused else 0
    for p in range(raw_width // 384):
        cut = [raw[:, pl.ds(p * 384 + 128 * i, 128)] for i in range(3)]
        low = lanes((width, 128)) < HD
        swapped = [pltpu.roll(c.astype(F32), HD, 1).astype(BF) for c in cut]
        q = jnp.where(low, cut[0], cut[1]) * BF(HD**-0.5)
        k = jnp.where(low, swapped[0], swapped[2])
        v = jnp.where(low, cut[1], cut[2])
        for i, part in enumerate((q, k, v)):
            wq[:, columns_of(own_columns + width * i + 128 * p, 128)] = part

    wremote = []
    if fused:
        pl.semaphore_wait(barrier, 7)
        slices = [wq.at[:, columns_of(own_columns + width * i, raw_width // 3)] for i in range(3)]
        for i, (src, dst) in enumerate([(x, x) for x in slices] + wparts):
            c = pltpu.make_async_remote_copy(
                src_ref=src, dst_ref=dst, send_sem=wsem.at[0, i], recv_sem=wsem.at[1, i],
                device_id=dev_mp, device_id_type=MESH,
            )
            c.start()
            wremote.append(c)

    def remote(src, dst, send, recv, dev):
        return pltpu.make_async_remote_copy(
            src_ref=src, dst_ref=dst, send_sem=send, recv_sem=recv, device_id=dev, device_id_type=MESH
        )

    def add(mine, got):
        mine[...] = mine[...] + got[...]

    def exchange(name, k):
        if not fused:
            return
        c = NAMES.index(name)
        g = G[name]
        direct = name in DIRECT
        own = g.at[mp]
        base = ac * 8 + bc * 4
        full = g.at[1 - mp]

        def send(src, dst, i, dev):
            return remote(src, dst, csend.at[c, i], crecv.at[c, i], dev)

        def to_z(src, dst_of):
            return [send(src(j), dst_of(j), 3 + j, dev_z[j]) for j in range(3)]

        if direct:
            slots = R_a[name]
            places = [(1 - ac) * 8 + bc * 4, ac * 8 + (1 - bc) * 4, (1 - ac) * 8 + (1 - bc) * 4]
            plane = [dev_a, dev_b, dev_d]
            stages = [
                lambda: [send(full, R_mp[name], 0, dev_mp)],
                lambda: [send(own.at[pl.ds(places[j], 4)], slots.at[j], 6 + j, plane[j]) for j in range(3)],
                lambda: [send(own.at[base + zs[j]], R_z[name].at[j], 3 + j, dev_z[j]) for j in range(3)],
                lambda: [send(full.at[base + zc], full.at[base + zc], 9 + j, dev_z[j]) for j in range(3)],
                lambda: [send(full.at[pl.ds(base, 4)], full.at[pl.ds(base, 4)], 12 + j, plane[j]) for j in range(3)],
                lambda: [send(full, b["X" + name], 1, dev_mp)],
            ]
        else:
            stages = [
                lambda: [send(full, R_mp[name], 0, dev_mp)],
                lambda: [send(own.at[pl.ds((1 - ac) * 8, 8)], R_a[name], 1, dev_a)],
                lambda: [send(own.at[pl.ds(ac * 8 + (1 - bc) * 4, 4)], R_b[name], 2, dev_b)],
                lambda: [send(own.at[base + zs[j]], R_z[name].at[j], 3 + j, dev_z[j]) for j in range(3)],
                lambda: [send(full.at[base + zc], full.at[base + zc], 6 + j, dev_z[j]) for j in range(3)],
                lambda: [send(full.at[pl.ds(base, 4)], full.at[pl.ds(base, 4)], 9, dev_b)],
                lambda: [send(full.at[pl.ds(ac * 8, 8)], full.at[pl.ds(ac * 8, 8)], 10, dev_a)],
            ]
        if 0 < k <= len(stages):
            for copy in stages[k - 1]():
                copy.wait()
        if k == 1:
            add(own, R_mp[name])
        if direct and k == 2:
            at = own.at[pl.ds(base, 4)]
            at[...] = (
                (at[...].astype(F32) + slots[0].astype(F32)) + (slots[1].astype(F32) + slots[2].astype(F32))
            ).astype(BF)
        if not direct and k == 2:
            add(own.at[pl.ds(ac * 8, 8)], R_a[name])
        if not direct and k == 3:
            add(own.at[pl.ds(base, 4)], R_b[name])
        if k == (3 if direct else 4):
            total = own[base + zc].astype(F32)
            for j in range(3):
                total = total + R_z[name][j].astype(F32)
            if name[0] == "Q":
                q, kk, v = total[:, :128] * (HD**-0.5), total[:, 128:256], total[:, 256:]
                total = jnp.concatenate(
                    [q[:, :HD], kk[:, :HD], v[:, :HD], q[:, HD:], kk[:, HD:], v[:, HD:]], axis=1
                )
            full[base + zc] = total.astype(BF)
        if k < len(stages):
            for copy in stages[k]():
                copy.start()
        if k == len(stages):
            results_out(name, True)

    def results_out(name, start):
        full, i = G[name].at[1 - mp], 2 * NAMES.index(name)
        if name not in DIRECT:
            moves = [pltpu.make_async_copy(full, F[name], lsem.at[i])]
        else:
            to = F["P" if name == "P" else "Q1"]
            moves = [pltpu.make_async_copy(full, to.at[mp], lsem.at[i])]
            moves.append(pltpu.make_async_copy(b["X" + name], to.at[1 - mp], lsem.at[i + 1]))

        def go():
            for m in moves:
                m.start() if start else m.wait()

        if name[0] == "Q" and name != "Q0":
            pl.when(mp == ("QA", "QB").index(name))(go)
        else:
            go()

    def exchange_small(k):
        if not fused:
            return
        legs = [(b["s_mp"], dev_mp, 0), (b["s_x"], dev_x, 1), (b["s_y"], dev_y, 2)]
        if k > 0 and k <= 3:
            buf, dev, s = legs[k - 1]
            remote(small, buf, ssend.at[s], srecv.at[s], dev).wait()
            small[...] = small[...] + buf[...]
        if k < 3:
            buf, dev, s = legs[k]
            remote(small, buf, ssend.at[s], srecv.at[s], dev).start()
        zcs = [remote(small, b["s_z"].at[zc], ssend.at[3 + j], srecv.at[3 + j], dev_z[j]) for j in range(3)]
        if k == 3:
            b["s_z"][zc] = small[...]
            for z in zcs:
                z.start()
        if k == 4:
            for z in zcs:
                z.wait()
            small[...] = (b["s_z"][0] + b["s_z"][1]) + (b["s_z"][2] + b["s_z"][3])

    causal = jnp.where(lanes((half, half)) <= lax.broadcasted_iota(jnp.int32, (half, half), 0), 0.0, NEG)
    def attend(w, p):
        R = rows_of(w, win)
        Q, K, V = (joined[R, columns_of(width * i + p * 128, 128)] for i in range(3))
        ak = augk[R, :]
        ones = jnp.ones((win, 128), BF)
        zero = jnp.zeros((win, 128), BF)
        aq = jnp.where(l64 < 8, (ones - ak) * BF(NEG), zero)
        qs, ks, vs = [], [], []
        for h in range(2):
            mine = lo if h == 0 else ~lo
            qs.append(jnp.where(mine, Q, aq))
            ks.append(jnp.where(mine, K, ak))
            vs.append(jnp.concatenate([jnp.where(mine, V, zero), jnp.where(mine, ones, zero)], axis=1))
        for qb in range(2):
            kl = half * (qb + 1)
            es, ms = [], []
            for h in range(2):
                s = dot(qs[h][qb * half : (qb + 1) * half], ks[h][:kl], 1, 1)
                if qb == 0:
                    s = s + causal
                else:
                    s = jnp.concatenate([s[:, :half], s[:, half:] + causal], axis=1)
                m = jnp.max(s, axis=1, keepdims=True)
                es.append(jnp.exp(s - m).astype(BF))
                ms.append(m)
            ov = dot(jnp.concatenate(es, axis=1), jnp.concatenate([v[:kl] for v in vs], axis=0))
            total = ov[:, 128:]
            rr = pl.ds(pl.multiple_of(w * win + qb * half, half), half)
            mix[rr, columns_of(p * 128, 128)] = (ov[:, :128] / total).astype(BF)
            low = lo[:half]
            lse = jnp.where(low, ms[0], ms[1]) + jnp.log(total)
            x = -pltpu.roll(lse, HD, 1)
            hi = x.astype(BF)
            x = x - hi.astype(F32)
            mid = x.astype(BF)
            last = (x - mid.astype(F32)).astype(BF)
            l6 = l64[:half]
            a = aq[qb * half : (qb + 1) * half]
            a = jnp.where(l6 == 8, hi, a)
            a = jnp.where(l6 == 9, mid, a)
            augq[rr, columns_of(p * 128, 128)] = jnp.where(l6 == 10, last, a)

    copies["tok"].wait()
    copies["pos"].wait()

    def place(w, _):
        R = rows_of(w, win)
        pb[R, :] = (tok[R, :].astype(F32) + pos[...].astype(F32)).astype(BF)
        return 0

    lax.fori_loop(0, windows, place, 0)
    for part in range(2 if fused else 1):
        if part:
            for c in wremote[:3]:
                c.wait()
        span = width // 2 if fused else width
        start = (mp if part == 0 else 1 - mp) * span if fused else 0

        def project(w, _):
            R = rows_of(w, win)
            for i in range(3):
                cs = columns_of(width * i + start, span)
                joined[R, cs] = dot(pb[R, :], wq[:, cs]).astype(BF)
            return 0

        lax.fori_loop(0, windows, project, 0)

    def attend_window(w, _):
        for p in range(pairs):
            attend(w, p)
        return 0

    lax.fori_loop(0, windows, attend_window, 0)

    for i in range(3):
        copies["w%d" % i].wait()
    for c in wremote[3:]:
        c.wait()
    copies["cot"].wait()

    def feed(w, _):
        R = rows_of(w, win)
        r1 = (tok[R, :].astype(F32) + pos[...].astype(F32)) + dot(mix[R, :], wo[...])
        center = r1 - row_mean(r1)
        rstd = lax.rsqrt(row_mean(center * center) + EPSILON)
        unit = center * rstd
        u1[R, :] = unit.astype(BF)
        rs1[...] = jnp.where(lanes((win, 128)) == w, rstd, rs1[...])
        normed = unit * g1[...] + b1[...]
        nf[...] = normed
        nb[R, :] = normed.astype(BF)

        r2 = nf[...]
        for c in range(hidden // 512):
            cs = pl.ds(c * 512, 512)
            v = dot(nb[R, :], wu[:, cs]).astype(BF)
            v2 = v * v
            t = jnp.tanh(v * (BF(GELU_A) + BF(GELU_A * GELU_B) * v2))
            h = BF(0.5) + BF(0.5) * t
            active = v * h
            act[R, cs] = active
            gp[R, cs] = h + h * ((BF(1) - h) * (v * (BF(2 * GELU_A) + BF(6 * GELU_A * GELU_B) * v2)))
            r2 = r2 + dot(active, wd[cs, :])
        center = r2 - row_mean(r2)
        rstd = lax.rsqrt(row_mean(center * center) + EPSILON)
        unit = center * rstd
        tok[R, :] = (unit * g2[...] + b2[...]).astype(BF)
        up = cot[R, :].astype(F32)
        small[0:1, :] += jnp.sum(up * unit, axis=0, keepdims=True)
        small[1:2, :] += jnp.sum(up, axis=0, keepdims=True)
        e = up * g2[...]
        cot[R, :] = (rstd * (e - row_mean(e) - unit * row_mean(e * unit))).astype(BF)
        return 0

    lax.fori_loop(0, windows, feed, 0)
    out_copy = pltpu.make_async_copy(tok, out_h, out_sem.at[0])
    out_copy.start()

    def hooked(phase, body, count, first=0):
        def one(t, _):
            body(t, 0)
            for at in range(count):
                steps = SCHEDULE.get((phase, first + at))
                if steps:
                    pl.when(t == at)(functools.partial(run_steps, steps))
            return 0

        if phase not in UNROLLED:
            lax.fori_loop(0, count, one, 0)
            return
        for t in range(count):
            body(t, 0)
            run_steps(SCHEDULE.get((phase, t), ()))

    def run_steps(steps):
        for name, k in steps:
            if name == "sm":
                exchange_small(k)
            else:
                exchange(name, k)

    halves = hidden // 1024

    def down_tile(part, m, _):
        tile = m * halves + part
        d = dot(act[:, columns_of(tile * 512, 512)], cot[...], 0, 0).astype(BF).reshape(16, 32, 512)
        G["D%d" % part][m] = d
        return 0

    for part in range(2):
        hooked("down", functools.partial(down_tile, part), 2, 2 * part)

    def slope(w, _):
        R = rows_of(w, win)
        for c in range(hidden // 512):
            cs = pl.ds(c * 512, 512)
            d = dot(cot[R, :], wd[pl.ds(c * 512, 512), :], 1, 1)
            gp[R, cs] = (d * gp[R, cs].astype(F32)).astype(BF)
        return 0

    hooked("slope", slope, windows)

    def up_tile(part, m, _):
        tile = m * halves + part
        d = dot(nb[...], gp[:, columns_of(tile * 512, 512)], 0, 0).astype(BF).reshape(16, 32, 512)
        G["U%d" % part][m] = d
        return 0

    for part in range(2):
        hooked("up", functools.partial(up_tile, part), 2, 2 * part)

    def norm_back(w, _):
        R = rows_of(w, win)
        ng = cot[R, :].astype(F32) + dot(gp[R, :], wu[...], 1, 1)
        unit = u1[R, :].astype(F32)
        small[2:3, :] += jnp.sum(ng * unit, axis=0, keepdims=True)
        small[3:4, :] += jnp.sum(ng, axis=0, keepdims=True)
        e = ng * g1[...]
        rstd = jnp.sum(jnp.where(lanes((win, 128)) == w, rs1[...], 0.0), axis=1, keepdims=True)
        rg = (rstd * (e - row_mean(e) - unit * row_mean(e * unit))).astype(BF)
        cot[R, :] = rg
        u1[R, :] = dot(rg, wo[...], 1, 1).astype(BF)
        return 0

    hooked("nb", norm_back, windows)

    G["O"][...] = dot(mix[...], cot[...], 0, 0).astype(BF).reshape(2, 16, half // 16, 512)
    run_steps(SCHEDULE.get(("O", 0), ()))

    flip = (lax.broadcasted_iota(jnp.int32, (256, 128), 0) % 128 < HD) != (lanes((256, 128)) < HD)
    swap = jnp.where(flip, 1.0, 0.0).astype(BF)

    def attend_back(w, p):
        R = rows_of(w, win)
        pc = columns_of(p * 128, 128)
        Q, K, V = (joined[R, columns_of(width * i + p * 128, 128)] for i in range(3))
        D = u1[R, pc]
        prod = D.astype(F32) * mix[R, pc].astype(F32)
        ph = prod.astype(BF)
        pr = (prod - ph.astype(F32)).astype(BF)
        x = -dot(jnp.concatenate([ph, pr], axis=1), swap)
        hi = x.astype(BF)
        mid = (x - hi.astype(F32)).astype(BF)
        zero = jnp.zeros((win, 128), BF)
        ad = jnp.where(l64 == 8, hi, jnp.where(l64 == 9, mid, zero))
        av = jnp.where((l64 == 8) | (l64 == 9), jnp.ones((win, 128), BF), zero)
        aq, ak = augq[R, pc], augk[R, :]
        QT, DT = Q.T, D.T
        probs, grads = [[], []], [[], []]
        for h in range(2):
            mine = lo if h == 0 else ~lo
            qa, ka, va, da = (jnp.where(mine, i, j) for i, j in ((Q, aq), (K, ak), (V, av), (D, ad)))
            for qb in range(2):
                kl = half * (qb + 1)
                qs = slice(qb * half, kl)
                s = dot(qa[qs], ka[:kl], 1, 1)
                s = s + causal if qb == 0 else jnp.concatenate([s[:, :half], s[:, half:] + causal], axis=1)
                e = jnp.exp(s)
                grads[h].append((e * dot(da[qs], va[:kl], 1, 1)).astype(BF))
                probs[h].append(e.astype(BF))
        dq, dk, dv = [None, None], [], []
        for h in range(2):
            km = jnp.where(lo if h == 0 else ~lo, K, zero)
            hs = slice(h * HD, (h + 1) * HD)
            for qb in range(2):
                x = dot(grads[h][qb], km[: half * (qb + 1)])
                dq[qb] = x if h == 0 else dq[qb] + x
            for left, (first, second), to in ((QT, grads[h], dk), (DT, probs[h], dv)):
                early = dot(left[hs], jnp.concatenate([first, second[:, :half]], axis=0))
                to.append(jnp.concatenate([early, dot(left[hs, half:], second[:, half:])], axis=1))
        for i in range(2):
            joined[pl.ds(pl.multiple_of(w * win + i * half, half), half), pc] = dq[i].astype(BF)
        for i, v in enumerate((dk, dv)):
            joined[R, columns_of(width * (i + 1) + p * 128, 128)] = jnp.concatenate(v, axis=0).astype(BF).T

    def qkv_grad(*some):
        def one(m, _):
            total = None
            for w in range(windows):
                R = pl.ds(w * win, win)
                right = jnp.concatenate(
                    [joined[R, pl.ds(width * i + p * 128, 128)] for p in some for i in range(3)], axis=1
                )
                d = dot(pb[R, columns_of(m * half, half)], right, 0, 0)
                total = d if total is None else total + d
            total = total.astype(BF)
            if len(some) == 2:
                for j in range(2):
                    G["Q0"][j, pl.ds(8 * m, 8)] = total[:, 384 * j : 384 * (j + 1)].reshape(8, 32, 384)
            else:
                G["QA" if some[0] == 1 else "QB"][m] = total.reshape(16, 16, 384)
            return 0

        lax.fori_loop(0, 2, one, 0)

    def add_position(p):
        cols = [pl.ds(width * i + p * 128, 128) for i in range(3)]
        total = []
        for c in cols:
            v = joined[pl.ds(0, win), c].astype(F32)
            for w in range(1, windows):
                v = v + joined[pl.ds(w * win, win), c].astype(F32)
            total.append(v.astype(BF))
        part = dot(jnp.concatenate(total, axis=1), jnp.concatenate([wq[:, c] for c in cols], axis=1), 1, 1)
        nf[...] = nf[...] + part

    def steps_at(phase, at):
        run_steps(SCHEDULE.get((phase, at), ()))

    total = cot[pl.ds(0, win), :].astype(F32)
    for w in range(1, windows):
        total = total + cot[pl.ds(w * win, win), :].astype(F32)
    nf[...] = total
    order = (0, 2, 1, 3)
    for i, p in enumerate(order):
        hooked("back%d" % i, lambda t, _: attend_back(t, p), windows)
        if i == 3:
            add_position(p)
            G["P"][...] = nf[...].astype(BF).reshape(2, 16, half // 16, 512)
            steps_at("P", 0)
        if i > 0:
            qkv_grad(*((0, 2) if i == 1 else (p,)))
        steps_at("q%d" % i, 0)
        if i < 3:
            add_position(p)
            steps_at("add%d" % i, 0)

    def finish(w, _):
        R = rows_of(w, win)
        cot[R, :] = (cot[R, :].astype(F32) + dot(joined[R, :], wq[...], 1, 1)).astype(BF)
        return 0

    hooked("fin", finish, windows)
    ig_copy = pltpu.make_async_copy(cot, ig_h, out_sem.at[1])
    ig_copy.start()
    small_copy = pltpu.make_async_copy(small, small_h, out_sem.at[2])
    small_copy.start()
    run_steps(TAIL)
    if fused:
        for name in NAMES:
            results_out(name, False)
    if not fused:
        outs = [pltpu.make_async_copy(G[nm], F[nm], in_sem.at[i]) for i, nm in enumerate(NAMES)]
        for c in outs:
            c.start()
        for c in outs:
            c.wait()
    out_copy.wait()
    ig_copy.wait()
    small_copy.wait()


def scratch_of(fused, dims):
    win, width, hidden, windows = dims
    rows = win * windows
    V, dma = pltpu.VMEM, pltpu.SemaphoreType.DMA
    b = {k: V((rows, width), BF) for k in ("tok", "cot", "mix", "u1", "pb", "nb", "augq")}
    b.update({k: V((rows, hidden), BF) for k in ("act", "gp")})
    b.update(
        pos=V((win, width), BF),
        augk=V((rows, 128), BF),
        wq=V((width, 3 * width), BF),
        wo=V((width, width), BF),
        wu=V((width, hidden), BF),
        wd=V((hidden, width), BF),
        joined=V((rows, 3 * width), BF),
        rs1=V((win, 128), F32),
        nf=V((win, width), F32),
        small=V((8, width), F32),
        in_sem=dma((12,)),
        out_sem=dma((3,)),
    )
    b.update({"G" + k: V((2, PIECES) + CHUNKS[k], BF) for k in NAMES})
    if fused:
        for k in NAMES:
            lead = {"M": (16,), "A": (8,), "B": (4,), "Z": (3,)}
            if k in DIRECT:
                lead = {"M": (16,), "A": (3, 4), "Z": (3,), "X": (16,)}
            b.update({buf + k: V(n + CHUNKS[k], BF) for buf, n in lead.items()})
        b.update({k: V((8, width), F32) for k in ("s_mp", "s_x", "s_y")})
        b.update(
            s_z=V((4, 8, width), F32),
            wsem=dma((2, 6)),
            csend=dma((len(NAMES), 15)),
            crecv=dma((len(NAMES), 15)),
            ssend=dma((6,)),
            srecv=dma((6,)),
            lsem=dma((2 * len(NAMES),)),
        )
    return b


def layer(fused, tok, cot, pos, seg, wq, wo, wu, wd, g1, b1, g2, b2, hidden):
    rows, width = tok.shape
    win = pos.shape[0]
    windows = rows // win
    hbm = pl.BlockSpec(memory_space=pl.ANY)
    vmem = pl.BlockSpec(memory_space=pltpu.VMEM)
    shape = jax.ShapeDtypeStruct
    full = {k: (PIECES,) + v if fused and k not in DIRECT else (2, PIECES) + v for k, v in CHUNKS.items()}
    full["Q1"] = full["QA"]
    outs = [shape((rows, width), BF), shape((rows, width), BF), shape((8, width), F32)]
    outs += [shape(full[k], BF) for k in (RESULTS if fused else NAMES)]
    scratch = list(scratch_of(fused, (win, width, hidden, windows)).values())
    params = dict(vmem_limit_bytes=64 << 20)
    if fused:
        params.update(collective_id=0, has_side_effects=True)
    return pl.pallas_call(
        functools.partial(kernel, fused, (win, width, hidden, windows)),
        out_shape=outs,
        in_specs=[hbm] * 3 + [vmem] + [hbm] * 4 + [vmem] * 4,
        out_specs=[hbm] * len(outs),
        scratch_shapes=scratch,
        compiler_params=pltpu.CompilerParams(**params),
        name="layer",
    )(tok, cot, pos, seg, wq, wo, wu, wd, g1, b1, g2, b2)


def widen(got, wide):
    rows = got.shape[-2]

    def one(i, _):
        piece = got[i] if len(got.shape) == 3 else got[i // PIECES, lax.rem(i, PIECES)]
        wide[pl.ds(pl.multiple_of(i * rows, rows), rows), :] = piece.astype(F32)
        return 0

    lax.fori_loop(0, wide.shape[0] // rows, one, 0)


def finish_kernel(*refs):
    (out_h, ig_h, small), grads = refs[:3], dict(zip(RESULTS, refs[3 : 3 + len(RESULTS)]))
    refs = refs[3 + len(RESULTS) :]
    out_o, ig_o, pos_o, qkv_o, wo_o, up_o, down_o = refs[:7]
    norms = refs[7:11]
    refs = refs[11:]
    got = dict(zip(RESULTS, refs[: len(RESULTS)]))
    wide = dict(zip(RESULTS, refs[len(RESULTS) : 2 * len(RESULTS)]))
    held, in_sem, out_sem = refs[2 * len(RESULTS) :]
    last, loads, passed = [], [], []
    for i, (src, dst) in enumerate(((out_h, out_o), (ig_h, ig_o))):
        passed.append(pltpu.make_async_copy(src, held.at[i], in_sem.at[len(RESULTS) + i]))
        last.append(pltpu.make_async_copy(held.at[i], dst, out_sem.at[len(RESULTS) + i]))
    for c in passed:
        c.start()
    for i, k in enumerate(RESULTS):
        loads.append(pltpu.make_async_copy(grads[k], got[k], in_sem.at[i]))
        loads[-1].start()
    rows = down_o.shape[0] // 2
    places = {
        "D0": down_o.at[pl.ds(0, rows)],
        "D1": down_o.at[pl.ds(rows, rows)],
        "U0": up_o.at[:, pl.ds(0, 512)],
        "U1": up_o.at[:, pl.ds(512, 512)],
        "O": wo_o,
        "Q0": qkv_o.at[:, pl.ds(0, 384)],
        "Q1": qkv_o.at[:, pl.ds(384, 384)],
        "P": pos_o,
    }
    for i in range(2):
        passed[i].wait()
        last[i].start()
    for i, k in enumerate(RESULTS):
        loads[i].wait()
        widen(got[k], wide[k])
        last.append(pltpu.make_async_copy(wide[k], places[k], out_sem.at[i]))
        last[-1].start()
    for ref, row in zip(norms, (2, 3, 0, 1)):
        ref[...] = small[row]
    for c in last:
        c.wait()


def finish(out, ig, small, grads, win, width, hidden):
    hbm = pl.BlockSpec(memory_space=pl.ANY)
    vmem = pl.BlockSpec(memory_space=pltpu.VMEM)
    shape = jax.ShapeDtypeStruct
    outs = [shape(out.shape, BF), shape(ig.shape, BF), shape((win, width), F32)]
    outs += [shape((width, 3 * width // 2), F32), shape((width // 2, width), F32)]
    outs += [shape((width, hidden // 2), F32), shape((hidden // 2, width), F32)]
    outs += [shape((width,), F32)] * 4
    dma = pltpu.SemaphoreType.DMA
    scratch = [pltpu.VMEM(g.shape, BF) for g in grads]
    scratch += [pltpu.VMEM((g.size // g.shape[-1], g.shape[-1]), F32) for g in grads]
    scratch += [pltpu.VMEM((2,) + out.shape, BF), dma((len(RESULTS) + 2,)), dma((len(RESULTS) + 2,))]
    return pl.pallas_call(
        finish_kernel,
        out_shape=outs,
        in_specs=[hbm, hbm, vmem] + [hbm] * len(RESULTS),
        out_specs=[hbm] * 7 + [vmem] * 4,
        scratch_shapes=scratch,
        compiler_params=pltpu.CompilerParams(vmem_limit_bytes=64 << 20),
        name="finish",
    )(out, ig, small, *grads)


def local(shards, tokens, segment_ids, cotangent, pos_table, w_qkv, w_out, w_up, w_down, g1, b1, g2, b2):
    dp_size, mp_size = shards
    width = tokens.shape[1]
    win = pos_table.shape[0]
    hidden = w_up.shape[1] * mp_size
    fused = dp_size == PIECES
    gains = [v.reshape(1, width) for v in (g1, b1, g2, b2)]
    if fused:
        out, ig, small, *grads = layer(
            True, tokens, cotangent, pos_table, segment_ids, w_qkv, w_out, w_up, w_down, *gains, hidden
        )
        return tuple(finish(out, ig, small, grads, win, width, hidden))
    windows = tokens.shape[0] // win
    seg = jnp.roll(segment_ids, -lax.axis_index("mp") * windows, axis=0)
    wq = lax.all_gather(w_qkv, "mp", axis=1, tiled=True)
    wo = lax.all_gather(w_out, "mp", axis=0, tiled=True)
    wu = lax.all_gather(w_up, "mp", axis=1, tiled=True)
    wd = lax.all_gather(w_down, "mp", axis=0, tiled=True)
    out, ig, small, *grads = layer(False, tokens, cotangent, pos_table, seg, wq, wo, wu, wd, *gains, hidden)
    g = dict(zip(NAMES, (v.astype(F32) for v in grads)))
    g = {
        k: v if k in DIRECT else lax.psum(lax.psum_scatter(v, "mp", scatter_dimension=0, tiled=False), "dp")
        for k, v in g.items()
    }
    pos, QA, QB, small = lax.psum((g["P"], g["QA"], g["QB"], small), ("dp", "mp"))
    g["Q1"] = jnp.where(lax.axis_index("mp") == 0, QA, QB)
    scale = jnp.array([HD**-0.5, 1, 1], F32)[:, None, None]
    Q = [(g[k].reshape(width, 3, 2, HD) * scale).transpose(0, 2, 1, 3).reshape(width, 6 * HD) for k in ("Q0", "Q1")]
    return (
        out,
        ig,
        pos.reshape(win, width),
        jnp.concatenate(Q, axis=1),
        g["O"].reshape(-1, width),
        jnp.concatenate([g["U0"].reshape(width, -1), g["U1"].reshape(width, -1)], axis=1),
        jnp.concatenate([g["D0"].reshape(-1, width), g["D1"].reshape(-1, width)], axis=0),
        small[2],
        small[3],
        small[0],
        small[1],
    )


def solution(mesh):
    cut, copied = P(("dp", "mp"), None), P()
    columns, split_rows = P(None, "mp"), P("mp", None)
    weights = (columns, split_rows, columns, split_rows)
    return jax.shard_map(
        functools.partial(local, (mesh.shape["dp"], mesh.shape["mp"])),
        mesh=mesh,
        in_specs=(cut, P("dp", None), cut, copied) + weights + (copied,) * 4,
        out_specs=(cut, cut, copied) + weights + (copied,) * 4,
        check_vma=False,
    )
```

```python
import functools

import jax
import jax.numpy as jnp
from jax import lax
from jax.experimental import pallas as pl
from jax.experimental.pallas import tpu as pltpu
from jax.sharding import PartitionSpec as P

BF = jnp.bfloat16
F32 = jnp.float32
MESH = pl.DeviceIdType.MESH
HD = 64
EPSILON = 1e-05
NEG = -1e30
GELU_A = 0.7978845608028654
GELU_B = 0.044715

CHUNKS = {
    "D0": (32, 512),
    "D1": (32, 512),
    "U0": (32, 512),
    "U1": (32, 512),
    "O": (16, 512),
    "Q0": (32, 384),
    "QA": (16, 384),
    "QB": (16, 384),
    "P": (16, 512),
}
NAMES = tuple(CHUNKS)
DIRECT = ("QA", "QB", "P")
RESULTS = ("D0", "D1", "U0", "U1", "O", "Q0", "Q1", "P")
PIECES = 16
UNROLLED = ("nb", )

SCHEDULE = {
    ("down", 1): (("D0", 0),),
    ("down", 3): (("D1", 0), ("D0", 1),),
    ("slope", 1): (("D1", 1),),
    ("up", 0): (("D0", 2),),
    ("up", 1): (("U0", 0),),
    ("up", 2): (("D1", 2),),
    ("up", 3): (("U1", 0), ("U0", 1),),
    ("nb", 0): (("D0", 3),),
    ("nb", 1): (("U1", 1), ("D1", 3),),
    ("nb", 3): (("U0", 2), ("D0", 4),),
    ("O", 0): (("sm", 0), ("O", 0),),
    ("back0", 0): (("U1", 2), ("D1", 4),),
    ("back0", 1): (("sm", 1), ("O", 1),),
    ("back0", 2): (("U0", 3), ("D0", 5),),
    ("back1", 0): (("sm", 2), ("U1", 3), ("D1", 5),),
    ("back1", 1): (("O", 2),),
    ("back1", 2): (("U0", 4), ("D0", 6),),
    ("back1", 3): (("sm", 3),),
    ("q1", 0): (("Q0", 0), ("O", 3), ("U1", 4), ("D1", 6),),
    ("back2", 0): (("sm", 4), ("U0", 5),),
    ("back2", 1): (("Q0", 1), ("O", 4), ("D0", 7),),
    ("back2", 3): (("U1", 5),),
    ("q2", 0): (("QA", 0), ("O", 5), ("U0", 6), ("D1", 7),),
    ("back3", 1): (("QA", 1), ("Q0", 2),),
    ("back3", 2): (("O", 6), ("U1", 6),),
    ("P", 0): (("P", 0),),
    ("q3", 0): (("QB", 0), ("U0", 7),),
    ("fin", 0): (("P", 1), ("QA", 2),),
    ("fin", 1): (("QB", 1), ("Q0", 3),),
    ("fin", 2): (("O", 7),),
    ("fin", 3): (("QA", 3),),
}
TAIL = (
    ("U1", 7),
    ("Q0", 4),
    ("QA", 4),
    ("P", 2),
    ("QB", 2),
    ("Q0", 5),
    ("P", 3),
    ("QA", 5),
    ("QB", 3),
    ("QA", 6),
    ("Q0", 6),
    ("P", 4),
    ("QB", 4),
    ("Q0", 7),
    ("P", 5),
    ("P", 6),
    ("QB", 5),
    ("QB", 6),
)


def dot(left, right, left_dim=1, right_dim=0):
    return lax.dot_general(
        left, right, (((left_dim,), (right_dim,)), ((), ())), preferred_element_type=F32
    )


def lanes(shape):
    return lax.broadcasted_iota(jnp.int32, shape, len(shape) - 1)


def rows_of(w, win):
    return pl.ds(pl.multiple_of(w * win, win), win)


def columns_of(start, size):
    return pl.ds(pl.multiple_of(start, 128), size)


def row_mean(v):
    return jnp.mean(v, axis=-1, keepdims=True)


def kernel(fused, dims, *refs):
    win, width, hidden, windows = dims
    half_hidden = hidden // 2
    half = win // 2
    (tok_h, cot_h, pos_h, seg, wq_h, wo_h, wu_h, wd_h, g1, b1, g2, b2) = refs[:12]
    refs = refs[12:]
    out_h, ig_h, small_h = refs[:3]
    results = RESULTS if fused else NAMES
    F = dict(zip(results, refs[3 : 3 + len(results)]))
    b = dict(zip(scratch_of(fused, dims), refs[3 + len(results) :]))
    tok, cot, pos, augk = b["tok"], b["cot"], b["pos"], b["augk"]
    wq, wo, wu, wd = b["wq"], b["wo"], b["wu"], b["wd"]
    joined, mix, u1, rs1, pb, nb = b["joined"], b["mix"], b["u1"], b["rs1"], b["pb"], b["nb"]
    act, gp, augq, nf, small = b["act"], b["gp"], b["augq"], b["nf"], b["small"]
    G, R_mp, R_a, R_b, R_z = ({k: b.get(buf + k) for k in NAMES} for buf in ("G", "M", "A", "B", "Z"))
    in_sem, out_sem = b["in_sem"], b["out_sem"]

    pairs = width // 128

    copies = {}

    def fetch(name, src, dst, k):
        copies[name] = pltpu.make_async_copy(src, dst, in_sem.at[k])
        copies[name].start()

    if fused:
        wsem, csend, crecv, ssend, srecv, lsem = (
            b[k] for k in ("wsem", "csend", "crecv", "ssend", "srecv", "lsem")
        )
        dp = lax.axis_index("dp")
        mp = lax.axis_index("mp")
        zc = dp // 4
        yc = lax.rem(dp // 2, 2)
        xc = lax.rem(dp, 2)
        ac = jnp.where(mp == 0, xc, yc)
        bc = jnp.where(mp == 0, yc, xc)
        step_a = jnp.where(mp == 0, 1, 2)
        step_b = jnp.where(mp == 0, 2, 1)
        dev_mp = (dp, 1 - mp)
        dev_a = (dp + step_a * (1 - 2 * ac), mp)
        dev_b = (dp + step_b * (1 - 2 * bc), mp)
        dev_d = (dp + step_a * (1 - 2 * ac) + step_b * (1 - 2 * bc), mp)
        dev_x = (dp + 1 - 2 * xc, mp)
        dev_y = (dp + 2 * (1 - 2 * yc), mp)
        zs = [lax.rem(zc + k, 4) for k in (1, 2, 3)]
        dev_z = [(lax.rem(dp, 4) + 4 * z, mp) for z in zs]
        barrier = pltpu.get_barrier_semaphore()
        for dev in [dev_mp, dev_a, dev_b, dev_d] + dev_z:
            pl.semaphore_signal(barrier, inc=1, device_id=dev, device_id_type=MESH)

    raw_width = wq_h.shape[1]
    raw = act.at[pl.ds(0, width), pl.ds(0, raw_width)]
    fetch("wq", wq_h, raw, 2)
    fetch("tok", tok_h, tok, 0)
    fetch("pos", pos_h, pos, 1)
    wparts = []
    if fused:
        wparts.append((wo_h, wo.at[pl.ds(pl.multiple_of(mp * half, half), half), :]))
        wparts.append((wu_h, wu.at[:, columns_of(half_hidden * mp, half_hidden)]))
        wparts.append((wd_h, wd.at[pl.ds(pl.multiple_of(mp * half_hidden, half_hidden), half_hidden), :]))
    else:
        wparts += [(wo_h, wo), (wu_h, wu), (wd_h, wd)]
    for i, (src, dst) in enumerate(wparts):
        fetch("w%d" % i, src, dst, 5 + i)
    fetch("cot", cot_h, cot, 4)
    small[...] = jnp.zeros_like(small)
    rs1[...] = jnp.zeros_like(rs1)

    l64 = lax.rem(lanes((win, 128)), HD)
    lo = lanes((win, 128)) < HD

    columns = seg[...].astype(F32).T
    mine = (mp if fused else 0) * windows
    for w in range(windows):
        R = pl.ds(w * win, win)
        column = jnp.sum(
            jnp.where(lanes(columns.shape) == mine + w, columns, 0.0), axis=1, keepdims=True
        ).astype(jnp.int32)
        augk[R, :] = jnp.where((l64 == column) | ((l64 >= 8) & (l64 < 11)), 1.0, 0.0).astype(BF)

    copies["wq"].wait()
    own_columns = mp * raw_width // 3 if fused else 0
    for p in range(raw_width // 384):
        cut = [raw[:, pl.ds(p * 384 + 128 * i, 128)] for i in range(3)]
        low = lanes((width, 128)) < HD
        swapped = [pltpu.roll(c.astype(F32), HD, 1).astype(BF) for c in cut]
        q = jnp.where(low, cut[0], cut[1]) * BF(HD**-0.5)
        k = jnp.where(low, swapped[0], swapped[2])
        v = jnp.where(low, cut[1], cut[2])
        for i, part in enumerate((q, k, v)):
            wq[:, columns_of(own_columns + width * i + 128 * p, 128)] = part

    wremote = []
    if fused:
        pl.semaphore_wait(barrier, 7)
        slices = [wq.at[:, columns_of(own_columns + width * i, raw_width // 3)] for i in range(3)]
        for i, (src, dst) in enumerate([(x, x) for x in slices] + wparts):
            c = pltpu.make_async_remote_copy(
                src_ref=src, dst_ref=dst, send_sem=wsem.at[0, i], recv_sem=wsem.at[1, i],
                device_id=dev_mp, device_id_type=MESH,
            )
            c.start()
            wremote.append(c)

    def remote(src, dst, send, recv, dev):
        return pltpu.make_async_remote_copy(
            src_ref=src, dst_ref=dst, send_sem=send, recv_sem=recv, device_id=dev, device_id_type=MESH
        )

    def add(mine, got):
        mine[...] = mine[...] + got[...]

    def exchange(name, k):
        if not fused:
            return
        c = NAMES.index(name)
        g = G[name]
        direct = name in DIRECT
        own = g.at[mp]
        base = ac * 8 + bc * 4
        full = g.at[1 - mp]

        def send(src, dst, i, dev):
            return remote(src, dst, csend.at[c, i], crecv.at[c, i], dev)

        def to_z(src, dst_of):
            return [send(src(j), dst_of(j), 3 + j, dev_z[j]) for j in range(3)]

        if direct:
            slots = R_a[name]
            places = [(1 - ac) * 8 + bc * 4, ac * 8 + (1 - bc) * 4, (1 - ac) * 8 + (1 - bc) * 4]
            plane = [dev_a, dev_b, dev_d]
            stages = [
                lambda: [send(full, R_mp[name], 0, dev_mp)],
                lambda: [send(own.at[pl.ds(places[j], 4)], slots.at[j], 6 + j, plane[j]) for j in range(3)],
                lambda: [send(own.at[base + zs[j]], R_z[name].at[j], 3 + j, dev_z[j]) for j in range(3)],
                lambda: [send(full.at[base + zc], full.at[base + zc], 9 + j, dev_z[j]) for j in range(3)],
                lambda: [send(full.at[pl.ds(base, 4)], full.at[pl.ds(base, 4)], 12 + j, plane[j]) for j in range(3)],
                lambda: [send(full, b["X" + name], 1, dev_mp)],
            ]
        else:
            stages = [
                lambda: [send(full, R_mp[name], 0, dev_mp)],
                lambda: [send(own.at[pl.ds((1 - ac) * 8, 8)], R_a[name], 1, dev_a)],
                lambda: [send(own.at[pl.ds(ac * 8 + (1 - bc) * 4, 4)], R_b[name], 2, dev_b)],
                lambda: [send(own.at[base + zs[j]], R_z[name].at[j], 3 + j, dev_z[j]) for j in range(3)],
                lambda: [send(full.at[base + zc], full.at[base + zc], 6 + j, dev_z[j]) for j in range(3)],
                lambda: [send(full.at[pl.ds(base, 4)], full.at[pl.ds(base, 4)], 9, dev_b)],
                lambda: [send(full.at[pl.ds(ac * 8, 8)], full.at[pl.ds(ac * 8, 8)], 10, dev_a)],
            ]
        if 0 < k <= len(stages):
            for copy in stages[k - 1]():
                copy.wait()
        if k == 1:
            add(own, R_mp[name])
        if direct and k == 2:
            at = own.at[pl.ds(base, 4)]
            at[...] = (
                (at[...].astype(F32) + slots[0].astype(F32)) + (slots[1].astype(F32) + slots[2].astype(F32))
            ).astype(BF)
        if not direct and k == 2:
            add(own.at[pl.ds(ac * 8, 8)], R_a[name])
        if not direct and k == 3:
            add(own.at[pl.ds(base, 4)], R_b[name])
        if k == (3 if direct else 4):
            total = own[base + zc].astype(F32)
            for j in range(3):
                total = total + R_z[name][j].astype(F32)
            if name[0] == "Q":
                q, kk, v = total[:, :128] * (HD**-0.5), total[:, 128:256], total[:, 256:]
                total = jnp.concatenate(
                    [q[:, :HD], kk[:, :HD], v[:, :HD], q[:, HD:], kk[:, HD:], v[:, HD:]], axis=1
                )
            full[base + zc] = total.astype(BF)
        if k < len(stages):
            for copy in stages[k]():
                copy.start()
        if k == len(stages):
            results_out(name, True)

    def results_out(name, start):
        full, i = G[name].at[1 - mp], 2 * NAMES.index(name)
        if name not in DIRECT:
            moves = [pltpu.make_async_copy(full, F[name], lsem.at[i])]
        else:
            to = F["P" if name == "P" else "Q1"]
            moves = [pltpu.make_async_copy(full, to.at[mp], lsem.at[i])]
            moves.append(pltpu.make_async_copy(b["X" + name], to.at[1 - mp], lsem.at[i + 1]))

        def go():
            for m in moves:
                m.start() if start else m.wait()

        if name[0] == "Q" and name != "Q0":
            pl.when(mp == ("QA", "QB").index(name))(go)
        else:
            go()

    def exchange_small(k):
        if not fused:
            return
        legs = [(b["s_mp"], dev_mp, 0), (b["s_x"], dev_x, 1), (b["s_y"], dev_y, 2)]
        if k > 0 and k <= 3:
            buf, dev, s = legs[k - 1]
            remote(small, buf, ssend.at[s], srecv.at[s], dev).wait()
            small[...] = small[...] + buf[...]
        if k < 3:
            buf, dev, s = legs[k]
            remote(small, buf, ssend.at[s], srecv.at[s], dev).start()
        zcs = [remote(small, b["s_z"].at[zc], ssend.at[3 + j], srecv.at[3 + j], dev_z[j]) for j in range(3)]
        if k == 3:
            b["s_z"][zc] = small[...]
            for z in zcs:
                z.start()
        if k == 4:
            for z in zcs:
                z.wait()
            small[...] = (b["s_z"][0] + b["s_z"][1]) + (b["s_z"][2] + b["s_z"][3])

    causal = jnp.where(lanes((half, half)) <= lax.broadcasted_iota(jnp.int32, (half, half), 0), 0.0, NEG)
    def attend(w, p):
        R = rows_of(w, win)
        Q, K, V = (joined[R, columns_of(width * i + p * 128, 128)] for i in range(3))
        ak = augk[R, :]
        ones = jnp.ones((win, 128), BF)
        zero = jnp.zeros((win, 128), BF)
        aq = jnp.where(l64 < 8, (ones - ak) * BF(NEG), zero)
        qs, ks, vs = [], [], []
        for h in range(2):
            mine = lo if h == 0 else ~lo
            qs.append(jnp.where(mine, Q, aq))
            ks.append(jnp.where(mine, K, ak))
            vs.append(jnp.concatenate([jnp.where(mine, V, zero), jnp.where(mine, ones, zero)], axis=1))
        for qb in range(2):
            kl = half * (qb + 1)
            es, ms = [], []
            for h in range(2):
                s = dot(qs[h][qb * half : (qb + 1) * half], ks[h][:kl], 1, 1)
                if qb == 0:
                    s = s + causal
                else:
                    s = jnp.concatenate([s[:, :half], s[:, half:] + causal], axis=1)
                m = jnp.max(s, axis=1, keepdims=True)
                es.append(jnp.exp(s - m).astype(BF))
                ms.append(m)
            ov = dot(jnp.concatenate(es, axis=1), jnp.concatenate([v[:kl] for v in vs], axis=0))
            total = ov[:, 128:]
            rr = pl.ds(pl.multiple_of(w * win + qb * half, half), half)
            mix[rr, columns_of(p * 128, 128)] = (ov[:, :128] / total).astype(BF)
            low = lo[:half]
            lse = jnp.where(low, ms[0], ms[1]) + jnp.log(total)
            x = -pltpu.roll(lse, HD, 1)
            hi = x.astype(BF)
            x = x - hi.astype(F32)
            mid = x.astype(BF)
            last = (x - mid.astype(F32)).astype(BF)
            l6 = l64[:half]
            a = aq[qb * half : (qb + 1) * half]
            a = jnp.where(l6 == 8, hi, a)
            a = jnp.where(l6 == 9, mid, a)
            augq[rr, columns_of(p * 128, 128)] = jnp.where(l6 == 10, last, a)

    copies["tok"].wait()
    copies["pos"].wait()

    def place(w, _):
        R = rows_of(w, win)
        pb[R, :] = (tok[R, :].astype(F32) + pos[...].astype(F32)).astype(BF)
        return 0

    lax.fori_loop(0, windows, place, 0)
    for part in range(2 if fused else 1):
        if part:
            for c in wremote[:3]:
                c.wait()
        span = width // 2 if fused else width
        start = (mp if part == 0 else 1 - mp) * span if fused else 0

        def project(w, _):
            R = rows_of(w, win)
            for i in range(3):
                cs = columns_of(width * i + start, span)
                joined[R, cs] = dot(pb[R, :], wq[:, cs]).astype(BF)
            return 0

        lax.fori_loop(0, windows, project, 0)

    def attend_window(w, _):
        for p in range(pairs):
            attend(w, p)
        return 0

    lax.fori_loop(0, windows, attend_window, 0)

    for i in range(3):
        copies["w%d" % i].wait()
    for c in wremote[3:]:
        c.wait()
    copies["cot"].wait()

    def feed(w, _):
        R = rows_of(w, win)
        r1 = (tok[R, :].astype(F32) + pos[...].astype(F32)) + dot(mix[R, :], wo[...])
        center = r1 - row_mean(r1)
        rstd = lax.rsqrt(row_mean(center * center) + EPSILON)
        unit = center * rstd
        u1[R, :] = unit.astype(BF)
        rs1[...] = jnp.where(lanes((win, 128)) == w, rstd, rs1[...])
        normed = unit * g1[...] + b1[...]
        nf[...] = normed
        nb[R, :] = normed.astype(BF)

        r2 = nf[...]
        for c in range(hidden // 512):
            cs = pl.ds(c * 512, 512)
            v = dot(nb[R, :], wu[:, cs]).astype(BF)
            v2 = v * v
            t = jnp.tanh(v * (BF(GELU_A) + BF(GELU_A * GELU_B) * v2))
            h = BF(0.5) + BF(0.5) * t
            active = v * h
            act[R, cs] = active
            gp[R, cs] = h + h * ((BF(1) - h) * (v * (BF(2 * GELU_A) + BF(6 * GELU_A * GELU_B) * v2)))
            r2 = r2 + dot(active, wd[cs, :])
        center = r2 - row_mean(r2)
        rstd = lax.rsqrt(row_mean(center * center) + EPSILON)
        unit = center * rstd
        tok[R, :] = (unit * g2[...] + b2[...]).astype(BF)
        up = cot[R, :].astype(F32)
        small[0:1, :] += jnp.sum(up * unit, axis=0, keepdims=True)
        small[1:2, :] += jnp.sum(up, axis=0, keepdims=True)
        e = up * g2[...]
        cot[R, :] = (rstd * (e - row_mean(e) - unit * row_mean(e * unit))).astype(BF)
        return 0

    lax.fori_loop(0, windows, feed, 0)
    out_copy = pltpu.make_async_copy(tok, out_h, out_sem.at[0])
    out_copy.start()

    def hooked(phase, body, count, first=0):
        def one(t, _):
            body(t, 0)
            for at in range(count):
                steps = SCHEDULE.get((phase, first + at))
                if steps:
                    pl.when(t == at)(functools.partial(run_steps, steps))
            return 0

        if phase not in UNROLLED:
            lax.fori_loop(0, count, one, 0)
            return
        for t in range(count):
            body(t, 0)
            run_steps(SCHEDULE.get((phase, t), ()))

    def run_steps(steps):
        for name, k in steps:
            if name == "sm":
                exchange_small(k)
            else:
                exchange(name, k)

    halves = hidden // 1024

    def down_tile(part, m, _):
        tile = m * halves + part
        d = dot(act[:, columns_of(tile * 512, 512)], cot[...], 0, 0).astype(BF).reshape(16, 32, 512)
        G["D%d" % part][m] = d
        return 0

    for part in range(2):
        hooked("down", functools.partial(down_tile, part), 2, 2 * part)

    def slope(w, _):
        R = rows_of(w, win)
        for c in range(hidden // 512):
            cs = pl.ds(c * 512, 512)
            d = dot(cot[R, :], wd[pl.ds(c * 512, 512), :], 1, 1)
            gp[R, cs] = (d * gp[R, cs].astype(F32)).astype(BF)
        return 0

    hooked("slope", slope, windows)

    def up_tile(part, m, _):
        tile = m * halves + part
        d = dot(nb[...], gp[:, columns_of(tile * 512, 512)], 0, 0).astype(BF).reshape(16, 32, 512)
        G["U%d" % part][m] = d
        return 0

    for part in range(2):
        hooked("up", functools.partial(up_tile, part), 2, 2 * part)

    def norm_back(w, _):
        R = rows_of(w, win)
        ng = cot[R, :].astype(F32) + dot(gp[R, :], wu[...], 1, 1)
        unit = u1[R, :].astype(F32)
        small[2:3, :] += jnp.sum(ng * unit, axis=0, keepdims=True)
        small[3:4, :] += jnp.sum(ng, axis=0, keepdims=True)
        e = ng * g1[...]
        rstd = jnp.sum(jnp.where(lanes((win, 128)) == w, rs1[...], 0.0), axis=1, keepdims=True)
        rg = (rstd * (e - row_mean(e) - unit * row_mean(e * unit))).astype(BF)
        cot[R, :] = rg
        u1[R, :] = dot(rg, wo[...], 1, 1).astype(BF)
        return 0

    hooked("nb", norm_back, windows)

    G["O"][...] = dot(mix[...], cot[...], 0, 0).astype(BF).reshape(2, 16, half // 16, 512)
    run_steps(SCHEDULE.get(("O", 0), ()))

    flip = (lax.broadcasted_iota(jnp.int32, (256, 128), 0) % 128 < HD) != (lanes((256, 128)) < HD)
    swap = jnp.where(flip, 1.0, 0.0).astype(BF)

    def attend_back(w, p):
        R = rows_of(w, win)
        pc = columns_of(p * 128, 128)
        Q, K, V = (joined[R, columns_of(width * i + p * 128, 128)] for i in range(3))
        D = u1[R, pc]
        prod = D.astype(F32) * mix[R, pc].astype(F32)
        ph = prod.astype(BF)
        pr = (prod - ph.astype(F32)).astype(BF)
        x = -dot(jnp.concatenate([ph, pr], axis=1), swap)
        hi = x.astype(BF)
        mid = (x - hi.astype(F32)).astype(BF)
        zero = jnp.zeros((win, 128), BF)
        ad = jnp.where(l64 == 8, hi, jnp.where(l64 == 9, mid, zero))
        av = jnp.where((l64 == 8) | (l64 == 9), jnp.ones((win, 128), BF), zero)
        aq, ak = augq[R, pc], augk[R, :]
        QT, DT = Q.T, D.T
        probs, grads = [[], []], [[], []]
        for h in range(2):
            mine = lo if h == 0 else ~lo
            qa, ka, va, da = (jnp.where(mine, i, j) for i, j in ((Q, aq), (K, ak), (V, av), (D, ad)))
            for qb in range(2):
                kl = half * (qb + 1)
                qs = slice(qb * half, kl)
                s = dot(qa[qs], ka[:kl], 1, 1)
                s = s + causal if qb == 0 else jnp.concatenate([s[:, :half], s[:, half:] + causal], axis=1)
                e = jnp.exp(s)
                grads[h].append((e * dot(da[qs], va[:kl], 1, 1)).astype(BF))
                probs[h].append(e.astype(BF))
        dq, dk, dv = [None, None], [], []
        for h in range(2):
            km = jnp.where(lo if h == 0 else ~lo, K, zero)
            hs = slice(h * HD, (h + 1) * HD)
            for qb in range(2):
                x = dot(grads[h][qb], km[: half * (qb + 1)])
                dq[qb] = x if h == 0 else dq[qb] + x
            for left, (first, second), to in ((QT, grads[h], dk), (DT, probs[h], dv)):
                early = dot(left[hs], jnp.concatenate([first, second[:, :half]], axis=0))
                to.append(jnp.concatenate([early, dot(left[hs, half:], second[:, half:])], axis=1))
        for i in range(2):
            joined[pl.ds(pl.multiple_of(w * win + i * half, half), half), pc] = dq[i].astype(BF)
        for i, v in enumerate((dk, dv)):
            joined[R, columns_of(width * (i + 1) + p * 128, 128)] = jnp.concatenate(v, axis=0).astype(BF).T

    def qkv_grad(*some):
        def one(m, _):
            total = None
            for w in range(windows):
                R = pl.ds(w * win, win)
                right = jnp.concatenate(
                    [joined[R, pl.ds(width * i + p * 128, 128)] for p in some for i in range(3)], axis=1
                )
                d = dot(pb[R, columns_of(m * half, half)], right, 0, 0)
                total = d if total is None else total + d
            total = total.astype(BF)
            if len(some) == 2:
                for j in range(2):
                    G["Q0"][j, pl.ds(8 * m, 8)] = total[:, 384 * j : 384 * (j + 1)].reshape(8, 32, 384)
            else:
                G["QA" if some[0] == 1 else "QB"][m] = total.reshape(16, 16, 384)
            return 0

        lax.fori_loop(0, 2, one, 0)

    def add_position(p):
        cols = [pl.ds(width * i + p * 128, 128) for i in range(3)]
        total = []
        for c in cols:
            v = joined[pl.ds(0, win), c].astype(F32)
            for w in range(1, windows):
                v = v + joined[pl.ds(w * win, win), c].astype(F32)
            total.append(v.astype(BF))
        part = dot(jnp.concatenate(total, axis=1), jnp.concatenate([wq[:, c] for c in cols], axis=1), 1, 1)
        nf[...] = nf[...] + part

    def steps_at(phase, at):
        run_steps(SCHEDULE.get((phase, at), ()))

    total = cot[pl.ds(0, win), :].astype(F32)
    for w in range(1, windows):
        total = total + cot[pl.ds(w * win, win), :].astype(F32)
    nf[...] = total
    order = (0, 2, 1, 3)
    for i, p in enumerate(order):
        hooked("back%d" % i, lambda t, _: attend_back(t, p), windows)
        if i == 3:
            add_position(p)
            G["P"][...] = nf[...].astype(BF).reshape(2, 16, half // 16, 512)
            steps_at("P", 0)
        if i > 0:
            qkv_grad(*((0, 2) if i == 1 else (p,)))
        steps_at("q%d" % i, 0)
        if i < 3:
            add_position(p)
            steps_at("add%d" % i, 0)

    def finish(w, _):
        R = rows_of(w, win)
        cot[R, :] = (cot[R, :].astype(F32) + dot(joined[R, :], wq[...], 1, 1)).astype(BF)
        return 0

    hooked("fin", finish, windows)
    ig_copy = pltpu.make_async_copy(cot, ig_h, out_sem.at[1])
    ig_copy.start()
    small_copy = pltpu.make_async_copy(small, small_h, out_sem.at[2])
    small_copy.start()
    run_steps(TAIL)
    if fused:
        for name in NAMES:
            results_out(name, False)
    if not fused:
        outs = [pltpu.make_async_copy(G[nm], F[nm], in_sem.at[i]) for i, nm in enumerate(NAMES)]
        for c in outs:
            c.start()
        for c in outs:
            c.wait()
    out_copy.wait()
    ig_copy.wait()
    small_copy.wait()


def scratch_of(fused, dims):
    win, width, hidden, windows = dims
    rows = win * windows
    V, dma = pltpu.VMEM, pltpu.SemaphoreType.DMA
    b = {k: V((rows, width), BF) for k in ("tok", "cot", "mix", "u1", "pb", "nb", "augq")}
    b.update({k: V((rows, hidden), BF) for k in ("act", "gp")})
    b.update(
        pos=V((win, width), BF),
        augk=V((rows, 128), BF),
        wq=V((width, 3 * width), BF),
        wo=V((width, width), BF),
        wu=V((width, hidden), BF),
        wd=V((hidden, width), BF),
        joined=V((rows, 3 * width), BF),
        rs1=V((win, 128), F32),
        nf=V((win, width), F32),
        small=V((8, width), F32),
        in_sem=dma((12,)),
        out_sem=dma((3,)),
    )
    b.update({"G" + k: V((2, PIECES) + CHUNKS[k], BF) for k in NAMES})
    if fused:
        for k in NAMES:
            lead = {"M": (16,), "A": (8,), "B": (4,), "Z": (3,)}
            if k in DIRECT:
                lead = {"M": (16,), "A": (3, 4), "Z": (3,), "X": (16,)}
            b.update({buf + k: V(n + CHUNKS[k], BF) for buf, n in lead.items()})
        b.update({k: V((8, width), F32) for k in ("s_mp", "s_x", "s_y")})
        b.update(
            s_z=V((4, 8, width), F32),
            wsem=dma((2, 6)),
            csend=dma((len(NAMES), 15)),
            crecv=dma((len(NAMES), 15)),
            ssend=dma((6,)),
            srecv=dma((6,)),
            lsem=dma((2 * len(NAMES),)),
        )
    return b


def layer(fused, tok, cot, pos, seg, wq, wo, wu, wd, g1, b1, g2, b2, hidden):
    rows, width = tok.shape
    win = pos.shape[0]
    windows = rows // win
    hbm = pl.BlockSpec(memory_space=pl.ANY)
    vmem = pl.BlockSpec(memory_space=pltpu.VMEM)
    shape = jax.ShapeDtypeStruct
    full = {k: (PIECES,) + v if fused and k not in DIRECT else (2, PIECES) + v for k, v in CHUNKS.items()}
    full["Q1"] = full["QA"]
    outs = [shape((rows, width), BF), shape((rows, width), BF), shape((8, width), F32)]
    outs += [shape(full[k], BF) for k in (RESULTS if fused else NAMES)]
    scratch = list(scratch_of(fused, (win, width, hidden, windows)).values())
    params = dict(vmem_limit_bytes=64 << 20)
    if fused:
        params.update(collective_id=0, has_side_effects=True)
    return pl.pallas_call(
        functools.partial(kernel, fused, (win, width, hidden, windows)),
        out_shape=outs,
        in_specs=[hbm] * 3 + [vmem] + [hbm] * 4 + [vmem] * 4,
        out_specs=[hbm] * len(outs),
        scratch_shapes=scratch,
        compiler_params=pltpu.CompilerParams(**params),
        name="layer",
    )(tok, cot, pos, seg, wq, wo, wu, wd, g1, b1, g2, b2)


def widen(got, wide):
    rows = got.shape[-2]

    def one(i, _):
        piece = got[i] if len(got.shape) == 3 else got[i // PIECES, lax.rem(i, PIECES)]
        wide[pl.ds(pl.multiple_of(i * rows, rows), rows), :] = piece.astype(F32)
        return 0

    lax.fori_loop(0, wide.shape[0] // rows, one, 0)


def finish_kernel(*refs):
    (out_h, ig_h, small), grads = refs[:3], dict(zip(RESULTS, refs[3 : 3 + len(RESULTS)]))
    refs = refs[3 + len(RESULTS) :]
    out_o, ig_o, pos_o, qkv_o, wo_o, up_o, down_o = refs[:7]
    norms = refs[7:11]
    refs = refs[11:]
    got = dict(zip(RESULTS, refs[: len(RESULTS)]))
    wide = dict(zip(RESULTS, refs[len(RESULTS) : 2 * len(RESULTS)]))
    held, in_sem, out_sem = refs[2 * len(RESULTS) :]
    last, loads, passed = [], [], []
    for i, (src, dst) in enumerate(((out_h, out_o), (ig_h, ig_o))):
        passed.append(pltpu.make_async_copy(src, held.at[i], in_sem.at[len(RESULTS) + i]))
        last.append(pltpu.make_async_copy(held.at[i], dst, out_sem.at[len(RESULTS) + i]))
    for c in passed:
        c.start()
    for i, k in enumerate(RESULTS):
        loads.append(pltpu.make_async_copy(grads[k], got[k], in_sem.at[i]))
        loads[-1].start()
    rows = down_o.shape[0] // 2
    places = {
        "D0": down_o.at[pl.ds(0, rows)],
        "D1": down_o.at[pl.ds(rows, rows)],
        "U0": up_o.at[:, pl.ds(0, 512)],
        "U1": up_o.at[:, pl.ds(512, 512)],
        "O": wo_o,
        "Q0": qkv_o.at[:, pl.ds(0, 384)],
        "Q1": qkv_o.at[:, pl.ds(384, 384)],
        "P": pos_o,
    }
    for i in range(2):
        passed[i].wait()
        last[i].start()
    for i, k in enumerate(RESULTS):
        loads[i].wait()
        widen(got[k], wide[k])
        last.append(pltpu.make_async_copy(wide[k], places[k], out_sem.at[i]))
        last[-1].start()
    for ref, row in zip(norms, (2, 3, 0, 1)):
        ref[...] = small[row]
    for c in last:
        c.wait()


def finish(out, ig, small, grads, win, width, hidden):
    hbm = pl.BlockSpec(memory_space=pl.ANY)
    vmem = pl.BlockSpec(memory_space=pltpu.VMEM)
    shape = jax.ShapeDtypeStruct
    outs = [shape(out.shape, BF), shape(ig.shape, BF), shape((win, width), F32)]
    outs += [shape((width, 3 * width // 2), F32), shape((width // 2, width), F32)]
    outs += [shape((width, hidden // 2), F32), shape((hidden // 2, width), F32)]
    outs += [shape((width,), F32)] * 4
    dma = pltpu.SemaphoreType.DMA
    scratch = [pltpu.VMEM(g.shape, BF) for g in grads]
    scratch += [pltpu.VMEM((g.size // g.shape[-1], g.shape[-1]), F32) for g in grads]
    scratch += [pltpu.VMEM((2,) + out.shape, BF), dma((len(RESULTS) + 2,)), dma((len(RESULTS) + 2,))]
    return pl.pallas_call(
        finish_kernel,
        out_shape=outs,
        in_specs=[hbm, hbm, vmem] + [hbm] * len(RESULTS),
        out_specs=[hbm] * 7 + [vmem] * 4,
        scratch_shapes=scratch,
        compiler_params=pltpu.CompilerParams(vmem_limit_bytes=64 << 20),
        name="finish",
    )(out, ig, small, *grads)


def local(shards, tokens, segment_ids, cotangent, pos_table, w_qkv, w_out, w_up, w_down, g1, b1, g2, b2):
    dp_size, mp_size = shards
    width = tokens.shape[1]
    win = pos_table.shape[0]
    hidden = w_up.shape[1] * mp_size
    fused = dp_size == PIECES
    gains = [v.reshape(1, width) for v in (g1, b1, g2, b2)]
    if fused:
        out, ig, small, *grads = layer(
            True, tokens, cotangent, pos_table, segment_ids, w_qkv, w_out, w_up, w_down, *gains, hidden
        )
        return tuple(finish(out, ig, small, grads, win, width, hidden))
    windows = tokens.shape[0] // win
    seg = jnp.roll(segment_ids, -lax.axis_index("mp") * windows, axis=0)
    wq = lax.all_gather(w_qkv, "mp", axis=1, tiled=True)
    wo = lax.all_gather(w_out, "mp", axis=0, tiled=True)
    wu = lax.all_gather(w_up, "mp", axis=1, tiled=True)
    wd = lax.all_gather(w_down, "mp", axis=0, tiled=True)
    out, ig, small, *grads = layer(False, tokens, cotangent, pos_table, seg, wq, wo, wu, wd, *gains, hidden)
    g = dict(zip(NAMES, (v.astype(F32) for v in grads)))
    g = {
        k: v if k in DIRECT else lax.psum(lax.psum_scatter(v, "mp", scatter_dimension=0, tiled=False), "dp")
        for k, v in g.items()
    }
    pos, QA, QB, small = lax.psum((g["P"], g["QA"], g["QB"], small), ("dp", "mp"))
    g["Q1"] = jnp.where(lax.axis_index("mp") == 0, QA, QB)
    scale = jnp.array([HD**-0.5, 1, 1], F32)[:, None, None]
    Q = [(g[k].reshape(width, 3, 2, HD) * scale).transpose(0, 2, 1, 3).reshape(width, 6 * HD) for k in ("Q0", "Q1")]
    return (
        out,
        ig,
        pos.reshape(win, width),
        jnp.concatenate(Q, axis=1),
        g["O"].reshape(-1, width),
        jnp.concatenate([g["U0"].reshape(width, -1), g["U1"].reshape(width, -1)], axis=1),
        jnp.concatenate([g["D0"].reshape(-1, width), g["D1"].reshape(-1, width)], axis=0),
        small[2],
        small[3],
        small[0],
        small[1],
    )


def solution(mesh):
    cut, copied = P(("dp", "mp"), None), P()
    columns, split_rows = P(None, "mp"), P("mp", None)
    weights = (columns, split_rows, columns, split_rows)
    return jax.shard_map(
        functools.partial(local, (mesh.shape["dp"], mesh.shape["mp"])),
        mesh=mesh,
        in_specs=(cut, P("dp", None), cut, copied) + weights + (copied,) * 4,
        out_specs=(cut, cut, copied) + weights + (copied,) * 4,
        check_vma=False,
    )
```
